32 devices in a mesh: table: 16 (over z, x, core), scal: 2 (over y).
Axes of the slice: x: 2, y: 2, z: 4, core: 2. Of those that a mesh axis runs over, the one named last changes fastest.
Arguments:
- cell_coords: float32 [4, 32768], P(None, ('table', 'scal')), may hold values from 0 to 1
- flamelet_table: float32 [65536, 1024], P('table', 'scal'), may hold values from -15 to 15
- owner_shard: int32 [32768, 1], P(('table', 'scal')), may hold values from 0 to 15; in each aligned block of 64 rows (0 to 63, 64 to 127, ...) at most 10 rows name the same one
- local_bin: int32 [32768], P(('table', 'scal')), may hold values from 0 to 4095
Outputs:
- filtered_fields: float32 [32, 256, 128], P(None, ('table', 'scal'))
- x_gradient: float32 [32, 256, 128], P(None, ('table', 'scal'))
The draws below stay inside these ranges and needn't reach their ends.
Inputs may be any that keep to these rules, and one draw needn't show every extreme that they name: `owner_shard`: in each aligned block of 64 rows (one group of one device's cells) no shard is named by more than 10 rows, a bound that some block reaches.
All inputs are finite; a program needn't handle non-finite values.
Results may differ from the reference program's by a relative error of at most 0.00012.
Values sent between devices are 32-bit elements; how exact they have to be, the bound alone decides.
No kernel may reach another device: no remote copies, remote signals or barrier semaphores. Data moves between devices by JAX's collectives and lax.ppermute only.
A program may use at most 128 MiB of HBM per device.

```python
import math
import jax
import jax.numpy as jnp
import numpy as np
from jax import lax

SCAL_ALL = 32
K = 32
BINS_DEV = 4096
BX = 8
LG = 8
NX = 128
LINES = 256
CELL_DEV = 1024
CELLS = 32768
MOST = 10
N_TABLE = 16
N_SCAL = 2


def with_ends(entries, rng, smallest, top_value):
    longest = entries.shape.index(max(entries.shape))
    spots = []
    for shift in (0, 1):
        where = [jax.random.randint(jax.random.fold_in(rng, axis), (), 0, length) for axis, length in enumerate(entries.shape)]
        where[longest] = (where[longest] + shift) % entries.shape[longest]
        spots.append(tuple(where))
    return entries.at[spots[0]].set(smallest).at[spots[1]].set(top_value)


def level_of(rng, shape, cuts, smallest, top_value):
    gain, own = 1.0, jax.random.fold_in(rng, 6)
    for axis_at, shards_of in cuts:
        draws = jnp.exp(jax.random.uniform(jax.random.fold_in(own, axis_at), (shards_of,), jnp.float32, smallest / len(cuts), top_value / len(cuts)))
        gain = gain * jnp.repeat(draws, shape[axis_at] // shards_of).reshape([-1 if axis == axis_at else 1 for axis in range(len(shape))])
    return gain


def shared_out(own_key, own, number, rows, count, top, limit, slope):
    ranking = jax.random.permutation(own_key, count)
    crowded, common = portions_of(count, rows * top, limit, slope, True), portions_of(count, rows * top, limit, slope, False)
    places = jnp.arange(count)

    def named(tallies, turn):
        used = int((tallies > 0).sum())
        fixed = max(1, used // 4)
        passed = fixed + (places - fixed + turn * (used - fixed)) % max(1, count - fixed)
        return jnp.zeros((count,), jnp.int32).at[ranking[jnp.where(places < fixed, places, passed)]].set(jnp.asarray(tallies, jnp.int32))

    tallies = jnp.where(number % 4 == 0, named(crowded, number // 4), named(common, number - number // 4 - 1))
    mixed = jax.random.permutation(jax.random.fold_in(own, 3), count)
    source_of, sink = mixed[0:count // 2 * 2:2], mixed[1:count // 2 * 2:2]
    slack = jnp.minimum(tallies[source_of] - 1, limit - tallies[sink]) // 2
    slack = jnp.where((source_of == ranking[0]) | (sink == ranking[0]) | (tallies[sink] == 0), 0, jnp.maximum(slack, 0))
    passed = jax.random.randint(jax.random.fold_in(own, 4), (count // 2,), 0, 1 << 20) % (slack + 1)
    tallies = tallies.at[source_of].add(-passed).at[sink].add(passed)
    labels = jnp.searchsorted(jnp.cumsum(tallies), jnp.arange(rows * top), side="right").astype(jnp.int32)
    grid = labels.reshape(top, rows).T
    grid = grid[jax.random.permutation(jax.random.fold_in(own, 1), rows)]
    turn = jax.random.randint(jax.random.fold_in(own, 2), (rows, 1), 0, top)
    return jnp.take_along_axis(grid, (jnp.arange(top)[None, :] + turn) % top, axis=1)


def portions_of(number_of, total, bound, lean, full):
    portions = [(1 << 20) // math.isqrt(grade ** lean) + 1 for grade in range(1, number_of + 1)]
    largest = bound if full else min(bound, max(-(-total // number_of), total * portions[0] // sum(portions)))
    least = 1 if total - largest >= number_of - 1 else 0
    counts, spare = [largest] + [least] * (number_of - 1), total - largest - least * (number_of - 1)
    while spare > 0:
        free = [i for i in range(1, number_of) if counts[i] < largest] or [i for i in range(1, number_of) if counts[i] < bound]
        pool, budget = sum([portions[i] for i in free]), spare
        for i in free:
            extra = min(bound - counts[i], max(1, budget * portions[i] // pool), spare)
            counts[i] = counts[i] + extra
            spare = spare - extra
    return np.array(counts)


def gaussian(rng, extent, spread, bound, pieces=(), held_as=jnp.bfloat16):
    array = spread * jax.random.normal(rng, extent, jnp.float32)
    if pieces:
        array = array * level_of(rng, extent, pieces, -0.22, 0.18)
    return jnp.clip(array, -bound, bound).astype(held_as)


def setup_inputs(seed: int = 0) -> dict:
    arg_keys = jax.random.split(jax.random.key(seed), 5)
    cell_coords = jnp.clip(1.0 * jax.random.uniform(arg_keys[0], (4, CELLS), jnp.float32) ** level_of(arg_keys[0], (4, CELLS), ((1, 32),), -0.2, 0.2), 0.0, 1.0)
    flamelet_table = gaussian(arg_keys[1], (N_TABLE * BINS_DEV, SCAL_ALL * K), 2.5, 15.0, ((0, 16), (1, 2)), jnp.float32)
    owner_shard_keys = jax.random.split(jax.random.fold_in(arg_keys[2], 1), CELLS // (BX * LG))
    owner_shard_turns = jax.random.permutation(jax.random.fold_in(arg_keys[2], 3), CELLS // (BX * LG))
    owner_shard = jax.vmap(lambda own, number: shared_out(jax.random.fold_in(arg_keys[2], 2), own, number, BX * LG, N_TABLE, 1, MOST, 2))(owner_shard_keys, owner_shard_turns).reshape((CELLS, 1))
    local_bin = with_ends(jax.random.randint(arg_keys[3], (CELLS,), 0, BINS_DEV), jax.random.fold_in(arg_keys[3], 1), 0, BINS_DEV - 1).astype(jnp.int32)
    return {"cell_coords": cell_coords, "flamelet_table": flamelet_table, "owner_shard": owner_shard, "local_bin": local_bin}


strength = 0.499

def spline_weights(coords):
    linear = [jnp.stack([1.0 - coords[axis_id], coords[axis_id]]) for axis_id in range(3)]
    frac_last = coords[3]
    square = frac_last * frac_last
    cube = square * frac_last
    remain = 1.0 - frac_last
    cubic = jnp.stack([remain * remain * remain / 6.0, (3.0 * cube - 6.0 * square + 4.0) / 6.0, (-3.0 * cube + 3.0 * square + 3.0 * frac_last + 1.0) / 6.0, cube / 6.0])
    product = linear[0][:, None, None, None, :] * linear[1][None, :, None, None, :] * linear[2][None, None, :, None, :] * cubic[None, None, None, :, :]
    return product.reshape(-1, coords.shape[1])

def filter_matrix(length):
    positions = jnp.arange(length)
    offset = positions[None, :] - positions[:, None]
    distance = jnp.abs(offset)
    interior = (positions >= 3) & (positions <= length - 4)
    coeffs = [(11.0 + 10.0 * strength) / 16.0, (15.0 + 34.0 * strength) / 64.0, (-3.0 + 6.0 * strength) / 32.0, (1.0 - 2.0 * strength) / 64.0]
    band = jnp.zeros((length, length), jnp.float32)
    for reach in range(4):
        band = band + jnp.where(distance == reach, coeffs[reach], 0.0).astype(jnp.float32)
    right_side = jnp.where(interior[:, None], band, (offset == 0).astype(jnp.float32))
    coupling = jnp.where(interior, strength, 0.0).astype(jnp.float32)
    main_diag = jnp.ones((length,), jnp.float32)
    return lax.linalg.tridiagonal_solve(coupling, main_diag, coupling, right_side)

def derivative_matrix(length):
    positions = jnp.arange(length)
    offset = positions[None, :] - positions[:, None]
    distance = jnp.abs(offset)
    direction = jnp.sign(offset).astype(jnp.float32)
    boundary = (positions == 0) | (positions == length - 1)
    second = (positions == 1) | (positions == length - 2)
    interior = jnp.logical_not(boundary | second)
    below_diag = jnp.where(interior, 1.0 / 3.0, jnp.where(second, 0.25, jnp.where(positions == length - 1, 2.0, 0.0))).astype(jnp.float32)
    above_diag = jnp.where(interior, 1.0 / 3.0, jnp.where(second, 0.25, jnp.where(positions == 0, 2.0, 0.0))).astype(jnp.float32)
    inner_rows = direction * (jnp.where(distance == 1, 7.0 / 9.0, 0.0) + jnp.where(distance == 2, 1.0 / 36.0, 0.0))
    second_rows = direction * jnp.where(distance == 1, 0.75, 0.0)
    first_row = jnp.where(offset == 0, -2.5, jnp.where(offset == 1, 2.0, jnp.where(offset == 2, 0.5, 0.0)))
    final_row = jnp.where(offset == 0, 2.5, jnp.where(offset == -1, -2.0, jnp.where(offset == -2, -0.5, 0.0)))
    right_side = jnp.where(interior[:, None], inner_rows, jnp.where(second[:, None], second_rows, jnp.where((positions == 0)[:, None], first_row, final_row))).astype(jnp.float32)
    main_diag = jnp.ones((length,), jnp.float32)
    return lax.linalg.tridiagonal_solve(below_diag, main_diag, above_diag, right_side)

def reference(cell_coords, flamelet_table, owner_shard, local_bin):
    row_index = (owner_shard[:, 0] * BINS_DEV + local_bin).astype(jnp.int32)
    block_count = row_index.shape[0] // CELL_DEV

    def one_block(inputs):
        coords, wanted = inputs
        weights = spline_weights(coords)
        gathered = jnp.take(flamelet_table, wanted, axis=0).reshape(CELL_DEV, SCAL_ALL, K)
        return jnp.einsum('nsk,kn->sn', gathered, weights, precision=lax.Precision.HIGHEST)
    looked = lax.map(one_block, (cell_coords.reshape(4, block_count, CELL_DEV).transpose(1, 0, 2), row_index.reshape(block_count, CELL_DEV)))
    looked = looked.transpose(1, 0, 2).reshape(SCAL_ALL, N_TABLE, N_SCAL, N_TABLE, LG, BX)
    gridded = looked.transpose(0, 3, 2, 4, 1, 5).reshape(SCAL_ALL * LINES, NX)
    filtered = jnp.dot(gridded, filter_matrix(NX).T, precision=lax.Precision.HIGHEST)
    gradient = jnp.dot(filtered, derivative_matrix(NX).T, precision=lax.Precision.HIGHEST)
    return (filtered.reshape(SCAL_ALL, LINES, NX), gradient.reshape(SCAL_ALL, LINES, NX))
```

```python
import functools

import jax
import jax.numpy as jnp
import numpy as np
from jax import lax
from jax.experimental import pallas as pl
from jax.experimental.pallas import tpu as pltpu
from jax.sharding import PartitionSpec as P

SCAL_ALL = 32
K = 32
BX = 8
LG = 8
GROUP = BX * LG
LANES = 128
AXES = ("table", "scal")

strength = 0.499


def thomas_solve(below, middle, above, right_side):
    length = middle.shape[0]
    upper_factor = np.zeros(length)
    solved = np.zeros(right_side.shape)
    for row in range(length):
        if row == 0:
            denom = middle[0]
            solved[0] = right_side[0] / denom
        else:
            denom = middle[row] - below[row] * upper_factor[row - 1]
            solved[row] = (right_side[row] - below[row] * solved[row - 1]) / denom
        upper_factor[row] = above[row] / denom
    for row in range(length - 2, -1, -1):
        solved[row] = solved[row] - upper_factor[row] * solved[row + 1]
    return solved


def filter_table(length):
    positions = np.arange(length)
    offset = positions[None, :] - positions[:, None]
    distance = np.abs(offset)
    interior = (positions >= 3) & (positions <= length - 4)
    coeffs = [
        (11.0 + 10.0 * strength) / 16.0,
        (15.0 + 34.0 * strength) / 64.0,
        (-3.0 + 6.0 * strength) / 32.0,
        (1.0 - 2.0 * strength) / 64.0,
    ]
    band = np.zeros((length, length))
    for reach in range(4):
        band = band + np.where(distance == reach, coeffs[reach], 0.0)
    right_side = np.where(interior[:, None], band, np.where(offset == 0, 1.0, 0.0))
    coupling = np.where(interior, strength, 0.0)
    return thomas_solve(coupling, np.ones(length), coupling, right_side)


def derivative_table(length):
    positions = np.arange(length)
    offset = positions[None, :] - positions[:, None]
    distance = np.abs(offset)
    direction = np.sign(offset) * 1.0
    boundary = (positions == 0) | (positions == length - 1)
    second = (positions == 1) | (positions == length - 2)
    interior = ~(boundary | second)
    below_diag = np.where(
        interior, 1.0 / 3.0, np.where(second, 0.25, np.where(positions == length - 1, 2.0, 0.0))
    )
    above_diag = np.where(
        interior, 1.0 / 3.0, np.where(second, 0.25, np.where(positions == 0, 2.0, 0.0))
    )
    inner_rows = direction * (
        np.where(distance == 1, 7.0 / 9.0, 0.0) + np.where(distance == 2, 1.0 / 36.0, 0.0)
    )
    second_rows = direction * np.where(distance == 1, 0.75, 0.0)
    first_row = np.where(
        offset == 0, -2.5, np.where(offset == 1, 2.0, np.where(offset == 2, 0.5, 0.0))
    )
    final_row = np.where(
        offset == 0, 2.5, np.where(offset == -1, -2.0, np.where(offset == -2, -0.5, 0.0))
    )
    right_side = np.where(
        interior[:, None],
        inner_rows,
        np.where(
            second[:, None], second_rows, np.where((positions == 0)[:, None], first_row, final_row)
        ),
    )
    return thomas_solve(below_diag, np.ones(length), above_diag, right_side)


class Plan:
    def __init__(self, table, scal, cells):
        self.table, self.scal, self.cells = table, scal, cells
        self.devices = table * scal
        self.cap = max(2, 5 * GROUP // (2 * table))
        self.near = LANES // table
        self.far = self.cap - self.near
        self.quad = 4 * self.far
        assert cells == table * GROUP and table * self.quad == LANES
        self.code = 1 << (self.cap - 1).bit_length()
        self.scalars = SCAL_ALL // scal
        self.cols = self.scalars * K // LANES
        self.few = self.scalars // 4
        self.rows = self.scalars + self.few
        self.nx = BX * table


def iota(shape, dim):
    return lax.broadcasted_iota(jnp.int32, shape, dim)


def pieces_of(values, count):
    pieces = []
    for _ in range(count - 1):
        piece = values.astype(jnp.bfloat16)
        pieces.append(piece)
        values = values - piece.astype(jnp.float32)
    pieces.append(values.astype(jnp.bfloat16))
    return pieces


def dot_rows(a, b):
    return lax.dot_general(a, b, (((1,), (1,)), ((), ())), preferred_element_type=jnp.float32)


def request_kernel(plan, coords_ref, owner_ref, bin_ref, out_ref, x_ref):
    p = plan
    row_count = p.cells // LANES
    half = iota((1, LANES), 1) // GROUP
    shard_ids = iota((p.table, LANES), 0)
    owners = owner_ref[...]
    bins = bin_ref[...]
    address = ((bins >> 3) * (8 * p.cols) + (bins & 7)).astype(jnp.float32)
    hits = [owners[i : i + 1, :] == shard_ids for i in range(row_count)]
    before = iota((LANES, LANES), 0)
    after = iota((LANES, LANES), 1)
    earlier = ((before < after) & (before // GROUP == after // GROUP)).astype(jnp.bfloat16)
    ones = jnp.concatenate([h.astype(jnp.float32) for h in hits], axis=0)
    counts = jnp.dot(ones.astype(jnp.bfloat16), earlier, preferred_element_type=jnp.float32)
    x_ref[0:4, :] = coords_ref[...]
    x_ref[5:8, :] = jnp.zeros((3, p.cells), jnp.float32)
    for i in range(row_count):
        x_ref[4:5, i * LANES : (i + 1) * LANES] = address[i : i + 1, :]
    lane_rows = iota((LANES, LANES), 0)
    left, right, codes = [], [], []
    for i in range(row_count):
        span = slice(i * p.table, (i + 1) * p.table)
        rank = jnp.sum(ones[span] * counts[span], axis=0, keepdims=True).astype(jnp.int32)
        codes.append((owners[i : i + 1, :] * p.code + rank).astype(jnp.float32))
        group = 2 * i + half
        near = jnp.where(rank < p.near, group * p.near + rank, -1)
        far = jnp.where(rank >= p.near, group * p.far + rank - p.near, -1)
        right.append(
            jnp.concatenate(
                [
                    (lane_rows == near).astype(jnp.float32),
                    (lane_rows % 32 == far).astype(jnp.float32),
                ],
                axis=0,
            ).astype(jnp.bfloat16)
        )
        fields = x_ref[:, i * LANES : (i + 1) * LANES]
        chosen = jnp.where(hits[i][:, None, :], fields[None], 0.0).reshape(p.table * 8, LANES)
        left.append(jnp.concatenate(pieces_of(chosen, 3), axis=0))
    placed = dot_rows(jnp.concatenate(left, axis=1), jnp.concatenate(right, axis=1))
    total = p.table * 8
    placed = placed[0:total] + placed[total : 2 * total] + placed[2 * total :]
    sub = iota((8, LANES), 0)
    block = iota((8, LANES), 1) // 32
    for o in range(p.table):
        near_part = placed[o * 8 : (o + 1) * 8, :LANES]
        far_part = placed[o * 8 : (o + 1) * 8, LANES:]
        far_coords = jnp.sum(jnp.where(sub == block, far_part, 0.0), axis=0, keepdims=True)
        message = jnp.where(
            sub < 5,
            near_part,
            jnp.where(sub == 5, far_coords, jnp.where(sub == 6, far_part[4:5], codes[o // 2])),
        )
        for sc in range(p.scal):
            out_ref[o * p.scal + sc] = message


def spline_rows(f):
    shape = (K, f[0].shape[1])
    k = iota(shape, 0)
    product = None
    for axis, bit in ((0, 16), (1, 8), (2, 4)):
        factor = jnp.where((k & bit) != 0, f[axis], 1.0 - f[axis])
        product = factor if product is None else product * factor
    last = f[3]
    square = last * last
    cube = square * last
    remain = 1.0 - last
    basis = [
        remain * remain * remain / 6.0,
        (3.0 * cube - 6.0 * square + 4.0) / 6.0,
        (-3.0 * cube + 3.0 * square + 3.0 * last + 1.0) / 6.0,
        cube / 6.0,
    ]
    d = k & 3
    cubic = jnp.where(d == 0, basis[0], jnp.where(d == 1, basis[1], jnp.where(d == 2, basis[2], basis[3])))
    return product * cubic


def lookup_kernel(
    plan, recv_ref, table_ref, out_ref, ints_ref, near_idx, far_idx, w_near, w_far, sem, *gathered
):
    p = plan
    ints_ref[0] = recv_ref[pl.ds(4, p.devices, stride=8), :].astype(jnp.int32)
    ints_ref[1] = recv_ref[pl.ds(6, p.devices, stride=8), :].astype(jnp.int32)
    copies = [
        pltpu.make_async_copy(ints_ref.at[0], near_idx, sem.at[0]),
        pltpu.make_async_copy(ints_ref.at[1], far_idx, sem.at[1]),
    ]
    for copy in copies:
        copy.start()

    lane = iota((1, LANES), 1)
    spread = (iota((3 * K, LANES), 0) % K == iota((3 * K, LANES), 1) % K).astype(jnp.float32)
    spread = spread.astype(jnp.bfloat16)

    def weigh(u, carry):
        blocks = [
            recv_ref[pl.ds(pl.multiple_of((4 * u + i) * 8, 8), 8), :] for i in range(4)
        ]
        parts = [spline_rows([block[f : f + 1, :] for f in range(4)]) for block in blocks]
        far = []
        for f in range(4):
            row = jnp.zeros((1, LANES), jnp.float32)
            for i in range(4):
                turned = pltpu.roll(blocks[i][5:6, :], (32 * (i - f)) % LANES, 1)
                row = jnp.where(lane // 32 == i, turned, row)
            far.append(row)
        parts.append(spline_rows(far))
        rows = jnp.concatenate(parts, axis=1)
        rows = jnp.concatenate(pieces_of(rows, 3), axis=0)
        weights = lax.dot_general(
            rows, spread, (((0,), (0,)), ((), ())), preferred_element_type=jnp.float32
        )
        for i in range(4):
            src = 4 * u + i
            t, s = src // p.scal, src % p.scal
            for g in range(p.table):
                start = (g * p.scal + s) * LANES + t * p.near
                w_near[pl.ds(pl.multiple_of(start, p.near), p.near), :] = weights[
                    i * LANES + g * p.near : i * LANES + (g + 1) * p.near
                ]
            for q in range(p.table // 4):
                start = (q * p.scal + s) * LANES + t * p.quad
                row = 4 * LANES + 32 * i + q * p.quad
                w_far[pl.ds(pl.multiple_of(start, p.quad), p.quad), :] = weights[row : row + p.quad]
        return carry

    lax.fori_loop(0, p.devices // 4, weigh, 0)
    for copy in copies:
        copy.wait()

    depth = p.cols * LANES
    choose = (iota((p.scalars, depth), 0) == iota((p.scalars, depth), 1) // K).astype(jnp.float32)
    choose = jnp.concatenate([choose.astype(jnp.bfloat16)] * 2, axis=1)

    def fetch(store, slot, address):
        if p.cols == 1:
            store[pl.ds(slot, 1), :] = table_ref[pl.ds(address, 1), :]
        else:
            store[pl.ds(slot, p.cols, stride=LANES), :] = table_ref[
                pl.ds(address, p.cols, stride=8), :
            ]

    def reduce(store, weights):
        high, low = [], []
        for c in range(p.cols):
            product = store[c * LANES : (c + 1) * LANES, :] * weights
            two = pieces_of(product, 2)
            high.append(two[0])
            low.append(two[1])
        return dot_rows(choose, jnp.concatenate(high + low, axis=1))

    def near_chunks(g, carry):
        for s in range(p.scal):
            for t in range(p.table):
                for q in range(p.near):
                    fetch(gathered[s], t * p.near + q, near_idx[t * p.scal + s, g * p.near + q])
        for s in range(p.scal):
            dest = g * p.scal + s
            weights = w_near[pl.ds(pl.multiple_of(dest * LANES, LANES), LANES), :]
            out_ref[pl.ds(dest * p.rows, p.scalars), :] = reduce(gathered[s], weights)
        return carry

    lax.fori_loop(0, p.table, near_chunks, 0)
    quad_of = (lane // p.far) % 4

    def far_chunks(quad, carry):
        for s in range(p.scal):
            for t in range(p.table):
                for q in range(p.quad):
                    fetch(gathered[s], t * p.quad + q, far_idx[t * p.scal + s, quad * p.quad + q])
        for s in range(p.scal):
            chunk = quad * p.scal + s
            weights = w_far[pl.ds(pl.multiple_of(chunk * LANES, LANES), LANES), :]
            tile = reduce(gathered[s], weights)
            for i in range(4):
                message = jnp.zeros((p.few, LANES), jnp.float32)
                for b in range(4):
                    turned = pltpu.roll(
                        tile[b * p.few : (b + 1) * p.few], ((b - i) * p.far) % LANES, 1
                    )
                    message = jnp.where(quad_of == b, turned, message)
                dest = (quad * 4 + i) * p.scal + s
                out_ref[pl.ds(dest * p.rows + p.scalars, p.few), :] = message
        return carry

    lax.fori_loop(0, p.table // 4, far_chunks, 0)


def slots_kernel(plan, me_ref, recv_ref, out_ref):
    p = plan
    table_at, scal_at = me_ref[0], me_ref[1]
    width = LG * p.nx
    codes = recv_ref[pl.ds(scal_at * 8 + 7, p.table, stride=8 * p.scal), :]
    cell = iota((LANES, width), 1)
    inside = (cell // p.nx) * BX + cell % BX + GROUP * (table_at % 2)
    move = (iota((LANES, width), 0) == inside).astype(jnp.float32).astype(jnp.bfloat16)
    moved = jnp.dot(codes.astype(jnp.bfloat16), move, preferred_element_type=jnp.float32)
    x_block = (iota((p.table, width), 1) % p.nx) // BX
    moved = jnp.where(iota((p.table, width), 0) == x_block, moved, 0.0)
    code = jnp.sum(moved, axis=0, keepdims=True).astype(jnp.int32)
    shard, slot = code // p.code, code % p.code
    t = (iota((1, width), 1) % p.nx) // BX
    near = jnp.where(slot < p.near, shard * LANES + t * p.near + slot, -1)
    far = jnp.where(
        slot >= p.near,
        (shard // 4 + p.table) * LANES + t * p.quad + (shard % 4) * p.far + slot - p.near,
        -1,
    )
    chosen = jnp.where(slot < p.near, near, far)
    step = 2 * LANES
    rows = iota((step, width), 0)

    def fill(i, carry):
        start = pl.multiple_of(i * step, step)
        hit = rows == chosen - start
        out_ref[pl.ds(start, step), :] = jnp.where(hit, 1.0, 0.0).astype(jnp.bfloat16)
        return carry

    lax.fori_loop(0, out_ref.shape[0] // step, fill, 0)


def filter_kernel(plan, recv_ref, place_ref, op_ref, filtered_ref, gradient_ref, left_ref):
    p = plan
    lane = iota((1, LANES), 1)
    quad_of = (lane // p.far) % 4
    for o in range(p.table):
        for sc in range(p.scal):
            start = (o * p.scal + sc) * p.rows
            left_ref[sc * p.scalars : (sc + 1) * p.scalars, o * LANES : (o + 1) * LANES] = recv_ref[
                start : start + p.scalars, :
            ]
    for quad in range(p.table // 4):
        for sc in range(p.scal):
            messages = []
            for i in range(4):
                start = ((quad * 4 + i) * p.scal + sc) * p.rows + p.scalars
                messages.append(recv_ref[start : start + p.few, :])
            for b in range(4):
                part = jnp.zeros((p.few, LANES), jnp.float32)
                for i in range(4):
                    turned = pltpu.roll(messages[i], ((i - b) * p.far) % LANES, 1)
                    part = jnp.where(quad_of == i, turned, part)
                row = sc * p.scalars + b * p.few
                col = (p.table + quad) * LANES
                left_ref[row : row + p.few, col : col + LANES] = part
    left = jnp.concatenate(pieces_of(left_ref[...], 3), axis=0)
    values = jnp.dot(left, place_ref[...], preferred_element_type=jnp.float32)
    values = values[0:SCAL_ALL] + values[SCAL_ALL : 2 * SCAL_ALL] + values[2 * SCAL_ALL :]
    lines = jnp.concatenate(
        [values[:, r * p.nx : (r + 1) * p.nx] for r in range(LG)], axis=0
    )
    both = jnp.dot(
        lines, op_ref[...], precision=lax.Precision.HIGHEST, preferred_element_type=jnp.float32
    )
    for r in range(LG):
        rows = slice(r * SCAL_ALL, (r + 1) * SCAL_ALL)
        filtered_ref[:, r, :] = both[rows, : p.nx]
        gradient_ref[:, r, :] = both[rows, p.nx :]


VMEM = pl.BlockSpec(memory_space=pltpu.VMEM)
SMEM = pl.BlockSpec(memory_space=pltpu.SMEM)


def call(kernel, plan, out_shape, in_specs, scratch, limit, cost, name):
    many = isinstance(out_shape, tuple)
    return pl.pallas_call(
        functools.partial(kernel, plan),
        out_shape=out_shape,
        in_specs=in_specs,
        out_specs=(VMEM,) * len(out_shape) if many else VMEM,
        scratch_shapes=scratch,
        compiler_params=pltpu.CompilerParams(vmem_limit_bytes=limit << 20),
        cost_estimate=pl.CostEstimate(flops=cost, bytes_accessed=cost // 256, transcendentals=0),
        name=name,
    )


def exchange(array):
    return lax.all_to_all(array, AXES, split_axis=0, concat_axis=0, tiled=True)


def on_device(plan, cell_coords, flamelet_table, owner_shard, local_bin):
    p = plan
    f32, i32 = jnp.float32, jnp.int32
    row_count = p.cells // LANES
    owners = owner_shard.reshape(row_count, LANES)
    bins = local_bin.reshape(row_count, LANES)
    requests = call(
        request_kernel,
        p,
        jax.ShapeDtypeStruct((p.devices, 8, LANES), f32),
        [VMEM] * 3,
        [pltpu.VMEM((8, p.cells), f32)],
        32,
        1 << 20,
        "requests",
    )(cell_coords, owners, bins)
    received = exchange(requests).reshape(p.devices * 8, LANES)

    bin_count, depth = flamelet_table.shape
    table = flamelet_table.reshape(bin_count // 8, 8, p.cols, LANES).transpose(0, 2, 1, 3)
    table = table.reshape(bin_count * p.cols, LANES)
    replies = call(
        lookup_kernel,
        p,
        jax.ShapeDtypeStruct((p.devices * p.rows, LANES), f32),
        [VMEM] * 2,
        [
            pltpu.VMEM((2, p.devices, LANES), i32),
            pltpu.SMEM((p.devices, LANES), i32),
            pltpu.SMEM((p.devices, LANES), i32),
            pltpu.VMEM((p.devices * LANES, LANES), f32),
            pltpu.VMEM((p.devices * LANES // 4, LANES), f32),
            pltpu.SemaphoreType.DMA((2,)),
        ]
        + [pltpu.VMEM((p.cols * LANES, LANES), f32) for _ in range(p.scal)],
        48,
        1 << 24,
        "lookup",
    )(received, table)
    answers = exchange(replies.reshape(p.devices, 1, p.rows * LANES))
    answers = answers.reshape(p.devices * p.rows, LANES)

    me = jnp.stack([lax.axis_index("table"), lax.axis_index("scal")]).astype(i32)
    place = call(
        slots_kernel,
        p,
        jax.ShapeDtypeStruct((p.table * 5 * LANES // 4, LG * p.nx), jnp.bfloat16),
        [SMEM, VMEM],
        [],
        48,
        1 << 24,
        "slots",
    )(me, received)
    filter_op = filter_table(p.nx).T
    both_op = np.concatenate([filter_op, filter_op @ derivative_table(p.nx).T], axis=1)
    out = jax.ShapeDtypeStruct((SCAL_ALL, LG, p.nx), f32)
    return call(
        filter_kernel,
        p,
        (out, out),
        [VMEM] * 3,
        [pltpu.VMEM((SCAL_ALL, p.table * 5 * LANES // 4), f32)],
        48,
        1 << 24,
        "filter",
    )(answers, place, jnp.asarray(both_op.astype(np.float32)))


def solution(mesh):
    table, scal = mesh.shape["table"], mesh.shape["scal"]

    def step(cell_coords, flamelet_table, owner_shard, local_bin):
        plan = Plan(table, scal, cell_coords.shape[1])
        return on_device(plan, cell_coords, flamelet_table, owner_shard, local_bin)

    return jax.shard_map(
        step,
        mesh=mesh,
        in_specs=(
            P(None, AXES),
            P("table", "scal"),
            P(AXES, None),
            P(AXES),
        ),
        out_specs=(P(None, AXES, None), P(None, AXES, None)),
        check_vma=False,
    )
```

```python
import functools

import jax
import jax.numpy as jnp
import numpy as np
from jax import lax
from jax.experimental import pallas as pl
from jax.experimental.pallas import tpu as pltpu
from jax.sharding import PartitionSpec as P

SCAL_ALL = 32
K = 32
BX = 8
LG = 8
GROUP = BX * LG
LANES = 128
AXES = ("table", "scal")

strength = 0.499


def thomas_solve(below, middle, above, right_side):
    length = middle.shape[0]
    upper_factor = np.zeros(length)
    solved = np.zeros(right_side.shape)
    for row in range(length):
        if row == 0:
            denom = middle[0]
            solved[0] = right_side[0] / denom
        else:
            denom = middle[row] - below[row] * upper_factor[row - 1]
            solved[row] = (right_side[row] - below[row] * solved[row - 1]) / denom
        upper_factor[row] = above[row] / denom
    for row in range(length - 2, -1, -1):
        solved[row] = solved[row] - upper_factor[row] * solved[row + 1]
    return solved


def filter_table(length):
    positions = np.arange(length)
    offset = positions[None, :] - positions[:, None]
    distance = np.abs(offset)
    interior = (positions >= 3) & (positions <= length - 4)
    coeffs = [
        (11.0 + 10.0 * strength) / 16.0,
        (15.0 + 34.0 * strength) / 64.0,
        (-3.0 + 6.0 * strength) / 32.0,
        (1.0 - 2.0 * strength) / 64.0,
    ]
    band = np.zeros((length, length))
    for reach in range(4):
        band = band + np.where(distance == reach, coeffs[reach], 0.0)
    right_side = np.where(interior[:, None], band, np.where(offset == 0, 1.0, 0.0))
    coupling = np.where(interior, strength, 0.0)
    return thomas_solve(coupling, np.ones(length), coupling, right_side)


def derivative_table(length):
    positions = np.arange(length)
    offset = positions[None, :] - positions[:, None]
    distance = np.abs(offset)
    direction = np.sign(offset) * 1.0
    boundary = (positions == 0) | (positions == length - 1)
    second = (positions == 1) | (positions == length - 2)
    interior = ~(boundary | second)
    below_diag = np.where(
        interior, 1.0 / 3.0, np.where(second, 0.25, np.where(positions == length - 1, 2.0, 0.0))
    )
    above_diag = np.where(
        interior, 1.0 / 3.0, np.where(second, 0.25, np.where(positions == 0, 2.0, 0.0))
    )
    inner_rows = direction * (
        np.where(distance == 1, 7.0 / 9.0, 0.0) + np.where(distance == 2, 1.0 / 36.0, 0.0)
    )
    second_rows = direction * np.where(distance == 1, 0.75, 0.0)
    first_row = np.where(
        offset == 0, -2.5, np.where(offset == 1, 2.0, np.where(offset == 2, 0.5, 0.0))
    )
    final_row = np.where(
        offset == 0, 2.5, np.where(offset == -1, -2.0, np.where(offset == -2, -0.5, 0.0))
    )
    right_side = np.where(
        interior[:, None],
        inner_rows,
        np.where(
            second[:, None], second_rows, np.where((positions == 0)[:, None], first_row, final_row)
        ),
    )
    return thomas_solve(below_diag, np.ones(length), above_diag, right_side)


class Plan:
    def __init__(self, table, scal, cells):
        self.table, self.scal, self.cells = table, scal, cells
        self.devices = table * scal
        self.cap = max(2, 5 * GROUP // (2 * table))
        self.near = LANES // table
        self.far = self.cap - self.near
        self.quad = 4 * self.far
        assert cells == table * GROUP and table * self.quad == LANES
        self.code = 1 << (self.cap - 1).bit_length()
        self.scalars = SCAL_ALL // scal
        self.cols = self.scalars * K // LANES
        self.few = self.scalars // 4
        self.rows = self.scalars + self.few
        self.nx = BX * table


def iota(shape, dim):
    return lax.broadcasted_iota(jnp.int32, shape, dim)


def pieces_of(values, count):
    pieces = []
    for _ in range(count - 1):
        piece = values.astype(jnp.bfloat16)
        pieces.append(piece)
        values = values - piece.astype(jnp.float32)
    pieces.append(values.astype(jnp.bfloat16))
    return pieces


def dot_rows(a, b):
    return lax.dot_general(a, b, (((1,), (1,)), ((), ())), preferred_element_type=jnp.float32)


def request_kernel(plan, coords_in, owner_in, bin_in, out_ref, x_ref, coords_ref, owner_ref, bin_ref, sem):
    p = plan
    row_count = p.cells // LANES
    copies = [
        pltpu.make_async_copy(owner_in, owner_ref, sem.at[0]),
        pltpu.make_async_copy(bin_in, bin_ref, sem.at[1]),
        pltpu.make_async_copy(coords_in, coords_ref, sem.at[2]),
    ]
    for copy in copies:
        copy.start()
    for copy in copies:
        copy.wait()
    half = iota((1, LANES), 1) // GROUP
    shard_ids = iota((p.table, LANES), 0)
    owners = owner_ref[...]
    bins = bin_ref[...]
    address = ((bins >> 3) * (8 * p.cols) + (bins & 7)).astype(jnp.float32)
    hits = [owners[i : i + 1, :] == shard_ids for i in range(row_count)]
    before = iota((LANES, LANES), 0)
    after = iota((LANES, LANES), 1)
    earlier = ((before < after) & (before // GROUP == after // GROUP)).astype(jnp.bfloat16)
    ones = jnp.concatenate([h.astype(jnp.float32) for h in hits], axis=0)
    counts = jnp.dot(ones.astype(jnp.bfloat16), earlier, preferred_element_type=jnp.float32)
    x_ref[0:4, :] = coords_ref[...]
    x_ref[5:8, :] = jnp.zeros((3, p.cells), jnp.float32)
    for i in range(row_count):
        x_ref[4:5, i * LANES : (i + 1) * LANES] = address[i : i + 1, :]
    lane_rows = iota((LANES, LANES), 0)
    left, right, codes = [], [], []
    for i in range(row_count):
        span = slice(i * p.table, (i + 1) * p.table)
        rank = jnp.sum(ones[span] * counts[span], axis=0, keepdims=True).astype(jnp.int32)
        codes.append((owners[i : i + 1, :] * p.code + rank).astype(jnp.float32))
        group = 2 * i + half
        near = jnp.where(rank < p.near, group * p.near + rank, -1)
        far = jnp.where(rank >= p.near, group * p.far + rank - p.near, -1)
        right.append(
            jnp.concatenate(
                [
                    (lane_rows == near).astype(jnp.float32),
                    (lane_rows % 32 == far).astype(jnp.float32),
                ],
                axis=0,
            ).astype(jnp.bfloat16)
        )
        fields = x_ref[:, i * LANES : (i + 1) * LANES]
        chosen = jnp.where(hits[i][:, None, :], fields[None], 0.0).reshape(p.table * 8, LANES)
        left.append(jnp.concatenate(pieces_of(chosen, 3), axis=0))
    placed = dot_rows(jnp.concatenate(left, axis=1), jnp.concatenate(right, axis=1))
    total = p.table * 8
    placed = placed[0:total] + placed[total : 2 * total] + placed[2 * total :]
    sub = iota((8, LANES), 0)
    block = iota((8, LANES), 1) // 32
    for o in range(p.table):
        near_part = placed[o * 8 : (o + 1) * 8, :LANES]
        far_part = placed[o * 8 : (o + 1) * 8, LANES:]
        far_coords = jnp.sum(jnp.where(sub == block, far_part, 0.0), axis=0, keepdims=True)
        message = jnp.where(
            sub < 5,
            near_part,
            jnp.where(sub == 5, far_coords, jnp.where(sub == 6, far_part[4:5], codes[o // 2])),
        )
        for sc in range(p.scal):
            out_ref[o * p.scal + sc] = message


def spline_rows(f):
    shape = (K, f[0].shape[1])
    k = iota(shape, 0)
    product = None
    for axis, bit in ((0, 16), (1, 8), (2, 4)):
        factor = jnp.where((k & bit) != 0, f[axis], 1.0 - f[axis])
        product = factor if product is None else product * factor
    last = f[3]
    square = last * last
    cube = square * last
    remain = 1.0 - last
    basis = [
        remain * remain * remain / 6.0,
        (3.0 * cube - 6.0 * square + 4.0) / 6.0,
        (-3.0 * cube + 3.0 * square + 3.0 * last + 1.0) / 6.0,
        cube / 6.0,
    ]
    d = k & 3
    cubic = jnp.where(d == 0, basis[0], jnp.where(d == 1, basis[1], jnp.where(d == 2, basis[2], basis[3])))
    return product * cubic


def lookup_kernel(
    plan,
    recv_ref,
    table_ref,
    out_ref,
    ints_ref,
    near_idx,
    far_idx,
    w_near,
    w_far,
    g_near,
    g_far,
    sem,
):
    p = plan
    ints_ref[0] = recv_ref[pl.ds(4, p.devices, stride=8), :].astype(jnp.int32)
    ints_ref[1] = recv_ref[pl.ds(6, p.devices, stride=8), :].astype(jnp.int32)
    copies = [
        pltpu.make_async_copy(ints_ref.at[0], near_idx, sem.at[0]),
        pltpu.make_async_copy(ints_ref.at[1], far_idx, sem.at[1]),
    ]
    for copy in copies:
        copy.start()

    lane = iota((1, LANES), 1)
    spread = (iota((3 * K, LANES), 0) % K == iota((3 * K, LANES), 1) % K).astype(jnp.float32)
    spread = spread.astype(jnp.bfloat16)
    chunk_rows = LANES * p.cols
    for copy in copies:
        copy.wait()

    def fetch(store, at, address):
        if p.cols == 1:
            store[pl.ds(at, 1), :] = table_ref[pl.ds(address, 1), :]
        else:
            store[pl.ds(at, p.cols, stride=8), :] = table_ref[pl.ds(address, p.cols, stride=8), :]

    def first_of(chunk, slot):
        return chunk * chunk_rows + (slot // 8) * (8 * p.cols) + slot % 8

    def serve(u, carry):
        blocks = [
            recv_ref[pl.ds(pl.multiple_of((4 * u + i) * 8, 8), 8), :] for i in range(4)
        ]
        parts = [spline_rows([block[f : f + 1, :] for f in range(4)]) for block in blocks]
        far = []
        for f in range(4):
            row = jnp.zeros((1, LANES), jnp.float32)
            for i in range(4):
                turned = pltpu.roll(blocks[i][5:6, :], (32 * (i - f)) % LANES, 1)
                row = jnp.where(lane // 32 == i, turned, row)
            far.append(row)
        parts.append(spline_rows(far))
        rows = jnp.concatenate(parts, axis=1)
        rows = jnp.concatenate(pieces_of(rows, 3), axis=0)
        weights = lax.dot_general(
            rows, spread, (((0,), (0,)), ((), ())), preferred_element_type=jnp.float32
        )
        for i in range(4):
            src = 4 * u + i
            t, s = src // p.scal, src % p.scal
            near_at, far_at = first_of(s, t * p.near), first_of(s, t * p.quad)
            for g in range(p.table):
                for q in range(p.near):
                    fetch(
                        g_near,
                        near_at + g * p.scal * chunk_rows + q,
                        near_idx[src, g * p.near + q],
                    )
                start = (g * p.scal + s) * LANES + t * p.near
                w_near[pl.ds(pl.multiple_of(start, p.near), p.near), :] = weights[
                    i * LANES + g * p.near : i * LANES + (g + 1) * p.near
                ]
            for q in range(p.table // 4):
                for j in range(p.quad):
                    fetch(
                        g_far,
                        far_at + q * p.scal * chunk_rows + j,
                        far_idx[src, q * p.quad + j],
                    )
                start = (q * p.scal + s) * LANES + t * p.quad
                row = 4 * LANES + 32 * i + q * p.quad
                w_far[pl.ds(pl.multiple_of(start, p.quad), p.quad), :] = weights[row : row + p.quad]
        return carry

    lax.fori_loop(0, p.devices // 4, serve, 0)

    step = min(2, p.cols)
    depth = step * LANES
    choices = []
    for c in range(0, p.cols, step):
        choose = iota((p.scalars, depth), 0) == (c * LANES + iota((p.scalars, depth), 1)) // K
        choices.append(choose.astype(jnp.float32).astype(jnp.bfloat16))

    def reduce(store, weight_ref, chunk):
        weights = weight_ref[pl.ds(pl.multiple_of(chunk * LANES, LANES), 2 * LANES), :]
        first = pl.multiple_of(chunk * chunk_rows, chunk_rows)
        total = None
        for c in range(0, p.cols, step):
            high, low = [], []
            for e in range(c, c + step):
                tiles = [
                    store[pl.ds(first + (b * p.cols + e) * 8, 8), :] for b in range(LANES // 4)
                ]
                two = pieces_of(jnp.concatenate(tiles, axis=0) * weights, 2)
                high.append(two[0])
                low.append(two[1])
            for half in (high, low):
                part = dot_rows(choices[c // step], jnp.concatenate(half, axis=1))
                total = part if total is None else total + part
        return total

    def near_chunks(pair, carry):
        both = reduce(g_near, w_near, 2 * pair)
        for i in range(2):
            out_ref[pl.ds((2 * pair + i) * p.rows, p.scalars), :] = both[
                :, i * LANES : (i + 1) * LANES
            ]
        return carry

    lax.fori_loop(0, p.devices // 2, near_chunks, 0)
    quad_of = (lane // p.far) % 4

    def far_chunks(pair, carry):
        both = reduce(g_far, w_far, 2 * pair)
        for n in range(2):
            chunk = 2 * pair + n
            quad, s = chunk // p.scal, chunk % p.scal
            tile = both[:, n * LANES : (n + 1) * LANES]
            for i in range(4):
                message = jnp.zeros((p.few, LANES), jnp.float32)
                for b in range(4):
                    turned = pltpu.roll(
                        tile[b * p.few : (b + 1) * p.few], ((b - i) * p.far) % LANES, 1
                    )
                    message = jnp.where(quad_of == b, turned, message)
                dest = (quad * 4 + i) * p.scal + s
                out_ref[pl.ds(dest * p.rows + p.scalars, p.few), :] = message
        return carry

    lax.fori_loop(0, p.devices // 8, far_chunks, 0)


def slots_kernel(plan, me_ref, recv_ref, out_ref):
    p = plan
    table_at, scal_at = me_ref[0], me_ref[1]
    width = LG * p.nx
    codes = recv_ref[pl.ds(scal_at * 8 + 7, p.table, stride=8 * p.scal), :]
    cell = iota((LANES, width), 1)
    inside = (cell // p.nx) * BX + cell % BX + GROUP * (table_at % 2)
    move = (iota((LANES, width), 0) == inside).astype(jnp.float32).astype(jnp.bfloat16)
    moved = jnp.dot(codes.astype(jnp.bfloat16), move, preferred_element_type=jnp.float32)
    x_block = (iota((p.table, width), 1) % p.nx) // BX
    moved = jnp.where(iota((p.table, width), 0) == x_block, moved, 0.0)
    code = jnp.sum(moved, axis=0, keepdims=True).astype(jnp.int32)
    shard, slot = code // p.code, code % p.code
    t = (iota((1, width), 1) % p.nx) // BX
    near = jnp.where(slot < p.near, shard * LANES + t * p.near + slot, -1)
    far = jnp.where(
        slot >= p.near,
        (shard // 4 + p.table) * LANES + t * p.quad + (shard % 4) * p.far + slot - p.near,
        -1,
    )
    chosen = jnp.where(slot < p.near, near, far)
    step = 2 * LANES
    rows = iota((step, width), 0)

    def fill(i, carry):
        start = pl.multiple_of(i * step, step)
        hit = rows == chosen - start
        out_ref[pl.ds(start, step), :] = jnp.where(hit, 1.0, 0.0).astype(jnp.bfloat16)
        return carry

    lax.fori_loop(0, out_ref.shape[0] // step, fill, 0)


def filter_kernel(plan, recv_ref, place_ref, op_ref, filtered_ref, gradient_ref, left_ref):
    p = plan
    lane = iota((1, LANES), 1)
    quad_of = (lane // p.far) % 4
    for o in range(p.table):
        for sc in range(p.scal):
            start = (o * p.scal + sc) * p.rows
            left_ref[sc * p.scalars : (sc + 1) * p.scalars, o * LANES : (o + 1) * LANES] = recv_ref[
                start : start + p.scalars, :
            ]
    for quad in range(p.table // 4):
        for sc in range(p.scal):
            messages = []
            for i in range(4):
                start = ((quad * 4 + i) * p.scal + sc) * p.rows + p.scalars
                messages.append(recv_ref[start : start + p.few, :])
            for b in range(4):
                part = jnp.zeros((p.few, LANES), jnp.float32)
                for i in range(4):
                    turned = pltpu.roll(messages[i], ((i - b) * p.far) % LANES, 1)
                    part = jnp.where(quad_of == i, turned, part)
                row = sc * p.scalars + b * p.few
                col = (p.table + quad) * LANES
                left_ref[row : row + p.few, col : col + LANES] = part
    left = jnp.concatenate(pieces_of(left_ref[...], 3), axis=0)
    values = jnp.dot(left, place_ref[...], preferred_element_type=jnp.float32)
    values = values[0:SCAL_ALL] + values[SCAL_ALL : 2 * SCAL_ALL] + values[2 * SCAL_ALL :]
    lines = jnp.concatenate(
        [values[:, r * p.nx : (r + 1) * p.nx] for r in range(LG)], axis=0
    )
    both = jnp.dot(
        lines, op_ref[...], precision=lax.Precision.HIGHEST, preferred_element_type=jnp.float32
    )
    for r in range(LG):
        rows = slice(r * SCAL_ALL, (r + 1) * SCAL_ALL)
        filtered_ref[:, r, :] = both[rows, : p.nx]
        gradient_ref[:, r, :] = both[rows, p.nx :]


VMEM = pl.BlockSpec(memory_space=pltpu.VMEM)
SMEM = pl.BlockSpec(memory_space=pltpu.SMEM)


def call(kernel, plan, out_shape, in_specs, scratch, limit, cost, name):
    many = isinstance(out_shape, tuple)
    return pl.pallas_call(
        functools.partial(kernel, plan),
        out_shape=out_shape,
        in_specs=in_specs,
        out_specs=(VMEM,) * len(out_shape) if many else VMEM,
        scratch_shapes=scratch,
        compiler_params=pltpu.CompilerParams(vmem_limit_bytes=limit << 20),
        cost_estimate=pl.CostEstimate(flops=cost, bytes_accessed=cost // 256, transcendentals=0),
        name=name,
    )


def exchange(array):
    return lax.all_to_all(array, AXES, split_axis=0, concat_axis=0, tiled=True)


def on_device(plan, cell_coords, flamelet_table, owner_shard, local_bin):
    p = plan
    f32, i32 = jnp.float32, jnp.int32
    row_count = p.cells // LANES
    owners = owner_shard.reshape(row_count, LANES)
    bins = local_bin.reshape(row_count, LANES)
    requests = call(
        request_kernel,
        p,
        jax.ShapeDtypeStruct((p.devices, 8, LANES), f32),
        [pl.BlockSpec(memory_space=pl.ANY)] * 3,
        [
            pltpu.VMEM((8, p.cells), f32),
            pltpu.VMEM(cell_coords.shape, f32),
            pltpu.VMEM(owners.shape, i32),
            pltpu.VMEM(bins.shape, i32),
            pltpu.SemaphoreType.DMA((3,)),
        ],
        32,
        1 << 20,
        "requests",
    )(cell_coords, owners, bins)
    received = exchange(requests).reshape(p.devices * 8, LANES)

    bin_count, depth = flamelet_table.shape
    table = flamelet_table.reshape(bin_count // 8, 8, p.cols, LANES).transpose(0, 2, 1, 3)
    table = table.reshape(bin_count * p.cols, LANES)
    replies = call(
        lookup_kernel,
        p,
        jax.ShapeDtypeStruct((p.devices * p.rows, LANES), f32),
        [VMEM] * 2,
        [
            pltpu.VMEM((2, p.devices, LANES), i32),
            pltpu.SMEM((p.devices, LANES), i32),
            pltpu.SMEM((p.devices, LANES), i32),
            pltpu.VMEM((p.devices * LANES, LANES), f32),
            pltpu.VMEM((p.devices * LANES // 4, LANES), f32),
            pltpu.VMEM((p.devices * LANES * p.cols, LANES), f32),
            pltpu.VMEM((p.devices * LANES * p.cols // 4, LANES), f32),
            pltpu.SemaphoreType.DMA((2,)),
        ],
        8 + (5 * p.devices * (p.cols + 1)) // 64 + (depth * bin_count >> 18),
        1 << 24,
        "lookup",
    )(received, table)
    answers = exchange(replies.reshape(p.devices, 1, p.rows * LANES))
    answers = answers.reshape(p.devices * p.rows, LANES)

    me = jnp.stack([lax.axis_index("table"), lax.axis_index("scal")]).astype(i32)
    place = call(
        slots_kernel,
        p,
        jax.ShapeDtypeStruct((p.table * 5 * LANES // 4, LG * p.nx), jnp.bfloat16),
        [SMEM, VMEM],
        [],
        8 + p.nx * p.table // 128,
        1 << 24,
        "slots",
    )(me, received)
    filter_op = filter_table(p.nx).T
    both_op = np.concatenate([filter_op, filter_op @ derivative_table(p.nx).T], axis=1)
    out = jax.ShapeDtypeStruct((SCAL_ALL, LG, p.nx), f32)
    return call(
        filter_kernel,
        p,
        (out, out),
        [VMEM] * 3,
        [pltpu.VMEM((SCAL_ALL, p.table * 5 * LANES // 4), f32)],
        8 + p.nx * p.table // 64,
        1 << 24,
        "filter",
    )(answers, place, jnp.asarray(both_op.astype(np.float32)))


def solution(mesh):
    table, scal = mesh.shape["table"], mesh.shape["scal"]

    def step(cell_coords, flamelet_table, owner_shard, local_bin):
        plan = Plan(table, scal, cell_coords.shape[1])
        return on_device(plan, cell_coords, flamelet_table, owner_shard, local_bin)

    return jax.shard_map(
        step,
        mesh=mesh,
        in_specs=(
            P(None, AXES),
            P("table", "scal"),
            P(AXES, None),
            P(AXES),
        ),
        out_specs=(P(None, AXES, None), P(None, AXES, None)),
        check_vma=False,
    )
```

```python
import functools

import jax
import jax.numpy as jnp
import numpy as np
from jax import lax
from jax.experimental import pallas as pl
from jax.experimental.pallas import tpu as pltpu
from jax.sharding import PartitionSpec as P

SCAL_ALL = 32
K = 32
BX = 8
LG = 8
GROUP = BX * LG
LANES = 128
AXES = ("table", "scal")
BATCH = 4
PARTS = 4

strength = 0.499


def thomas_solve(below, middle, above, right_side):
    length = middle.shape[0]
    upper_factor = np.zeros(length)
    solved = np.zeros(right_side.shape)
    for row in range(length):
        if row == 0:
            denom = middle[0]
            solved[0] = right_side[0] / denom
        else:
            denom = middle[row] - below[row] * upper_factor[row - 1]
            solved[row] = (right_side[row] - below[row] * solved[row - 1]) / denom
        upper_factor[row] = above[row] / denom
    for row in range(length - 2, -1, -1):
        solved[row] = solved[row] - upper_factor[row] * solved[row + 1]
    return solved


def filter_table(length):
    positions = np.arange(length)
    offset = positions[None, :] - positions[:, None]
    distance = np.abs(offset)
    interior = (positions >= 3) & (positions <= length - 4)
    coeffs = [
        (11.0 + 10.0 * strength) / 16.0,
        (15.0 + 34.0 * strength) / 64.0,
        (-3.0 + 6.0 * strength) / 32.0,
        (1.0 - 2.0 * strength) / 64.0,
    ]
    band = np.zeros((length, length))
    for reach in range(4):
        band = band + np.where(distance == reach, coeffs[reach], 0.0)
    right_side = np.where(interior[:, None], band, np.where(offset == 0, 1.0, 0.0))
    coupling = np.where(interior, strength, 0.0)
    return thomas_solve(coupling, np.ones(length), coupling, right_side)


def derivative_table(length):
    positions = np.arange(length)
    offset = positions[None, :] - positions[:, None]
    distance = np.abs(offset)
    direction = np.sign(offset) * 1.0
    boundary = (positions == 0) | (positions == length - 1)
    second = (positions == 1) | (positions == length - 2)
    interior = ~(boundary | second)
    below_diag = np.where(
        interior, 1.0 / 3.0, np.where(second, 0.25, np.where(positions == length - 1, 2.0, 0.0))
    )
    above_diag = np.where(
        interior, 1.0 / 3.0, np.where(second, 0.25, np.where(positions == 0, 2.0, 0.0))
    )
    inner_rows = direction * (
        np.where(distance == 1, 7.0 / 9.0, 0.0) + np.where(distance == 2, 1.0 / 36.0, 0.0)
    )
    second_rows = direction * np.where(distance == 1, 0.75, 0.0)
    first_row = np.where(
        offset == 0, -2.5, np.where(offset == 1, 2.0, np.where(offset == 2, 0.5, 0.0))
    )
    final_row = np.where(
        offset == 0, 2.5, np.where(offset == -1, -2.0, np.where(offset == -2, -0.5, 0.0))
    )
    right_side = np.where(
        interior[:, None],
        inner_rows,
        np.where(
            second[:, None], second_rows, np.where((positions == 0)[:, None], first_row, final_row)
        ),
    )
    return thomas_solve(below_diag, np.ones(length), above_diag, right_side)


class Plan:
    def __init__(self, table, scal, cells):
        self.table, self.scal, self.cells = table, scal, cells
        self.devices = table * scal
        self.cap = max(2, 5 * GROUP // (2 * table))
        self.near = LANES // table
        self.far = self.cap - self.near
        self.quad = 4 * self.far
        assert cells == table * GROUP and table * self.quad == LANES
        self.code = 1 << (self.cap - 1).bit_length()
        self.scalars = SCAL_ALL // scal
        self.cols = self.scalars * K // LANES
        self.few = self.scalars // 4
        self.rows = self.scalars + self.few
        self.nx = BX * table
        self.chunks = self.devices + self.devices // 4


def iota(shape, dim):
    return lax.broadcasted_iota(jnp.int32, shape, dim)


def pieces_of(values, count):
    pieces = []
    for _ in range(count - 1):
        piece = values.astype(jnp.bfloat16)
        pieces.append(piece)
        values = values - piece.astype(jnp.float32)
    pieces.append(values.astype(jnp.bfloat16))
    return pieces


def dot_rows(a, b):
    return lax.dot_general(a, b, (((1,), (1,)), ((), ())), preferred_element_type=jnp.float32)


def request_kernel(plan, coords_in, owner_in, bin_in, out_ref, x_ref, coords_ref, owner_ref, bin_ref, sem):
    p = plan
    row_count = p.cells // LANES
    copies = [
        pltpu.make_async_copy(owner_in, owner_ref, sem.at[0]),
        pltpu.make_async_copy(bin_in, bin_ref, sem.at[1]),
        pltpu.make_async_copy(coords_in, coords_ref, sem.at[2]),
    ]
    for copy in copies:
        copy.start()
    for copy in copies:
        copy.wait()
    half = iota((1, LANES), 1) // GROUP
    shard_ids = iota((p.table, LANES), 0)
    owners = owner_ref[...]
    bins = bin_ref[...]
    address = ((bins >> 3) * (8 * p.cols) + (bins & 7)).astype(jnp.float32)
    hits = [owners[i : i + 1, :] == shard_ids for i in range(row_count)]
    before = iota((LANES, LANES), 0)
    after = iota((LANES, LANES), 1)
    earlier = ((before < after) & (before // GROUP == after // GROUP)).astype(jnp.bfloat16)
    ones = jnp.concatenate([h.astype(jnp.float32) for h in hits], axis=0)
    counts = jnp.dot(ones.astype(jnp.bfloat16), earlier, preferred_element_type=jnp.float32)
    x_ref[0:4, :] = coords_ref[...]
    x_ref[5:8, :] = jnp.zeros((3, p.cells), jnp.float32)
    for i in range(row_count):
        x_ref[4:5, i * LANES : (i + 1) * LANES] = address[i : i + 1, :]
    lane_rows = iota((LANES, LANES), 0)
    left, right, codes = [], [], []
    for i in range(row_count):
        span = slice(i * p.table, (i + 1) * p.table)
        rank = jnp.sum(ones[span] * counts[span], axis=0, keepdims=True).astype(jnp.int32)
        codes.append((owners[i : i + 1, :] * p.code + rank).astype(jnp.float32))
        group = 2 * i + half
        near = jnp.where(rank < p.near, group * p.near + rank, -1)
        far = jnp.where(rank >= p.near, group * p.far + rank - p.near, -1)
        right.append(
            jnp.concatenate(
                [
                    (lane_rows == near).astype(jnp.float32),
                    (lane_rows % 32 == far).astype(jnp.float32),
                ],
                axis=0,
            ).astype(jnp.bfloat16)
        )
        fields = x_ref[:, i * LANES : (i + 1) * LANES]
        chosen = jnp.where(hits[i][:, None, :], fields[None], 0.0).reshape(p.table * 8, LANES)
        left.append(jnp.concatenate(pieces_of(chosen, 3), axis=0))
    placed = dot_rows(jnp.concatenate(left, axis=1), jnp.concatenate(right, axis=1))
    total = p.table * 8
    placed = placed[0:total] + placed[total : 2 * total] + placed[2 * total :]
    sub = iota((8, LANES), 0)
    block = iota((8, LANES), 1) // 32
    for o in range(p.table):
        near_part = placed[o * 8 : (o + 1) * 8, :LANES]
        far_part = placed[o * 8 : (o + 1) * 8, LANES:]
        far_coords = jnp.sum(jnp.where(sub == block, far_part, 0.0), axis=0, keepdims=True)
        message = jnp.where(
            sub < 5,
            near_part,
            jnp.where(sub == 5, far_coords, jnp.where(sub == 6, far_part[4:5], codes[o // 2])),
        )
        for sc in range(p.scal):
            out_ref[o * p.scal + sc] = message


def spline_rows(f):
    shape = (K, f[0].shape[1])
    k = iota(shape, 0)
    product = None
    for axis, bit in ((0, 16), (1, 8), (2, 4)):
        factor = jnp.where((k & bit) != 0, f[axis], 1.0 - f[axis])
        product = factor if product is None else product * factor
    last = f[3]
    square = last * last
    cube = square * last
    remain = 1.0 - last
    basis = [
        remain * remain * remain / 6.0,
        (3.0 * cube - 6.0 * square + 4.0) / 6.0,
        (-3.0 * cube + 3.0 * square + 3.0 * last + 1.0) / 6.0,
        cube / 6.0,
    ]
    d = k & 3
    cubic = jnp.where(d == 0, basis[0], jnp.where(d == 1, basis[1], jnp.where(d == 2, basis[2], basis[3])))
    return product * cubic


def swap_blocks(x, count, width):
    row, block = iota(x.shape, 0), iota(x.shape, 1) // width
    bit = 1
    while bit < count:
        up = pltpu.roll(pltpu.roll(x, x.shape[0] - bit, 0), bit * width, 1)
        down = pltpu.roll(pltpu.roll(x, bit, 0), LANES - bit * width, 1)
        low_row, low_block = (row & bit) == 0, (block & bit) == 0
        x = jnp.where(low_row == low_block, x, jnp.where(low_row, up, down))
        bit *= 2
    return x


def lookup_kernel(
    plan,
    recv_ref,
    table_in,
    out_ref,
    table_ref,
    ints_ref,
    idx_ref,
    field_ref,
    tile_ref,
    sem,
    *stores,
):
    p = plan
    quads = p.table // 4
    part = table_ref.shape[0] // PARTS
    loads = [
        pltpu.make_async_copy(
            table_in.at[pl.ds(i * part, part)], table_ref.at[pl.ds(i * part, part)], sem.at[1 + i]
        )
        for i in range(PARTS)
    ]
    for load in loads[: PARTS // 2]:
        load.start()

    def received(r):
        rows = [recv_ref[pl.ds(s * 8 + r, p.table, stride=8 * p.scal), :] for s in range(p.scal)]
        return jnp.concatenate(rows, axis=0)

    addresses = jnp.concatenate([received(4), received(6)], axis=0)
    addresses = swap_blocks(addresses, p.table, p.near).astype(jnp.int32)
    ints_ref[0 : p.devices, :] = addresses[: p.devices]
    for s in range(p.scal):
        first = p.devices + s * p.table
        to = p.devices + s * quads
        ints_ref[to : to + quads, :] = addresses[first : first + quads]
    copy = pltpu.make_async_copy(ints_ref, idx_ref, sem.at[0])
    copy.start()
    for load in loads[PARTS // 2 :]:
        load.start()
    fields = jnp.concatenate([received(f) for f in (0, 1, 2, 3, 5)], axis=0)
    fields = swap_blocks(fields, p.table, p.near)
    for f in range(4):
        field_ref[f * p.chunks : f * p.chunks + p.devices, :] = fields[
            f * p.devices : (f + 1) * p.devices
        ]
        for s in range(p.scal):
            first = 4 * p.devices + s * p.table + f * quads
            to = f * p.chunks + p.devices + s * quads
            field_ref[to : to + quads, :] = fields[first : first + quads]
    copy.wait()

    part_rows = p.scalars * 8
    shape = (p.scalars, 2 * part_rows)
    choose = (iota(shape, 0) == (iota(shape, 1) % part_rows) // 8).astype(jnp.float32)
    choose = choose.astype(jnp.bfloat16)

    def fetch(store, chunk, part):
        step = LANES // p.cols
        for slot in range(part * step, (part + 1) * step):
            address = idx_ref[chunk, slot]
            at = (slot // 8) * (8 * p.cols) + slot % 8
            if p.cols == 1:
                store[pl.ds(at, 1), :] = table_ref[pl.ds(address, 1), :]
            else:
                store[pl.ds(at, p.cols, stride=8), :] = table_ref[
                    pl.ds(address, p.cols, stride=8), :
                ]

    def reduce(store, chunk, ahead):
        weights = spline_rows([field_ref[pl.ds(f * p.chunks + chunk, 1), :] for f in range(4)])
        parts = []
        for c in range(p.cols):
            tiles = [store[(b * p.cols + c) * 8 : (b * p.cols + c + 1) * 8, :] for b in range(16)]
            turned = jnp.concatenate(tiles, axis=0).T
            for m in range(4):
                product = turned[m * K : (m + 1) * K] * weights
                parts.append((product[0:8] + product[8:16]) + (product[16:24] + product[24:32]))
            ahead(c)
        parts = jnp.concatenate(pieces_of(jnp.concatenate(parts, axis=0), 2), axis=0)
        tile = jnp.dot(choose, parts, preferred_element_type=jnp.float32)
        tile_ref[pl.ds(pl.multiple_of(chunk * p.scalars, p.scalars), p.scalars), :] = tile

    for load in loads:
        load.wait()
    for n in range(BATCH):
        for c in range(p.cols):
            fetch(stores[n], n, c)

    def two_batches(i, carry):
        for half in range(2):
            now = (2 * i + half) * BATCH
            later = jnp.minimum(now + BATCH, p.chunks - BATCH)
            for n in range(BATCH):
                ahead = functools.partial(fetch, stores[(1 - half) * BATCH + n], later + n)
                reduce(stores[half * BATCH + n], now + n, ahead)
        return carry

    lax.fori_loop(0, p.chunks // (2 * BATCH), two_batches, 0)

    for g in range(p.table):
        for s in range(p.scal):
            dest, chunk = g * p.scal + s, s * p.table + g
            out_ref[dest * p.rows : dest * p.rows + p.scalars, :] = tile_ref[
                chunk * p.scalars : (chunk + 1) * p.scalars, :
            ]
    quad_of = (iota((1, LANES), 1) // p.far) % 4
    for quad in range(quads):
        for s in range(p.scal):
            first = (p.devices + s * quads + quad) * p.scalars
            tile = tile_ref[first : first + p.scalars, :]
            turned = [pltpu.roll(tile, (d * p.far) % LANES, 1) if d else tile for d in range(4)]
            wrapped = [
                pltpu.roll(tile, (-d * p.far) % LANES, 1) if d else tile for d in range(4)
            ]
            for i in range(4):
                message = jnp.zeros((p.few, LANES), jnp.float32)
                for b in range(4):
                    moved = turned[b - i] if b >= i else wrapped[i - b]
                    message = jnp.where(
                        quad_of == b, moved[b * p.few : (b + 1) * p.few], message
                    )
                start = ((quad * 4 + i) * p.scal + s) * p.rows + p.scalars
                out_ref[start : start + p.few, :] = message


def lookup_scratch(plan, table_shape):
    p = plan
    return [
        pltpu.VMEM(table_shape, jnp.float32),
        pltpu.VMEM((p.chunks, LANES), jnp.int32),
        pltpu.SMEM((p.chunks, LANES), jnp.int32),
        pltpu.VMEM((4 * p.chunks, LANES), jnp.float32),
        pltpu.VMEM((p.chunks * p.scalars, LANES), jnp.float32),
        pltpu.SemaphoreType.DMA((1 + PARTS,)),
    ] + [pltpu.VMEM((p.cols * LANES, LANES), jnp.float32) for _ in range(2 * BATCH)]


def slots_kernel(plan, me_ref, recv_ref, out_ref):
    p = plan
    table_at, scal_at = me_ref[0], me_ref[1]
    half_x = p.nx // 2
    width = LG * half_x
    codes = recv_ref[pl.ds(scal_at * 8 + 7, p.table, stride=8 * p.scal), :].astype(jnp.bfloat16)
    step = 2 * LANES
    for h in range(2):
        x = iota((1, width), 1) % half_x + h * half_x
        inside = (iota((1, width), 1) // half_x) * BX + x % BX + GROUP * (table_at % 2)
        move = (iota((LANES, width), 0) == inside).astype(jnp.float32).astype(jnp.bfloat16)
        moved = jnp.dot(codes, move, preferred_element_type=jnp.float32)
        t = x // BX
        moved = jnp.where(iota((p.table, width), 0) == t, moved, 0.0)
        code = jnp.sum(moved, axis=0, keepdims=True).astype(jnp.int32)
        shard, slot = code // p.code, code % p.code
        t = t - h * (p.table // 2)
        near = (shard // 2) * LANES + (shard % 2) * GROUP + t * p.near + slot
        quad = shard // 4
        far = (p.table // 2 + quad // 2) * LANES + (quad % 2) * GROUP
        far = far + t * p.quad + (shard % 4) * p.far + slot - p.near
        chosen = jnp.where(slot < p.near, near, far)
        rows = iota((step, width), 0)

        def fill(i, carry):
            start = pl.multiple_of(i * step, step)
            hit = rows == chosen - start
            out_ref[h, pl.ds(start, step), :] = jnp.where(hit, 1.0, 0.0).astype(jnp.bfloat16)
            return carry

        lax.fori_loop(0, out_ref.shape[1] // step, fill, 0)


def filter_kernel(plan, recv_ref, place_ref, op_ref, filtered_ref, gradient_ref, *left_refs):
    p = plan
    lane = iota((1, LANES), 1)
    low = lane < GROUP
    quad_of = (lane // p.far) % 4

    def halves(first, second, rows, col):
        turned = [pltpu.roll(tile, GROUP, 1) for tile in (first, second)]
        left_refs[0][rows, col : col + LANES] = jnp.where(low, first, turned[1])
        left_refs[1][rows, col : col + LANES] = jnp.where(low, turned[0], second)

    for o in range(0, p.table, 2):
        for sc in range(p.scal):
            tiles = []
            for i in range(2):
                start = ((o + i) * p.scal + sc) * p.rows
                tiles.append(recv_ref[start : start + p.scalars, :])
            halves(*tiles, slice(sc * p.scalars, (sc + 1) * p.scalars), o // 2 * LANES)
    for quad in range(0, p.table // 4, 2):
        for sc in range(p.scal):
            for b in range(4):
                parts = []
                for n in range(2):
                    part = jnp.zeros((p.few, LANES), jnp.float32)
                    for i in range(4):
                        start = (((quad + n) * 4 + i) * p.scal + sc) * p.rows + p.scalars
                        turned = recv_ref[start : start + p.few, :]
                        turned = pltpu.roll(turned, ((i - b) * p.far) % LANES, 1)
                        part = jnp.where(quad_of == i, turned, part)
                    parts.append(part)
                row = sc * p.scalars + b * p.few
                halves(*parts, slice(row, row + p.few), (p.table + quad) // 2 * LANES)
    sides = []
    for h in range(2):
        left = jnp.concatenate(pieces_of(left_refs[h][...], 3), axis=0)
        values = jnp.dot(left, place_ref[h], preferred_element_type=jnp.float32)
        sides.append(
            values[0:SCAL_ALL] + values[SCAL_ALL : 2 * SCAL_ALL] + values[2 * SCAL_ALL :]
        )
    half_x = p.nx // 2
    lines = jnp.concatenate(
        [
            jnp.concatenate([side[:, r * half_x : (r + 1) * half_x] for side in sides], axis=1)
            for r in range(LG)
        ],
        axis=0,
    )
    both = jnp.dot(
        lines, op_ref[...], precision=lax.Precision.HIGHEST, preferred_element_type=jnp.float32
    )
    for r in range(LG):
        rows = slice(r * SCAL_ALL, (r + 1) * SCAL_ALL)
        filtered_ref[:, r, :] = both[rows, : p.nx]
        gradient_ref[:, r, :] = both[rows, p.nx :]


VMEM = pl.BlockSpec(memory_space=pltpu.VMEM)
SMEM = pl.BlockSpec(memory_space=pltpu.SMEM)
HBM = pl.BlockSpec(memory_space=pltpu.HBM)


def call(kernel, plan, out_shape, in_specs, scratch, limit, cost, name):
    many = isinstance(out_shape, tuple)
    return pl.pallas_call(
        functools.partial(kernel, plan),
        out_shape=out_shape,
        in_specs=in_specs,
        out_specs=(VMEM,) * len(out_shape) if many else VMEM,
        scratch_shapes=scratch,
        compiler_params=pltpu.CompilerParams(vmem_limit_bytes=limit << 20),
        cost_estimate=pl.CostEstimate(flops=cost, bytes_accessed=cost // 256, transcendentals=0),
        name=name,
    )


def exchange(array):
    return lax.all_to_all(array, AXES, split_axis=0, concat_axis=0, tiled=True)


def on_device(plan, cell_coords, flamelet_table, owner_shard, local_bin):
    p = plan
    f32, i32 = jnp.float32, jnp.int32
    row_count = p.cells // LANES
    owners = owner_shard.reshape(row_count, LANES)
    bins = local_bin.reshape(row_count, LANES)
    requests = call(
        request_kernel,
        p,
        jax.ShapeDtypeStruct((p.devices, 8, LANES), f32),
        [HBM] * 3,
        [
            pltpu.VMEM((8, p.cells), f32),
            pltpu.VMEM(cell_coords.shape, f32),
            pltpu.VMEM(owners.shape, i32),
            pltpu.VMEM(bins.shape, i32),
            pltpu.SemaphoreType.DMA((3,)),
        ],
        60,
        1 << 20,
        "requests",
    )(cell_coords, owners, bins)
    received = exchange(requests).reshape(p.devices * 8, LANES)

    bin_count, depth = flamelet_table.shape
    table = flamelet_table.reshape(bin_count // 8, 8, p.cols, LANES).transpose(0, 2, 1, 3)
    table = table.reshape(bin_count * p.cols, LANES)
    replies = call(
        lookup_kernel,
        p,
        jax.ShapeDtypeStruct((p.devices * p.rows, LANES), f32),
        [VMEM, HBM],
        lookup_scratch(p, table.shape),
        50,
        1 << 24,
        "lookup",
    )(received, table)
    answers = exchange(replies.reshape(p.devices, 1, p.rows * LANES))
    answers = answers.reshape(p.devices * p.rows, LANES)

    me = jnp.stack([lax.axis_index("table"), lax.axis_index("scal")]).astype(i32)
    place = call(
        slots_kernel,
        p,
        jax.ShapeDtypeStruct((2, p.table * 5 * LANES // 8, LG * p.nx // 2), jnp.bfloat16),
        [SMEM, VMEM],
        [],
        8 + p.nx * p.table // 128,
        1 << 24,
        "slots",
    )(me, received)
    filter_op = filter_table(p.nx).T
    both_op = np.concatenate([filter_op, filter_op @ derivative_table(p.nx).T], axis=1)
    out = jax.ShapeDtypeStruct((SCAL_ALL, LG, p.nx), f32)
    return call(
        filter_kernel,
        p,
        (out, out),
        [VMEM] * 3,
        [pltpu.VMEM((SCAL_ALL, p.table * 5 * LANES // 8), f32)] * 2,
        8 + p.nx * p.table // 64,
        1 << 24,
        "filter",
    )(answers, place, jnp.asarray(both_op.astype(np.float32)))


def solution(mesh):
    table, scal = mesh.shape["table"], mesh.shape["scal"]

    def step(cell_coords, flamelet_table, owner_shard, local_bin):
        plan = Plan(table, scal, cell_coords.shape[1])
        return on_device(plan, cell_coords, flamelet_table, owner_shard, local_bin)

    return jax.shard_map(
        step,
        mesh=mesh,
        in_specs=(
            P(None, AXES),
            P("table", "scal"),
            P(AXES, None),
            P(AXES),
        ),
        out_specs=(P(None, AXES, None), P(None, AXES, None)),
        check_vma=False,
    )
```

```python
import functools

import jax
import jax.numpy as jnp
import numpy as np
from jax import lax
from jax.experimental import pallas as pl
from jax.experimental.pallas import tpu as pltpu
from jax.sharding import PartitionSpec as P

SCAL_ALL = 32
K = 32
BX = 8
LG = 8
GROUP = BX * LG
LANES = 128
AXES = ("table", "scal")
BATCH = 4

strength = 0.499


def thomas_solve(below, middle, above, right_side):
    length = middle.shape[0]
    upper_factor = np.zeros(length)
    solved = np.zeros(right_side.shape)
    for row in range(length):
        if row == 0:
            denom = middle[0]
            solved[0] = right_side[0] / denom
        else:
            denom = middle[row] - below[row] * upper_factor[row - 1]
            solved[row] = (right_side[row] - below[row] * solved[row - 1]) / denom
        upper_factor[row] = above[row] / denom
    for row in range(length - 2, -1, -1):
        solved[row] = solved[row] - upper_factor[row] * solved[row + 1]
    return solved


def filter_table(length):
    positions = np.arange(length)
    offset = positions[None, :] - positions[:, None]
    distance = np.abs(offset)
    interior = (positions >= 3) & (positions <= length - 4)
    coeffs = [
        (11.0 + 10.0 * strength) / 16.0,
        (15.0 + 34.0 * strength) / 64.0,
        (-3.0 + 6.0 * strength) / 32.0,
        (1.0 - 2.0 * strength) / 64.0,
    ]
    band = np.zeros((length, length))
    for reach in range(4):
        band = band + np.where(distance == reach, coeffs[reach], 0.0)
    right_side = np.where(interior[:, None], band, np.where(offset == 0, 1.0, 0.0))
    coupling = np.where(interior, strength, 0.0)
    return thomas_solve(coupling, np.ones(length), coupling, right_side)


def derivative_table(length):
    positions = np.arange(length)
    offset = positions[None, :] - positions[:, None]
    distance = np.abs(offset)
    direction = np.sign(offset) * 1.0
    boundary = (positions == 0) | (positions == length - 1)
    second = (positions == 1) | (positions == length - 2)
    interior = ~(boundary | second)
    below_diag = np.where(
        interior, 1.0 / 3.0, np.where(second, 0.25, np.where(positions == length - 1, 2.0, 0.0))
    )
    above_diag = np.where(
        interior, 1.0 / 3.0, np.where(second, 0.25, np.where(positions == 0, 2.0, 0.0))
    )
    inner_rows = direction * (
        np.where(distance == 1, 7.0 / 9.0, 0.0) + np.where(distance == 2, 1.0 / 36.0, 0.0)
    )
    second_rows = direction * np.where(distance == 1, 0.75, 0.0)
    first_row = np.where(
        offset == 0, -2.5, np.where(offset == 1, 2.0, np.where(offset == 2, 0.5, 0.0))
    )
    final_row = np.where(
        offset == 0, 2.5, np.where(offset == -1, -2.0, np.where(offset == -2, -0.5, 0.0))
    )
    right_side = np.where(
        interior[:, None],
        inner_rows,
        np.where(
            second[:, None], second_rows, np.where((positions == 0)[:, None], first_row, final_row)
        ),
    )
    return thomas_solve(below_diag, np.ones(length), above_diag, right_side)


class Plan:
    def __init__(self, table, scal, cells):
        self.table, self.scal, self.cells = table, scal, cells
        self.devices = table * scal
        self.cap = max(2, 5 * GROUP // (2 * table))
        self.near = LANES // table
        self.far = self.cap - self.near
        self.quad = 4 * self.far
        assert cells == table * GROUP and table * self.quad == LANES
        self.code = 1 << (self.cap - 1).bit_length()
        self.scalars = SCAL_ALL // scal
        self.cols = self.scalars * K // LANES
        self.few = self.scalars // 4
        self.rows = self.scalars + self.few
        self.nx = BX * table
        self.chunks = self.devices + self.devices // 4


def iota(shape, dim):
    return lax.broadcasted_iota(jnp.int32, shape, dim)


def pieces_of(values, count):
    pieces = []
    for _ in range(count - 1):
        piece = values.astype(jnp.bfloat16)
        pieces.append(piece)
        values = values - piece.astype(jnp.float32)
    pieces.append(values.astype(jnp.bfloat16))
    return pieces


def dot_rows(a, b):
    return lax.dot_general(a, b, (((1,), (1,)), ((), ())), preferred_element_type=jnp.float32)


def request_kernel(plan, coords_in, owner_in, bin_in, out_ref, x_ref, coords_ref, owner_ref, bin_ref, sem):
    p = plan
    row_count = p.cells // LANES
    copies = [
        pltpu.make_async_copy(owner_in, owner_ref, sem.at[0]),
        pltpu.make_async_copy(bin_in, bin_ref, sem.at[1]),
        pltpu.make_async_copy(coords_in, coords_ref, sem.at[2]),
    ]
    for copy in copies:
        copy.start()
    for copy in copies:
        copy.wait()
    half = iota((1, LANES), 1) // GROUP
    shard_ids = iota((p.table, LANES), 0)
    owners = owner_ref[...]
    bins = bin_ref[...]
    address = ((bins >> 3) * (8 * p.cols) + (bins & 7)).astype(jnp.float32)
    hits = [owners[i : i + 1, :] == shard_ids for i in range(row_count)]
    before = iota((LANES, LANES), 0)
    after = iota((LANES, LANES), 1)
    earlier = ((before < after) & (before // GROUP == after // GROUP)).astype(jnp.bfloat16)
    ones = jnp.concatenate([h.astype(jnp.float32) for h in hits], axis=0)
    counts = jnp.dot(ones.astype(jnp.bfloat16), earlier, preferred_element_type=jnp.float32)
    x_ref[0:4, :] = coords_ref[...]
    x_ref[5:8, :] = jnp.zeros((3, p.cells), jnp.float32)
    for i in range(row_count):
        x_ref[4:5, i * LANES : (i + 1) * LANES] = address[i : i + 1, :]
    lane_rows = iota((LANES, LANES), 0)
    left, right, codes = [], [], []
    for i in range(row_count):
        span = slice(i * p.table, (i + 1) * p.table)
        rank = jnp.sum(ones[span] * counts[span], axis=0, keepdims=True).astype(jnp.int32)
        codes.append((owners[i : i + 1, :] * p.code + rank).astype(jnp.float32))
        group = 2 * i + half
        near = jnp.where(rank < p.near, group * p.near + rank, -1)
        far = jnp.where(rank >= p.near, group * p.far + rank - p.near, -1)
        right.append(
            jnp.concatenate(
                [
                    (lane_rows == near).astype(jnp.float32),
                    (lane_rows % 32 == far).astype(jnp.float32),
                ],
                axis=0,
            ).astype(jnp.bfloat16)
        )
        fields = x_ref[:, i * LANES : (i + 1) * LANES]
        chosen = jnp.where(hits[i][:, None, :], fields[None], 0.0).reshape(p.table * 8, LANES)
        left.append(jnp.concatenate(pieces_of(chosen, 3), axis=0))
    placed = dot_rows(jnp.concatenate(left, axis=1), jnp.concatenate(right, axis=1))
    total = p.table * 8
    placed = placed[0:total] + placed[total : 2 * total] + placed[2 * total :]
    sub = iota((8, LANES), 0)
    block = iota((8, LANES), 1) // 32
    for o in range(p.table):
        near_part = placed[o * 8 : (o + 1) * 8, :LANES]
        far_part = placed[o * 8 : (o + 1) * 8, LANES:]
        far_coords = jnp.sum(jnp.where(sub == block, far_part, 0.0), axis=0, keepdims=True)
        message = jnp.where(
            sub < 5,
            near_part,
            jnp.where(sub == 5, far_coords, jnp.where(sub == 6, far_part[4:5], codes[o // 2])),
        )
        for sc in range(p.scal):
            out_ref[o * p.scal + sc] = message


def spline_rows(f):
    shape = (K, f[0].shape[1])
    k = iota(shape, 0)
    product = None
    for axis, bit in ((0, 16), (1, 8), (2, 4)):
        factor = jnp.where((k & bit) != 0, f[axis], 1.0 - f[axis])
        product = factor if product is None else product * factor
    last = f[3]
    square = last * last
    cube = square * last
    remain = 1.0 - last
    basis = [
        remain * remain * remain / 6.0,
        (3.0 * cube - 6.0 * square + 4.0) / 6.0,
        (-3.0 * cube + 3.0 * square + 3.0 * last + 1.0) / 6.0,
        cube / 6.0,
    ]
    d = k & 3
    cubic = jnp.where(d == 0, basis[0], jnp.where(d == 1, basis[1], jnp.where(d == 2, basis[2], basis[3])))
    return product * cubic


def swap_blocks(x, count, width):
    row, block = iota(x.shape, 0), iota(x.shape, 1) // width
    bit = 1
    while bit < count:
        up = pltpu.roll(pltpu.roll(x, x.shape[0] - bit, 0), bit * width, 1)
        down = pltpu.roll(pltpu.roll(x, bit, 0), LANES - bit * width, 1)
        low_row, low_block = (row & bit) == 0, (block & bit) == 0
        x = jnp.where(low_row == low_block, x, jnp.where(low_row, up, down))
        bit *= 2
    return x


def lookup_kernel(
    plan,
    recv_ref,
    early_ref,
    table_in,
    out_ref,
    table_ref,
    ints_ref,
    idx_ref,
    field_ref,
    tile_ref,
    sem,
    *stores,
):
    p = plan
    quads = p.table // 4
    early = early_ref.shape[0]
    late = table_ref.shape[0] - early
    loads = [
        pltpu.make_async_copy(
            table_in.at[pl.ds(early, late // 2)], table_ref.at[pl.ds(early, late // 2)], sem.at[1]
        ),
        pltpu.make_async_copy(
            table_in.at[pl.ds(early + late // 2, late // 2)],
            table_ref.at[pl.ds(early + late // 2, late // 2)],
            sem.at[2],
        ),
        pltpu.make_async_copy(early_ref, table_ref.at[pl.ds(0, early)], sem.at[3]),
    ]
    loads[0].start()

    def received(r):
        rows = [recv_ref[pl.ds(s * 8 + r, p.table, stride=8 * p.scal), :] for s in range(p.scal)]
        return jnp.concatenate(rows, axis=0)

    addresses = jnp.concatenate([received(4), received(6)], axis=0)
    addresses = swap_blocks(addresses, p.table, p.near).astype(jnp.int32)
    ints_ref[0 : p.devices, :] = addresses[: p.devices]
    for s in range(p.scal):
        first = p.devices + s * p.table
        to = p.devices + s * quads
        ints_ref[to : to + quads, :] = addresses[first : first + quads]
    copy = pltpu.make_async_copy(ints_ref, idx_ref, sem.at[0])
    copy.start()
    for load in loads[1:]:
        load.start()
    fields = jnp.concatenate([received(f) for f in (0, 1, 2, 3, 5)], axis=0)
    fields = swap_blocks(fields, p.table, p.near)
    for f in range(4):
        field_ref[f * p.chunks : f * p.chunks + p.devices, :] = fields[
            f * p.devices : (f + 1) * p.devices
        ]
        for s in range(p.scal):
            first = 4 * p.devices + s * p.table + f * quads
            to = f * p.chunks + p.devices + s * quads
            field_ref[to : to + quads, :] = fields[first : first + quads]
    copy.wait()

    def fetch(store, chunk, part):
        step = LANES // p.cols
        for slot in range(part * step, (part + 1) * step):
            address = idx_ref[chunk, slot]
            if p.cols == 1:
                store[slot : slot + 1, :] = table_ref[pl.ds(address, 1), :]
            else:
                store[slot * p.cols : (slot + 1) * p.cols, :] = table_ref[
                    pl.ds(address, p.cols, stride=8), :
                ]

    def reduce(store, chunk, ahead):
        weights = spline_rows([field_ref[pl.ds(f * p.chunks + chunk, 1), :] for f in range(4)])
        parts = []
        for c in range(p.cols):
            rows = pl.ds(c, LANES, stride=p.cols) if p.cols > 1 else pl.ds(0, LANES)
            turned = store[rows, :].T
            for m in range(4):
                product = turned[m * K : (m + 1) * K] * weights
                parts.append((product[0:8] + product[8:16]) + (product[16:24] + product[24:32]))
            ahead(c)
        tile = jnp.sum(jnp.concatenate(parts, axis=0).reshape(p.scalars, 8, LANES), axis=1)
        tile_ref[pl.ds(pl.multiple_of(chunk * p.scalars, p.scalars), p.scalars), :] = tile

    for load in loads:
        load.wait()
    for n in range(BATCH):
        for c in range(p.cols):
            fetch(stores[n], n, c)

    def two_batches(i, carry):
        for half in range(2):
            now = (2 * i + half) * BATCH
            later = jnp.minimum(now + BATCH, p.chunks - BATCH)
            for n in range(BATCH):
                ahead = functools.partial(fetch, stores[(1 - half) * BATCH + n], later + n)
                reduce(stores[half * BATCH + n], now + n, ahead)
        return carry

    lax.fori_loop(0, p.chunks // (2 * BATCH), two_batches, 0)

    for g in range(p.table):
        for s in range(p.scal):
            dest, chunk = g * p.scal + s, s * p.table + g
            out_ref[dest * p.rows : dest * p.rows + p.scalars, :] = tile_ref[
                chunk * p.scalars : (chunk + 1) * p.scalars, :
            ]
    quad_of = (iota((1, LANES), 1) // p.far) % 4
    for quad in range(quads):
        for s in range(p.scal):
            first = (p.devices + s * quads + quad) * p.scalars
            tile = tile_ref[first : first + p.scalars, :]
            turned = [pltpu.roll(tile, (d * p.far) % LANES, 1) if d else tile for d in range(4)]
            wrapped = [
                pltpu.roll(tile, (-d * p.far) % LANES, 1) if d else tile for d in range(4)
            ]
            for i in range(4):
                message = jnp.zeros((p.few, LANES), jnp.float32)
                for b in range(4):
                    moved = turned[b - i] if b >= i else wrapped[i - b]
                    message = jnp.where(
                        quad_of == b, moved[b * p.few : (b + 1) * p.few], message
                    )
                start = ((quad * 4 + i) * p.scal + s) * p.rows + p.scalars
                out_ref[start : start + p.few, :] = message


def lookup_scratch(plan, table_shape):
    p = plan
    return [
        pltpu.VMEM(table_shape, jnp.float32),
        pltpu.VMEM((p.chunks, LANES), jnp.int32),
        pltpu.SMEM((p.chunks, LANES), jnp.int32),
        pltpu.VMEM((4 * p.chunks, LANES), jnp.float32),
        pltpu.VMEM((p.chunks * p.scalars, LANES), jnp.float32),
        pltpu.SemaphoreType.DMA((4,)),
    ] + [pltpu.VMEM((p.cols * LANES, LANES), jnp.float32) for _ in range(2 * BATCH)]


def slots_kernel(plan, me_ref, recv_ref, out_ref):
    p = plan
    table_at, scal_at = me_ref[0], me_ref[1]
    half_x = p.nx // 2
    width = LG * half_x
    codes = recv_ref[pl.ds(scal_at * 8 + 7, p.table, stride=8 * p.scal), :].astype(jnp.bfloat16)
    step = 2 * LANES
    for h in range(2):
        x = iota((1, width), 1) % half_x + h * half_x
        inside = (iota((1, width), 1) // half_x) * BX + x % BX + GROUP * (table_at % 2)
        move = (iota((LANES, width), 0) == inside).astype(jnp.float32).astype(jnp.bfloat16)
        moved = jnp.dot(codes, move, preferred_element_type=jnp.float32)
        t = x // BX
        moved = jnp.where(iota((p.table, width), 0) == t, moved, 0.0)
        code = jnp.sum(moved, axis=0, keepdims=True).astype(jnp.int32)
        shard, slot = code // p.code, code % p.code
        t = t - h * (p.table // 2)
        near = (shard // 2) * LANES + (shard % 2) * GROUP + t * p.near + slot
        quad = shard // 4
        far = (p.table // 2 + quad // 2) * LANES + (quad % 2) * GROUP
        far = far + t * p.quad + (shard % 4) * p.far + slot - p.near
        chosen = jnp.where(slot < p.near, near, far)
        rows = iota((step, width), 0)

        def fill(i, carry):
            start = pl.multiple_of(i * step, step)
            hit = rows == chosen - start
            out_ref[h, pl.ds(start, step), :] = jnp.where(hit, 1.0, 0.0).astype(jnp.bfloat16)
            return carry

        lax.fori_loop(0, out_ref.shape[1] // step, fill, 0)


def filter_kernel(plan, recv_ref, place_ref, op_ref, filtered_ref, gradient_ref, *left_refs):
    p = plan
    lane = iota((1, LANES), 1)
    low = lane < GROUP
    quad_of = (lane // p.far) % 4

    def halves(first, second, rows, col):
        turned = [pltpu.roll(tile, GROUP, 1) for tile in (first, second)]
        left_refs[0][rows, col : col + LANES] = jnp.where(low, first, turned[1])
        left_refs[1][rows, col : col + LANES] = jnp.where(low, turned[0], second)

    for o in range(0, p.table, 2):
        for sc in range(p.scal):
            tiles = []
            for i in range(2):
                start = ((o + i) * p.scal + sc) * p.rows
                tiles.append(recv_ref[start : start + p.scalars, :])
            halves(*tiles, slice(sc * p.scalars, (sc + 1) * p.scalars), o // 2 * LANES)
    for quad in range(0, p.table // 4, 2):
        for sc in range(p.scal):
            for b in range(4):
                parts = []
                for n in range(2):
                    part = jnp.zeros((p.few, LANES), jnp.float32)
                    for i in range(4):
                        start = (((quad + n) * 4 + i) * p.scal + sc) * p.rows + p.scalars
                        turned = recv_ref[start : start + p.few, :]
                        turned = pltpu.roll(turned, ((i - b) * p.far) % LANES, 1)
                        part = jnp.where(quad_of == i, turned, part)
                    parts.append(part)
                row = sc * p.scalars + b * p.few
                halves(*parts, slice(row, row + p.few), (p.table + quad) // 2 * LANES)
    sides = []
    for h in range(2):
        left = jnp.concatenate(pieces_of(left_refs[h][...], 3), axis=0)
        values = jnp.dot(left, place_ref[h], preferred_element_type=jnp.float32)
        sides.append(
            values[0:SCAL_ALL] + values[SCAL_ALL : 2 * SCAL_ALL] + values[2 * SCAL_ALL :]
        )
    half_x = p.nx // 2
    lines = jnp.concatenate(
        [
            jnp.concatenate([side[:, r * half_x : (r + 1) * half_x] for side in sides], axis=1)
            for r in range(LG)
        ],
        axis=0,
    )
    both = jnp.dot(
        lines, op_ref[...], precision=lax.Precision.HIGHEST, preferred_element_type=jnp.float32
    )
    for r in range(LG):
        rows = slice(r * SCAL_ALL, (r + 1) * SCAL_ALL)
        filtered_ref[:, r, :] = both[rows, : p.nx]
        gradient_ref[:, r, :] = both[rows, p.nx :]


VMEM = pl.BlockSpec(memory_space=pltpu.VMEM)
SMEM = pl.BlockSpec(memory_space=pltpu.SMEM)
HBM = pl.BlockSpec(memory_space=pltpu.HBM)


def call(kernel, plan, out_shape, in_specs, scratch, limit, cost, name):
    many = isinstance(out_shape, tuple)
    return pl.pallas_call(
        functools.partial(kernel, plan),
        out_shape=out_shape,
        in_specs=in_specs,
        out_specs=(VMEM,) * len(out_shape) if many else VMEM,
        scratch_shapes=scratch,
        compiler_params=pltpu.CompilerParams(vmem_limit_bytes=limit << 20),
        cost_estimate=pl.CostEstimate(flops=cost, bytes_accessed=cost // 256, transcendentals=0),
        name=name,
    )


def exchange(array):
    return lax.all_to_all(array, AXES, split_axis=0, concat_axis=0, tiled=True)


def on_device(plan, cell_coords, flamelet_table, owner_shard, local_bin):
    p = plan
    f32, i32 = jnp.float32, jnp.int32
    row_count = p.cells // LANES
    owners = owner_shard.reshape(row_count, LANES)
    bins = local_bin.reshape(row_count, LANES)
    requests = call(
        request_kernel,
        p,
        jax.ShapeDtypeStruct((p.devices, 8, LANES), f32),
        [HBM] * 3,
        [
            pltpu.VMEM((8, p.cells), f32),
            pltpu.VMEM(cell_coords.shape, f32),
            pltpu.VMEM(owners.shape, i32),
            pltpu.VMEM(bins.shape, i32),
            pltpu.SemaphoreType.DMA((3,)),
        ],
        60,
        1 << 20,
        "requests",
    )(cell_coords, owners, bins)
    received = exchange(requests).reshape(p.devices * 8, LANES)

    bin_count, depth = flamelet_table.shape
    table = flamelet_table.reshape(bin_count // 8, 8, p.cols, LANES).transpose(0, 2, 1, 3)
    table = table.reshape(bin_count * p.cols, LANES)
    early = table[: bin_count * p.cols * 11 // 32]
    replies = call(
        lookup_kernel,
        p,
        jax.ShapeDtypeStruct((p.devices * p.rows, LANES), f32),
        [VMEM, VMEM, HBM],
        lookup_scratch(p, table.shape),
        50,
        1 << 24,
        "lookup",
    )(received, early, table)
    answers = exchange(replies.reshape(p.devices, 1, p.rows * LANES))
    answers = answers.reshape(p.devices * p.rows, LANES)

    me = jnp.stack([lax.axis_index("table"), lax.axis_index("scal")]).astype(i32)
    place = call(
        slots_kernel,
        p,
        jax.ShapeDtypeStruct((2, p.table * 5 * LANES // 8, LG * p.nx // 2), jnp.bfloat16),
        [SMEM, VMEM],
        [],
        8 + p.nx * p.table // 128,
        1 << 24,
        "slots",
    )(me, received)
    filter_op = filter_table(p.nx).T
    both_op = np.concatenate([filter_op, filter_op @ derivative_table(p.nx).T], axis=1)
    out = jax.ShapeDtypeStruct((SCAL_ALL, LG, p.nx), f32)
    return call(
        filter_kernel,
        p,
        (out, out),
        [VMEM] * 3,
        [pltpu.VMEM((SCAL_ALL, p.table * 5 * LANES // 8), f32)] * 2,
        8 + p.nx * p.table // 64,
        1 << 24,
        "filter",
    )(answers, place, jnp.asarray(both_op.astype(np.float32)))


def solution(mesh):
    table, scal = mesh.shape["table"], mesh.shape["scal"]

    def step(cell_coords, flamelet_table, owner_shard, local_bin):
        plan = Plan(table, scal, cell_coords.shape[1])
        return on_device(plan, cell_coords, flamelet_table, owner_shard, local_bin)

    return jax.shard_map(
        step,
        mesh=mesh,
        in_specs=(
            P(None, AXES),
            P("table", "scal"),
            P(AXES, None),
            P(AXES),
        ),
        out_specs=(P(None, AXES, None), P(None, AXES, None)),
        check_vma=False,
    )
```

```python
import functools

import jax
import jax.numpy as jnp
import numpy as np
from jax import lax
from jax.experimental import pallas as pl
from jax.experimental.pallas import tpu as pltpu
from jax.sharding import PartitionSpec as P

SCAL_ALL = 32
K = 32
BX = 8
LG = 8
GROUP = BX * LG
LANES = 128
AXES = ("table", "scal")
BATCH = 4

strength = 0.499


def thomas_solve(below, middle, above, right_side):
    length = middle.shape[0]
    upper_factor = np.zeros(length)
    solved = np.zeros(right_side.shape)
    for row in range(length):
        if row == 0:
            denom = middle[0]
            solved[0] = right_side[0] / denom
        else:
            denom = middle[row] - below[row] * upper_factor[row - 1]
            solved[row] = (right_side[row] - below[row] * solved[row - 1]) / denom
        upper_factor[row] = above[row] / denom
    for row in range(length - 2, -1, -1):
        solved[row] = solved[row] - upper_factor[row] * solved[row + 1]
    return solved


def filter_table(length):
    positions = np.arange(length)
    offset = positions[None, :] - positions[:, None]
    distance = np.abs(offset)
    interior = (positions >= 3) & (positions <= length - 4)
    coeffs = [
        (11.0 + 10.0 * strength) / 16.0,
        (15.0 + 34.0 * strength) / 64.0,
        (-3.0 + 6.0 * strength) / 32.0,
        (1.0 - 2.0 * strength) / 64.0,
    ]
    band = np.zeros((length, length))
    for reach in range(4):
        band = band + np.where(distance == reach, coeffs[reach], 0.0)
    right_side = np.where(interior[:, None], band, np.where(offset == 0, 1.0, 0.0))
    coupling = np.where(interior, strength, 0.0)
    return thomas_solve(coupling, np.ones(length), coupling, right_side)


def derivative_table(length):
    positions = np.arange(length)
    offset = positions[None, :] - positions[:, None]
    distance = np.abs(offset)
    direction = np.sign(offset) * 1.0
    boundary = (positions == 0) | (positions == length - 1)
    second = (positions == 1) | (positions == length - 2)
    interior = ~(boundary | second)
    below_diag = np.where(
        interior, 1.0 / 3.0, np.where(second, 0.25, np.where(positions == length - 1, 2.0, 0.0))
    )
    above_diag = np.where(
        interior, 1.0 / 3.0, np.where(second, 0.25, np.where(positions == 0, 2.0, 0.0))
    )
    inner_rows = direction * (
        np.where(distance == 1, 7.0 / 9.0, 0.0) + np.where(distance == 2, 1.0 / 36.0, 0.0)
    )
    second_rows = direction * np.where(distance == 1, 0.75, 0.0)
    first_row = np.where(
        offset == 0, -2.5, np.where(offset == 1, 2.0, np.where(offset == 2, 0.5, 0.0))
    )
    final_row = np.where(
        offset == 0, 2.5, np.where(offset == -1, -2.0, np.where(offset == -2, -0.5, 0.0))
    )
    right_side = np.where(
        interior[:, None],
        inner_rows,
        np.where(
            second[:, None], second_rows, np.where((positions == 0)[:, None], first_row, final_row)
        ),
    )
    return thomas_solve(below_diag, np.ones(length), above_diag, right_side)


class Plan:
    def __init__(self, table, scal, cells):
        self.table, self.scal, self.cells = table, scal, cells
        self.devices = table * scal
        self.cap = max(2, 5 * GROUP // (2 * table))
        self.near = LANES // table
        self.far = self.cap - self.near
        self.quad = 4 * self.far
        assert cells == table * GROUP and table * self.quad == LANES
        self.code = 1 << (self.cap - 1).bit_length()
        self.scalars = SCAL_ALL // scal
        self.cols = self.scalars * K // LANES
        self.few = self.scalars // 4
        self.rows = self.scalars + self.few
        self.nx = BX * table
        self.chunks = self.devices + self.devices // 4
        self.padded = -(-self.chunks // LANES) * LANES


def iota(shape, dim):
    return lax.broadcasted_iota(jnp.int32, shape, dim)


def pieces_of(values, count):
    pieces = []
    for _ in range(count - 1):
        piece = values.astype(jnp.bfloat16)
        pieces.append(piece)
        values = values - piece.astype(jnp.float32)
    pieces.append(values.astype(jnp.bfloat16))
    return pieces


def dot_rows(a, b):
    return lax.dot_general(a, b, (((1,), (1,)), ((), ())), preferred_element_type=jnp.float32)


def request_kernel(plan, coords_in, owner_in, bin_in, out_ref, x_ref, coords_ref, owner_ref, bin_ref, sem):
    p = plan
    row_count = p.cells // LANES
    copies = [
        pltpu.make_async_copy(owner_in, owner_ref, sem.at[0]),
        pltpu.make_async_copy(bin_in, bin_ref, sem.at[1]),
        pltpu.make_async_copy(coords_in, coords_ref, sem.at[2]),
    ]
    for copy in copies:
        copy.start()
    for copy in copies:
        copy.wait()
    half = iota((1, LANES), 1) // GROUP
    shard_ids = iota((p.table, LANES), 0)
    owners = owner_ref[...]
    bins = bin_ref[...]
    address = ((bins >> 3) * (8 * p.cols) + (bins & 7)).astype(jnp.float32)
    hits = [owners[i : i + 1, :] == shard_ids for i in range(row_count)]
    before = iota((LANES, LANES), 0)
    after = iota((LANES, LANES), 1)
    earlier = ((before < after) & (before // GROUP == after // GROUP)).astype(jnp.bfloat16)
    ones = jnp.concatenate([h.astype(jnp.float32) for h in hits], axis=0)
    counts = jnp.dot(ones.astype(jnp.bfloat16), earlier, preferred_element_type=jnp.float32)
    x_ref[0:4, :] = coords_ref[...]
    x_ref[5:8, :] = jnp.zeros((3, p.cells), jnp.float32)
    for i in range(row_count):
        x_ref[4:5, i * LANES : (i + 1) * LANES] = address[i : i + 1, :]
    lane_rows = iota((LANES, LANES), 0)
    left, right, codes = [], [], []
    for i in range(row_count):
        span = slice(i * p.table, (i + 1) * p.table)
        rank = jnp.sum(ones[span] * counts[span], axis=0, keepdims=True).astype(jnp.int32)
        codes.append((owners[i : i + 1, :] * p.code + rank).astype(jnp.float32))
        group = 2 * i + half
        near = jnp.where(rank < p.near, group * p.near + rank, -1)
        far = jnp.where(rank >= p.near, group * p.far + rank - p.near, -1)
        right.append(
            jnp.concatenate(
                [
                    (lane_rows == near).astype(jnp.float32),
                    (lane_rows % 32 == far).astype(jnp.float32),
                ],
                axis=0,
            ).astype(jnp.bfloat16)
        )
        fields = x_ref[:, i * LANES : (i + 1) * LANES]
        chosen = []
        for piece in pieces_of(fields, 3):
            piece = jnp.where(hits[i][:, None, :], piece.astype(jnp.float32)[None], 0.0)
            chosen.append(piece.reshape(p.table * 8, LANES).astype(jnp.bfloat16))
        left.append(jnp.concatenate(chosen, axis=0))
    placed = dot_rows(jnp.concatenate(left, axis=1), jnp.concatenate(right, axis=1))
    total = p.table * 8
    placed = placed[0:total] + placed[total : 2 * total] + placed[2 * total :]
    sub = iota((8, LANES), 0)
    block = iota((8, LANES), 1) // 32
    for o in range(p.table):
        near_part = placed[o * 8 : (o + 1) * 8, :LANES]
        far_part = placed[o * 8 : (o + 1) * 8, LANES:]
        far_coords = jnp.sum(jnp.where(sub == block, far_part, 0.0), axis=0, keepdims=True)
        message = jnp.where(
            sub < 5,
            near_part,
            jnp.where(sub == 5, far_coords, jnp.where(sub == 6, far_part[4:5], codes[o // 2])),
        )
        for sc in range(p.scal):
            out_ref[o * p.scal + sc] = message


def spline_rows(f):
    shape = (K, f[0].shape[1])
    k = iota(shape, 0)
    product = None
    for axis, bit in ((0, 16), (1, 8), (2, 4)):
        factor = jnp.where((k & bit) != 0, f[axis], 1.0 - f[axis])
        product = factor if product is None else product * factor
    last = f[3]
    square = last * last
    cube = square * last
    remain = 1.0 - last
    basis = [
        remain * remain * remain / 6.0,
        (3.0 * cube - 6.0 * square + 4.0) / 6.0,
        (-3.0 * cube + 3.0 * square + 3.0 * last + 1.0) / 6.0,
        cube / 6.0,
    ]
    d = k & 3
    cubic = jnp.where(d == 0, basis[0], jnp.where(d == 1, basis[1], jnp.where(d == 2, basis[2], basis[3])))
    return product * cubic


def swap_blocks(x, count, width):
    row, block = iota(x.shape, 0), iota(x.shape, 1) // width
    bit = 1
    while bit < count:
        up = pltpu.roll(pltpu.roll(x, x.shape[0] - bit, 0), bit * width, 1)
        down = pltpu.roll(pltpu.roll(x, bit, 0), LANES - bit * width, 1)
        low_row, low_block = (row & bit) == 0, (block & bit) == 0
        x = jnp.where(low_row == low_block, x, jnp.where(low_row, up, down))
        bit *= 2
    return x


def lookup_kernel(
    plan,
    recv_ref,
    early_ref,
    table_in,
    out_ref,
    table_ref,
    ints_ref,
    field_ref,
    tile_ref,
    sem,
    *rest,
):
    p = plan
    idx_refs, stores = rest[:16], rest[16:]
    quads = p.table // 4
    early = early_ref.shape[0]
    late = table_ref.shape[0] - early
    loads = [
        pltpu.make_async_copy(
            table_in.at[pl.ds(early, late // 2)], table_ref.at[pl.ds(early, late // 2)], sem.at[1]
        ),
        pltpu.make_async_copy(
            table_in.at[pl.ds(early + late // 2, late // 2)],
            table_ref.at[pl.ds(early + late // 2, late // 2)],
            sem.at[2],
        ),
        pltpu.make_async_copy(early_ref, table_ref.at[pl.ds(0, early)], sem.at[3]),
    ]
    loads[0].start()

    def received(r):
        rows = [recv_ref[pl.ds(s * 8 + r, p.table, stride=8 * p.scal), :] for s in range(p.scal)]
        return jnp.concatenate(rows, axis=0)

    addresses = jnp.concatenate([received(4), received(6)], axis=0)
    addresses = swap_blocks(addresses, p.table, p.near)
    order = [addresses[: p.devices]]
    for s in range(p.scal):
        first = p.devices + s * p.table
        order.append(addresses[first : first + quads])
    blank = p.padded - p.chunks
    order.append(jnp.zeros((blank, LANES), jnp.float32))
    order = jnp.concatenate(order, axis=0)
    for first in range(0, p.padded, LANES):
        turned = order[first : first + LANES].T
        ints_ref[:, first : first + LANES] = turned.astype(jnp.int32)
    copies = [
        pltpu.make_async_copy(ints_ref.at[pl.ds(8 * i, 8)], idx_refs[i], sem.at[0])
        for i in range(16)
    ]
    for copy in copies:
        copy.start()
    for load in loads[1:]:
        load.start()
    fields = jnp.concatenate([received(f) for f in (0, 1, 2, 3, 5)], axis=0)
    fields = swap_blocks(fields, p.table, p.near)
    for f in range(4):
        field_ref[f * p.chunks : f * p.chunks + p.devices, :] = fields[
            f * p.devices : (f + 1) * p.devices
        ]
        for s in range(p.scal):
            first = 4 * p.devices + s * p.table + f * quads
            to = f * p.chunks + p.devices + s * quads
            field_ref[to : to + quads, :] = fields[first : first + quads]
    for copy in copies:
        copy.wait()

    def fetch(store, chunk, part):
        step = LANES // p.cols
        for slot in range(part * step, (part + 1) * step):
            address = idx_refs[slot // 8][slot % 8, chunk]
            if p.cols == 1:
                store[slot : slot + 1, :] = table_ref[pl.ds(address, 1), :]
            else:
                store[slot * p.cols : (slot + 1) * p.cols, :] = table_ref[
                    pl.ds(address, p.cols, stride=8), :
                ]

    def reduce(store, chunk, ahead=None):
        weights = spline_rows([field_ref[pl.ds(f * p.chunks + chunk, 1), :] for f in range(4)])
        parts = []
        for c in range(p.cols):
            rows = pl.ds(c, LANES, stride=p.cols) if p.cols > 1 else pl.ds(0, LANES)
            turned = store[rows, :].T
            for m in range(4):
                product = turned[m * K : (m + 1) * K] * weights
                parts.append((product[0:8] + product[8:16]) + (product[16:24] + product[24:32]))
            if ahead is not None:
                ahead(c)
        tile = jnp.sum(jnp.concatenate(parts, axis=0).reshape(p.scalars, 8, LANES), axis=1)
        tile_ref[pl.ds(pl.multiple_of(chunk * p.scalars, p.scalars), p.scalars), :] = tile

    for load in loads:
        load.wait()
    for n in range(BATCH):
        for c in range(p.cols):
            fetch(stores[n], n, c)

    def batch(now, half, more):
        for n in range(BATCH):
            ahead = None
            if more:
                store = stores[(1 - half) * BATCH + n]
                ahead = functools.partial(fetch, store, now + BATCH + n)
            reduce(stores[half * BATCH + n], now + n, ahead)

    def two_batches(i, carry):
        batch(2 * i * BATCH, 0, True)
        batch((2 * i + 1) * BATCH, 1, True)
        return carry

    lax.fori_loop(0, p.chunks // (2 * BATCH) - 1, two_batches, 0)
    batch(p.chunks - 2 * BATCH, 0, True)
    batch(p.chunks - BATCH, 1, False)

    for g in range(p.table):
        for s in range(p.scal):
            dest, chunk = g * p.scal + s, s * p.table + g
            out_ref[dest * p.rows : dest * p.rows + p.scalars, :] = tile_ref[
                chunk * p.scalars : (chunk + 1) * p.scalars, :
            ]
    quad_of = (iota((1, LANES), 1) // p.far) % 4
    for quad in range(quads):
        for s in range(p.scal):
            first = (p.devices + s * quads + quad) * p.scalars
            tile = tile_ref[first : first + p.scalars, :]
            turned = [pltpu.roll(tile, (d * p.far) % LANES, 1) if d else tile for d in range(4)]
            wrapped = [
                pltpu.roll(tile, (-d * p.far) % LANES, 1) if d else tile for d in range(4)
            ]
            for i in range(4):
                message = jnp.zeros((p.few, LANES), jnp.float32)
                for b in range(4):
                    moved = turned[b - i] if b >= i else wrapped[i - b]
                    message = jnp.where(
                        quad_of == b, moved[b * p.few : (b + 1) * p.few], message
                    )
                start = ((quad * 4 + i) * p.scal + s) * p.rows + p.scalars
                out_ref[start : start + p.few, :] = message


def lookup_scratch(plan, table_shape):
    p = plan
    return [
        pltpu.VMEM(table_shape, jnp.float32),
        pltpu.VMEM((LANES, p.padded), jnp.int32),
        pltpu.VMEM((4 * p.chunks, LANES), jnp.float32),
        pltpu.VMEM((p.chunks * p.scalars, LANES), jnp.float32),
        pltpu.SemaphoreType.DMA((4,)),
    ] + [pltpu.SMEM((8, p.padded), jnp.int32)] * 16 + [pltpu.VMEM((p.cols * LANES, LANES), jnp.float32) for _ in range(2 * BATCH)]


def slots_kernel(plan, me_ref, recv_ref, out_ref):
    p = plan
    table_at, scal_at = me_ref[0], me_ref[1]
    half_x = p.nx // 2
    width = LG * half_x
    codes = recv_ref[pl.ds(scal_at * 8 + 7, p.table, stride=8 * p.scal), :].astype(jnp.bfloat16)
    step = 2 * LANES
    for h in range(2):
        x = iota((1, width), 1) % half_x + h * half_x
        inside = (iota((1, width), 1) // half_x) * BX + x % BX + GROUP * (table_at % 2)
        move = (iota((LANES, width), 0) == inside).astype(jnp.float32).astype(jnp.bfloat16)
        moved = jnp.dot(codes, move, preferred_element_type=jnp.float32)
        t = x // BX
        moved = jnp.where(iota((p.table, width), 0) == t, moved, 0.0)
        code = jnp.sum(moved, axis=0, keepdims=True).astype(jnp.int32)
        shard, slot = code // p.code, code % p.code
        t = t - h * (p.table // 2)
        near = (shard // 2) * LANES + (shard % 2) * GROUP + t * p.near + slot
        quad = shard // 4
        far = (p.table // 2 + quad // 2) * LANES + (quad % 2) * GROUP
        far = far + t * p.quad + (shard % 4) * p.far + slot - p.near
        chosen = jnp.where(slot < p.near, near, far)
        rows = iota((step, width), 0)

        def fill(i, carry):
            start = pl.multiple_of(i * step, step)
            hit = rows == chosen - start
            out_ref[h, pl.ds(start, step), :] = jnp.where(hit, 1.0, 0.0).astype(jnp.bfloat16)
            return carry

        lax.fori_loop(0, out_ref.shape[1] // step, fill, 0)


def filter_kernel(plan, recv_ref, place_ref, op_ref, filtered_ref, gradient_ref, *left_refs):
    p = plan
    lane = iota((1, LANES), 1)
    low = lane < GROUP
    quad_of = (lane // p.far) % 4

    def halves(first, second, rows, col):
        turned = [pltpu.roll(tile, GROUP, 1) for tile in (first, second)]
        left_refs[0][rows, col : col + LANES] = jnp.where(low, first, turned[1])
        left_refs[1][rows, col : col + LANES] = jnp.where(low, turned[0], second)

    for o in range(0, p.table, 2):
        for sc in range(p.scal):
            tiles = []
            for i in range(2):
                start = ((o + i) * p.scal + sc) * p.rows
                tiles.append(recv_ref[start : start + p.scalars, :])
            halves(*tiles, slice(sc * p.scalars, (sc + 1) * p.scalars), o // 2 * LANES)
    for quad in range(0, p.table // 4, 2):
        for sc in range(p.scal):
            for b in range(4):
                parts = []
                for n in range(2):
                    part = jnp.zeros((p.few, LANES), jnp.float32)
                    for i in range(4):
                        start = (((quad + n) * 4 + i) * p.scal + sc) * p.rows + p.scalars
                        turned = recv_ref[start : start + p.few, :]
                        turned = pltpu.roll(turned, ((i - b) * p.far) % LANES, 1)
                        part = jnp.where(quad_of == i, turned, part)
                    parts.append(part)
                row = sc * p.scalars + b * p.few
                halves(*parts, slice(row, row + p.few), (p.table + quad) // 2 * LANES)
    sides = []
    for h in range(2):
        left = jnp.concatenate(pieces_of(left_refs[h][...], 3), axis=0)
        values = jnp.dot(left, place_ref[h], preferred_element_type=jnp.float32)
        sides.append(
            values[0:SCAL_ALL] + values[SCAL_ALL : 2 * SCAL_ALL] + values[2 * SCAL_ALL :]
        )
    half_x = p.nx // 2
    lines = jnp.concatenate(
        [
            jnp.concatenate([side[:, r * half_x : (r + 1) * half_x] for side in sides], axis=1)
            for r in range(LG)
        ],
        axis=0,
    )
    both = jnp.dot(
        lines, op_ref[...], precision=lax.Precision.HIGHEST, preferred_element_type=jnp.float32
    )
    for r in range(LG):
        rows = slice(r * SCAL_ALL, (r + 1) * SCAL_ALL)
        for part in range(p.nx // LANES):
            at = pl.ds(part * SCAL_ALL * LG + r, SCAL_ALL, stride=LG)
            first = part * LANES
            filtered_ref[at, :] = both[rows, first : first + LANES]
            gradient_ref[at, :] = both[rows, p.nx + first : p.nx + first + LANES]


VMEM = pl.BlockSpec(memory_space=pltpu.VMEM)
SMEM = pl.BlockSpec(memory_space=pltpu.SMEM)
HBM = pl.BlockSpec(memory_space=pltpu.HBM)


def call(kernel, plan, out_shape, in_specs, scratch, limit, cost, name):
    many = isinstance(out_shape, tuple)
    return pl.pallas_call(
        functools.partial(kernel, plan),
        out_shape=out_shape,
        in_specs=in_specs,
        out_specs=(VMEM,) * len(out_shape) if many else VMEM,
        scratch_shapes=scratch,
        compiler_params=pltpu.CompilerParams(vmem_limit_bytes=limit << 20),
        cost_estimate=pl.CostEstimate(flops=cost, bytes_accessed=cost // 256, transcendentals=0),
        name=name,
    )


def exchange(array):
    return lax.all_to_all(array, AXES, split_axis=0, concat_axis=0, tiled=True)


def on_device(plan, cell_coords, flamelet_table, owner_shard, local_bin):
    p = plan
    f32, i32 = jnp.float32, jnp.int32
    row_count = p.cells // LANES
    owners = owner_shard.reshape(row_count, LANES)
    bins = local_bin.reshape(row_count, LANES)
    requests = call(
        request_kernel,
        p,
        jax.ShapeDtypeStruct((p.devices, 8, LANES), f32),
        [HBM] * 3,
        [
            pltpu.VMEM((8, p.cells), f32),
            pltpu.VMEM(cell_coords.shape, f32),
            pltpu.VMEM(owners.shape, i32),
            pltpu.VMEM(bins.shape, i32),
            pltpu.SemaphoreType.DMA((3,)),
        ],
        60,
        1 << 20,
        "requests",
    )(cell_coords, owners, bins)
    received = exchange(requests).reshape(p.devices * 8, LANES)

    bin_count, depth = flamelet_table.shape
    table = flamelet_table.reshape(bin_count // 8, 8, p.cols, LANES).transpose(0, 2, 1, 3)
    table = table.reshape(bin_count * p.cols, LANES)
    early = table[: bin_count * p.cols * 11 // 32]
    replies = call(
        lookup_kernel,
        p,
        jax.ShapeDtypeStruct((p.devices * p.rows, LANES), f32),
        [VMEM, VMEM, HBM],
        lookup_scratch(p, table.shape),
        50,
        1 << 24,
        "lookup",
    )(received, early, table)
    answers = exchange(replies.reshape(p.devices, 1, p.rows * LANES))
    answers = answers.reshape(p.devices * p.rows, LANES)

    me = jnp.stack([lax.axis_index("table"), lax.axis_index("scal")]).astype(i32)
    place = call(
        slots_kernel,
        p,
        jax.ShapeDtypeStruct((2, p.table * 5 * LANES // 8, LG * p.nx // 2), jnp.bfloat16),
        [SMEM, VMEM],
        [],
        8 + p.nx * p.table // 128,
        1 << 24,
        "slots",
    )(me, received)
    filter_op = filter_table(p.nx).T
    both_op = np.concatenate([filter_op, filter_op @ derivative_table(p.nx).T], axis=1)
    out = jax.ShapeDtypeStruct((p.nx // LANES * SCAL_ALL * LG, LANES), f32)
    outs = call(
        filter_kernel,
        p,
        (out, out),
        [VMEM] * 3,
        [pltpu.VMEM((SCAL_ALL, p.table * 5 * LANES // 8), f32)] * 2,
        8 + p.nx * p.table // 64,
        1 << 24,
        "filter",
    )(answers, place, jnp.asarray(both_op.astype(np.float32)))
    outs = [out.reshape(p.nx // LANES, SCAL_ALL, LG, LANES).transpose(1, 2, 0, 3) for out in outs]
    return tuple(out.reshape(SCAL_ALL, LG, p.nx) for out in outs)


def solution(mesh):
    table, scal = mesh.shape["table"], mesh.shape["scal"]

    def step(cell_coords, flamelet_table, owner_shard, local_bin):
        plan = Plan(table, scal, cell_coords.shape[1])
        return on_device(plan, cell_coords, flamelet_table, owner_shard, local_bin)

    return jax.shard_map(
        step,
        mesh=mesh,
        in_specs=(
            P(None, AXES),
            P("table", "scal"),
            P(AXES, None),
            P(AXES),
        ),
        out_specs=(P(None, AXES, None), P(None, AXES, None)),
        check_vma=False,
    )
```

```python
import functools

import jax
import jax.numpy as jnp
import numpy as np
from jax import lax
from jax.experimental import pallas as pl
from jax.experimental.pallas import tpu as pltpu
from jax.sharding import PartitionSpec as P

SCAL_ALL = 32
K = 32
BX = 8
LG = 8
GROUP = BX * LG
LANES = 128
AXES = ("table", "scal")
BATCH = 4

strength = 0.499


def thomas_solve(below, middle, above, right_side):
    length = middle.shape[0]
    upper_factor = np.zeros(length)
    solved = np.zeros(right_side.shape)
    for row in range(length):
        if row == 0:
            denom = middle[0]
            solved[0] = right_side[0] / denom
        else:
            denom = middle[row] - below[row] * upper_factor[row - 1]
            solved[row] = (right_side[row] - below[row] * solved[row - 1]) / denom
        upper_factor[row] = above[row] / denom
    for row in range(length - 2, -1, -1):
        solved[row] = solved[row] - upper_factor[row] * solved[row + 1]
    return solved


def filter_table(length):
    positions = np.arange(length)
    offset = positions[None, :] - positions[:, None]
    distance = np.abs(offset)
    interior = (positions >= 3) & (positions <= length - 4)
    coeffs = [
        (11.0 + 10.0 * strength) / 16.0,
        (15.0 + 34.0 * strength) / 64.0,
        (-3.0 + 6.0 * strength) / 32.0,
        (1.0 - 2.0 * strength) / 64.0,
    ]
    band = np.zeros((length, length))
    for reach in range(4):
        band = band + np.where(distance == reach, coeffs[reach], 0.0)
    right_side = np.where(interior[:, None], band, np.where(offset == 0, 1.0, 0.0))
    coupling = np.where(interior, strength, 0.0)
    return thomas_solve(coupling, np.ones(length), coupling, right_side)


def derivative_table(length):
    positions = np.arange(length)
    offset = positions[None, :] - positions[:, None]
    distance = np.abs(offset)
    direction = np.sign(offset) * 1.0
    boundary = (positions == 0) | (positions == length - 1)
    second = (positions == 1) | (positions == length - 2)
    interior = ~(boundary | second)
    below_diag = np.where(
        interior, 1.0 / 3.0, np.where(second, 0.25, np.where(positions == length - 1, 2.0, 0.0))
    )
    above_diag = np.where(
        interior, 1.0 / 3.0, np.where(second, 0.25, np.where(positions == 0, 2.0, 0.0))
    )
    inner_rows = direction * (
        np.where(distance == 1, 7.0 / 9.0, 0.0) + np.where(distance == 2, 1.0 / 36.0, 0.0)
    )
    second_rows = direction * np.where(distance == 1, 0.75, 0.0)
    first_row = np.where(
        offset == 0, -2.5, np.where(offset == 1, 2.0, np.where(offset == 2, 0.5, 0.0))
    )
    final_row = np.where(
        offset == 0, 2.5, np.where(offset == -1, -2.0, np.where(offset == -2, -0.5, 0.0))
    )
    right_side = np.where(
        interior[:, None],
        inner_rows,
        np.where(
            second[:, None], second_rows, np.where((positions == 0)[:, None], first_row, final_row)
        ),
    )
    return thomas_solve(below_diag, np.ones(length), above_diag, right_side)


class Plan:
    def __init__(self, table, scal, cells):
        self.table, self.scal, self.cells = table, scal, cells
        self.devices = table * scal
        self.cap = max(2, 5 * GROUP // (2 * table))
        self.near = LANES // table
        self.far = self.cap - self.near
        self.quad = 4 * self.far
        assert cells == table * GROUP and table * self.quad == LANES
        self.code = 1 << (self.cap - 1).bit_length()
        self.scalars = SCAL_ALL // scal
        self.cols = self.scalars * K // LANES
        self.few = self.scalars // 4
        self.rows = self.scalars + self.few
        self.nx = BX * table
        self.chunks = self.devices + self.devices // 4
        self.padded = -(-self.chunks // LANES) * LANES


def iota(shape, dim):
    return lax.broadcasted_iota(jnp.int32, shape, dim)


def pieces_of(values, count):
    pieces = []
    for _ in range(count - 1):
        piece = values.astype(jnp.bfloat16)
        pieces.append(piece)
        values = values - piece.astype(jnp.float32)
    pieces.append(values.astype(jnp.bfloat16))
    return pieces


def dot_rows(a, b):
    return lax.dot_general(a, b, (((1,), (1,)), ((), ())), preferred_element_type=jnp.float32)


def request_kernel(
    plan,
    coords_in,
    owner_in,
    bin_in,
    table_in,
    out_ref,
    early_ref,
    x_ref,
    coords_ref,
    owner_ref,
    bin_ref,
    sem,
):
    p = plan
    row_count = p.cells // LANES
    copies = [
        pltpu.make_async_copy(owner_in, owner_ref, sem.at[0]),
        pltpu.make_async_copy(bin_in, bin_ref, sem.at[1]),
        pltpu.make_async_copy(coords_in, coords_ref, sem.at[2]),
    ]
    early = pltpu.make_async_copy(
        table_in.at[pl.ds(0, early_ref.shape[0])], early_ref, sem.at[3]
    )
    for copy in copies + [early]:
        copy.start()
    for copy in copies:
        copy.wait()
    half = iota((1, LANES), 1) // GROUP
    shard_ids = iota((p.table, LANES), 0)
    owners = owner_ref[...]
    bins = bin_ref[...]
    address = ((bins >> 3) * (8 * p.cols) + (bins & 7)).astype(jnp.float32)
    hits = [owners[i : i + 1, :] == shard_ids for i in range(row_count)]
    before = iota((LANES, LANES), 0)
    after = iota((LANES, LANES), 1)
    earlier = ((before < after) & (before // GROUP == after // GROUP)).astype(jnp.bfloat16)
    ones = jnp.concatenate([h.astype(jnp.float32) for h in hits], axis=0)
    counts = jnp.dot(ones.astype(jnp.bfloat16), earlier, preferred_element_type=jnp.float32)
    x_ref[0:4, :] = coords_ref[...]
    x_ref[5:8, :] = jnp.zeros((3, p.cells), jnp.float32)
    for i in range(row_count):
        x_ref[4:5, i * LANES : (i + 1) * LANES] = address[i : i + 1, :]
    lane_rows = iota((LANES, LANES), 0)
    left, right, codes = [], [], []
    for i in range(row_count):
        span = slice(i * p.table, (i + 1) * p.table)
        rank = jnp.sum(ones[span] * counts[span], axis=0, keepdims=True).astype(jnp.int32)
        codes.append((owners[i : i + 1, :] * p.code + rank).astype(jnp.float32))
        group = 2 * i + half
        near = jnp.where(rank < p.near, group * p.near + rank, -1)
        far = jnp.where(rank >= p.near, group * p.far + rank - p.near, -1)
        right.append(
            jnp.concatenate(
                [
                    (lane_rows == near).astype(jnp.float32),
                    (lane_rows % 32 == far).astype(jnp.float32),
                ],
                axis=0,
            ).astype(jnp.bfloat16)
        )
        fields = x_ref[:, i * LANES : (i + 1) * LANES]
        chosen = []
        for piece in pieces_of(fields, 3):
            piece = jnp.where(hits[i][:, None, :], piece.astype(jnp.float32)[None], 0.0)
            chosen.append(piece.reshape(p.table * 8, LANES).astype(jnp.bfloat16))
        left.append(jnp.concatenate(chosen, axis=0))
    placed = dot_rows(jnp.concatenate(left, axis=1), jnp.concatenate(right, axis=1))
    total = p.table * 8
    placed = placed[0:total] + placed[total : 2 * total] + placed[2 * total :]
    sub = iota((8, LANES), 0)
    block = iota((8, LANES), 1) // 32
    for o in range(p.table):
        near_part = placed[o * 8 : (o + 1) * 8, :LANES]
        far_part = placed[o * 8 : (o + 1) * 8, LANES:]
        far_coords = jnp.sum(jnp.where(sub == block, far_part, 0.0), axis=0, keepdims=True)
        message = jnp.where(
            sub < 5,
            near_part,
            jnp.where(sub == 5, far_coords, jnp.where(sub == 6, far_part[4:5], codes[o // 2])),
        )
        for sc in range(p.scal):
            out_ref[o * p.scal + sc] = message
    early.wait()


def spline_rows(f):
    shape = (K, f[0].shape[1])
    k = iota(shape, 0)
    product = None
    for axis, bit in ((0, 16), (1, 8), (2, 4)):
        factor = jnp.where((k & bit) != 0, f[axis], 1.0 - f[axis])
        product = factor if product is None else product * factor
    last = f[3]
    square = last * last
    cube = square * last
    remain = 1.0 - last
    basis = [
        remain * remain * remain / 6.0,
        (3.0 * cube - 6.0 * square + 4.0) / 6.0,
        (-3.0 * cube + 3.0 * square + 3.0 * last + 1.0) / 6.0,
        cube / 6.0,
    ]
    d = k & 3
    cubic = jnp.where(d == 0, basis[0], jnp.where(d == 1, basis[1], jnp.where(d == 2, basis[2], basis[3])))
    return product * cubic


def swap_blocks(x, count, width):
    row, block = iota(x.shape, 0), iota(x.shape, 1) // width
    bit = 1
    while bit < count:
        up = pltpu.roll(pltpu.roll(x, x.shape[0] - bit, 0), bit * width, 1)
        down = pltpu.roll(pltpu.roll(x, bit, 0), LANES - bit * width, 1)
        low_row, low_block = (row & bit) == 0, (block & bit) == 0
        x = jnp.where(low_row == low_block, x, jnp.where(low_row, up, down))
        bit *= 2
    return x


def fill_slots(plan, me_ref, recv_ref, out_ref):
    p = plan
    table_at, scal_at = me_ref[0], me_ref[1]
    part_x = p.nx // 4
    width = LG * part_x
    codes = recv_ref[pl.ds(scal_at * 8 + 7, p.table, stride=8 * p.scal), :].astype(jnp.bfloat16)
    step = LANES
    for h in range(4):
        x = iota((1, width), 1) % part_x + h * part_x
        inside = (iota((1, width), 1) // part_x) * BX + x % BX + GROUP * (table_at % 2)
        move = (iota((LANES, width), 0) == inside).astype(jnp.float32).astype(jnp.bfloat16)
        moved = jnp.dot(codes, move, preferred_element_type=jnp.float32)
        t = x // BX
        moved = jnp.where(iota((p.table, width), 0) == t, moved, 0.0)
        code = jnp.sum(moved, axis=0, keepdims=True).astype(jnp.int32)
        shard, slot = code // p.code, code % p.code
        t = t - h * (p.table // 4)
        near = (shard // 4) * LANES + (shard % 4) * 32 + t * p.near + slot
        quad = shard // 4
        far = (p.table // 4 + quad // 4) * LANES + (quad % 4) * 32
        far = far + t * p.quad + (shard % 4) * p.far + slot - p.near
        chosen = jnp.where(slot < p.near, near, far)
        rows = iota((step, width), 0)
        for start in range(0, out_ref.shape[1], step):
            hit = rows == chosen - start
            out_ref[h, start : start + step, :] = jnp.where(hit, 1.0, 0.0).astype(jnp.bfloat16)


def swap_four(tiles):
    block = iota((1, LANES), 1) // 32
    for bit in (2, 1):
        low = (block & bit) == 0
        turned = [pltpu.roll(tile, 32 * bit, 1) for tile in tiles]
        back = [pltpu.roll(tile, LANES - 32 * bit, 1) for tile in tiles] if bit == 1 else turned
        out = list(tiles)
        for i in range(4):
            if not i & bit:
                out[i] = jnp.where(low, tiles[i], turned[i + bit])
                out[i + bit] = jnp.where(low, back[i], tiles[i + bit])
        tiles = out
    return tiles


def lookup_kernel(
    plan,
    me_ref,
    recv_ref,
    early_ref,
    table_in,
    out_ref,
    place_ref,
    table_ref,
    ints_ref,
    field_ref,
    tile_ref,
    sem,
    *rest,
):
    p = plan
    idx_refs, stores = rest[:16], rest[16:]
    quads = p.table // 4
    early = early_ref.shape[0]
    late = table_ref.shape[0] - early
    loads = [
        pltpu.make_async_copy(
            table_in.at[pl.ds(early, late // 2)], table_ref.at[pl.ds(early, late // 2)], sem.at[1]
        ),
        pltpu.make_async_copy(
            table_in.at[pl.ds(early + late // 2, late // 2)],
            table_ref.at[pl.ds(early + late // 2, late // 2)],
            sem.at[2],
        ),
        pltpu.make_async_copy(early_ref, table_ref.at[pl.ds(0, early)], sem.at[3]),
    ]
    loads[0].start()

    def received(r):
        rows = [recv_ref[pl.ds(s * 8 + r, p.table, stride=8 * p.scal), :] for s in range(p.scal)]
        return jnp.concatenate(rows, axis=0)

    addresses = jnp.concatenate([received(4), received(6)], axis=0)
    addresses = swap_blocks(addresses, p.table, p.near)
    order = [addresses[: p.devices]]
    for s in range(p.scal):
        first = p.devices + s * p.table
        order.append(addresses[first : first + quads])
    blank = p.padded - p.chunks
    order.append(jnp.zeros((blank, LANES), jnp.float32))
    order = jnp.concatenate(order, axis=0)
    for first in range(0, p.padded, LANES):
        turned = order[first : first + LANES].T
        ints_ref[:, first : first + LANES] = turned.astype(jnp.int32)
    copies = [
        pltpu.make_async_copy(ints_ref.at[pl.ds(8 * i, 8)], idx_refs[i], sem.at[0])
        for i in range(16)
    ]
    for copy in copies:
        copy.start()
    for load in loads[1:]:
        load.start()
    fields = jnp.concatenate([received(f) for f in (0, 1, 2, 3, 5)], axis=0)
    fields = swap_blocks(fields, p.table, p.near)
    for f in range(4):
        field_ref[f * p.chunks : f * p.chunks + p.devices, :] = fields[
            f * p.devices : (f + 1) * p.devices
        ]
        for s in range(p.scal):
            first = 4 * p.devices + s * p.table + f * quads
            to = f * p.chunks + p.devices + s * quads
            field_ref[to : to + quads, :] = fields[first : first + quads]
    fill_slots(p, me_ref, recv_ref, place_ref)
    for copy in copies:
        copy.wait()

    def fetch(store, chunk, part):
        step = LANES // p.cols
        for slot in range(part * step, (part + 1) * step):
            address = idx_refs[slot // 8][slot % 8, chunk]
            if p.cols == 1:
                store[slot : slot + 1, :] = table_ref[pl.ds(address, 1), :]
            else:
                store[slot * p.cols : (slot + 1) * p.cols, :] = table_ref[
                    pl.ds(address, p.cols, stride=8), :
                ]

    def reduce(store, chunk, ahead=None):
        weights = spline_rows([field_ref[pl.ds(f * p.chunks + chunk, 1), :] for f in range(4)])
        parts = []
        for c in range(p.cols):
            rows = pl.ds(c, LANES, stride=p.cols) if p.cols > 1 else pl.ds(0, LANES)
            turned = store[rows, :].T
            for m in range(4):
                product = turned[m * K : (m + 1) * K] * weights
                parts.append((product[0:8] + product[8:16]) + (product[16:24] + product[24:32]))
            if ahead is not None:
                ahead(c)
        tile = jnp.sum(jnp.concatenate(parts, axis=0).reshape(p.scalars, 8, LANES), axis=1)
        tile_ref[pl.ds(pl.multiple_of(chunk * p.scalars, p.scalars), p.scalars), :] = tile

    for load in loads:
        load.wait()
    for n in range(BATCH):
        for c in range(p.cols):
            fetch(stores[n], n, c)

    def batch(now, half, more):
        for n in range(BATCH):
            ahead = None
            if more:
                store = stores[(1 - half) * BATCH + n]
                ahead = functools.partial(fetch, store, now + BATCH + n)
            reduce(stores[half * BATCH + n], now + n, ahead)

    def two_batches(i, carry):
        batch(2 * i * BATCH, 0, True)
        batch((2 * i + 1) * BATCH, 1, True)
        return carry

    lax.fori_loop(0, p.chunks // (2 * BATCH) - 1, two_batches, 0)
    batch(p.chunks - 2 * BATCH, 0, True)
    batch(p.chunks - BATCH, 1, False)

    for g in range(p.table):
        for s in range(p.scal):
            dest, chunk = g * p.scal + s, s * p.table + g
            out_ref[dest * p.rows : dest * p.rows + p.scalars, :] = tile_ref[
                chunk * p.scalars : (chunk + 1) * p.scalars, :
            ]
    quad_of = (iota((1, LANES), 1) // p.far) % 4
    for quad in range(quads):
        for s in range(p.scal):
            first = (p.devices + s * quads + quad) * p.scalars
            tile = tile_ref[first : first + p.scalars, :]
            turned = [pltpu.roll(tile, (d * p.far) % LANES, 1) if d else tile for d in range(4)]
            wrapped = [
                pltpu.roll(tile, (-d * p.far) % LANES, 1) if d else tile for d in range(4)
            ]
            for i in range(4):
                message = jnp.zeros((p.few, LANES), jnp.float32)
                for b in range(4):
                    moved = turned[b - i] if b >= i else wrapped[i - b]
                    message = jnp.where(
                        quad_of == b, moved[b * p.few : (b + 1) * p.few], message
                    )
                start = ((quad * 4 + i) * p.scal + s) * p.rows + p.scalars
                out_ref[start : start + p.few, :] = message


def lookup_scratch(plan, table_shape):
    p = plan
    return [
        pltpu.VMEM(table_shape, jnp.float32),
        pltpu.VMEM((LANES, p.padded), jnp.int32),
        pltpu.VMEM((4 * p.chunks, LANES), jnp.float32),
        pltpu.VMEM((p.chunks * p.scalars, LANES), jnp.float32),
        pltpu.SemaphoreType.DMA((4,)),
    ] + [pltpu.SMEM((8, p.padded), jnp.int32)] * 16 + [pltpu.VMEM((p.cols * LANES, LANES), jnp.float32) for _ in range(2 * BATCH)]


def filter_kernel(plan, recv_ref, place_ref, op_ref, filtered_ref, gradient_ref, *left_refs):
    p = plan
    quad_of = (iota((1, LANES), 1) // p.far) % 4

    def put(tiles, first_row, col):
        for left_ref, tile in zip(left_refs, swap_four(tiles), strict=True):
            left_ref[first_row : first_row + tile.shape[0], col : col + LANES] = tile

    for sc in range(p.scal):
        for o in range(0, p.table, 4):
            starts = [((o + i) * p.scal + sc) * p.rows for i in range(4)]
            tiles = [recv_ref[start : start + p.scalars, :] for start in starts]
            put(tiles, sc * p.scalars, o // 4 * LANES)
        for quad in range(0, p.table // 4, 4):
            tiles = []
            for n in range(4):
                starts = [((quad + n) * 4 + i) * p.scal + sc for i in range(4)]
                starts = [start * p.rows + p.scalars for start in starts]
                tile = []
                for b in range(4):
                    part = jnp.zeros((p.few, LANES), jnp.float32)
                    for i in range(4):
                        turned = recv_ref[starts[i] : starts[i] + p.few, :]
                        turned = pltpu.roll(turned, ((i - b) * p.far) % LANES, 1)
                        part = jnp.where(quad_of == i, turned, part)
                    tile.append(part)
                tiles.append(jnp.concatenate(tile, axis=0))
            put(tiles, sc * p.scalars, (p.table // 4 + quad // 4) * LANES)
    sides = []
    for h in range(4):
        left = jnp.concatenate(pieces_of(left_refs[h][...], 3), axis=0)
        values = jnp.dot(left, place_ref[h], preferred_element_type=jnp.float32)
        sides.append(
            values[0:SCAL_ALL] + values[SCAL_ALL : 2 * SCAL_ALL] + values[2 * SCAL_ALL :]
        )
    part_x = p.nx // 4
    if part_x == 32:
        lines = []
        for first in range(0, LG * part_x, LANES):
            lines.extend(swap_four([side[:, first : first + LANES] for side in sides]))
    else:
        lines = [
            jnp.concatenate([side[:, r * part_x : (r + 1) * part_x] for side in sides], axis=1)
            for r in range(LG)
        ]
    lines = jnp.concatenate(lines, axis=0)
    both = jnp.dot(
        lines, op_ref[...], precision=lax.Precision.HIGHEST, preferred_element_type=jnp.float32
    )
    for r in range(LG):
        rows = slice(r * SCAL_ALL, (r + 1) * SCAL_ALL)
        for part in range(p.nx // LANES):
            at = pl.ds(part * SCAL_ALL * LG + r, SCAL_ALL, stride=LG)
            first = part * LANES
            filtered_ref[at, :] = both[rows, first : first + LANES]
            gradient_ref[at, :] = both[rows, p.nx + first : p.nx + first + LANES]


VMEM = pl.BlockSpec(memory_space=pltpu.VMEM)
SMEM = pl.BlockSpec(memory_space=pltpu.SMEM)
HBM = pl.BlockSpec(memory_space=pltpu.HBM)


def call(kernel, plan, out_shape, in_specs, scratch, limit, cost, name):
    many = isinstance(out_shape, tuple)
    return pl.pallas_call(
        functools.partial(kernel, plan),
        out_shape=out_shape,
        in_specs=in_specs,
        out_specs=(VMEM,) * len(out_shape) if many else VMEM,
        scratch_shapes=scratch,
        compiler_params=pltpu.CompilerParams(vmem_limit_bytes=limit << 20),
        cost_estimate=pl.CostEstimate(flops=cost, bytes_accessed=cost // 256, transcendentals=0),
        name=name,
    )


def exchange(array):
    return lax.all_to_all(array, AXES, split_axis=0, concat_axis=0, tiled=True)


def on_device(plan, cell_coords, flamelet_table, owner_shard, local_bin):
    p = plan
    f32, i32 = jnp.float32, jnp.int32
    row_count = p.cells // LANES
    owners = owner_shard.reshape(row_count, LANES)
    bins = local_bin.reshape(row_count, LANES)
    bin_count, depth = flamelet_table.shape
    table = flamelet_table.reshape(bin_count // 8, 8, p.cols, LANES).transpose(0, 2, 1, 3)
    table = table.reshape(bin_count * p.cols, LANES)
    requests, early = call(
        request_kernel,
        p,
        (
            jax.ShapeDtypeStruct((p.devices, 8, LANES), f32),
            jax.ShapeDtypeStruct((bin_count * p.cols * 11 // 32, LANES), f32),
        ),
        [HBM] * 4,
        [
            pltpu.VMEM((8, p.cells), f32),
            pltpu.VMEM(cell_coords.shape, f32),
            pltpu.VMEM(owners.shape, i32),
            pltpu.VMEM(bins.shape, i32),
            pltpu.SemaphoreType.DMA((4,)),
        ],
        32,
        1 << 20,
        "requests",
    )(*[pltpu.with_memory_space_constraint(a, pltpu.HBM) for a in (cell_coords, owners, bins, table)])
    me = jnp.stack([lax.axis_index("table"), lax.axis_index("scal")]).astype(i32)
    me, requests = lax.optimization_barrier((me, requests))
    received = exchange(requests).reshape(p.devices * 8, LANES)
    replies, place = call(
        lookup_kernel,
        p,
        (
            jax.ShapeDtypeStruct((p.devices * p.rows, LANES), f32),
            jax.ShapeDtypeStruct((4, p.table * 5 * LANES // 16, LG * p.nx // 4), jnp.bfloat16),
        ),
        [SMEM, VMEM, VMEM, HBM],
        lookup_scratch(p, table.shape),
        30,
        1 << 24,
        "lookup",
    )(me, received, early, pltpu.with_memory_space_constraint(table, pltpu.HBM))
    answers = exchange(replies.reshape(p.devices, 1, p.rows * LANES))
    answers = answers.reshape(p.devices * p.rows, LANES)

    filter_op = filter_table(p.nx).T
    both_op = np.concatenate([filter_op, filter_op @ derivative_table(p.nx).T], axis=1)
    both_op = jnp.asarray(both_op.astype(np.float32))
    out = jax.ShapeDtypeStruct((p.nx // LANES * SCAL_ALL * LG, LANES), f32)
    outs = call(
        filter_kernel,
        p,
        (out, out),
        [VMEM] * 3,
        [pltpu.VMEM((SCAL_ALL, p.table * 5 * LANES // 16), f32)] * 4,
        8 + p.nx * p.table // 64,
        1 << 24,
        "filter",
    )(answers, place, both_op)
    outs = [out.reshape(p.nx // LANES, SCAL_ALL, LG, LANES).transpose(1, 2, 0, 3) for out in outs]
    return tuple(out.reshape(SCAL_ALL, LG, p.nx) for out in outs)


def solution(mesh):
    table, scal = mesh.shape["table"], mesh.shape["scal"]

    def step(cell_coords, flamelet_table, owner_shard, local_bin):
        plan = Plan(table, scal, cell_coords.shape[1])
        return on_device(plan, cell_coords, flamelet_table, owner_shard, local_bin)

    return jax.shard_map(
        step,
        mesh=mesh,
        in_specs=(
            P(None, AXES),
            P("table", "scal"),
            P(AXES, None),
            P(AXES),
        ),
        out_specs=(P(None, AXES, None), P(None, AXES, None)),
        check_vma=False,
    )
```

```python
import functools

import jax
import jax.numpy as jnp
import numpy as np
from jax import lax
from jax.experimental import pallas as pl
from jax.experimental.pallas import tpu as pltpu
from jax.sharding import PartitionSpec as P

SCAL_ALL = 32
K = 32
BX = 8
LG = 8
GROUP = BX * LG
LANES = 128
AXES = ("table", "scal")
BATCH = 4

strength = 0.499


def thomas_solve(below, middle, above, right_side):
    length = middle.shape[0]
    upper_factor = np.zeros(length)
    solved = np.zeros(right_side.shape)
    for row in range(length):
        if row == 0:
            denom = middle[0]
            solved[0] = right_side[0] / denom
        else:
            denom = middle[row] - below[row] * upper_factor[row - 1]
            solved[row] = (right_side[row] - below[row] * solved[row - 1]) / denom
        upper_factor[row] = above[row] / denom
    for row in range(length - 2, -1, -1):
        solved[row] = solved[row] - upper_factor[row] * solved[row + 1]
    return solved


def filter_table(length):
    positions = np.arange(length)
    offset = positions[None, :] - positions[:, None]
    distance = np.abs(offset)
    interior = (positions >= 3) & (positions <= length - 4)
    coeffs = [
        (11.0 + 10.0 * strength) / 16.0,
        (15.0 + 34.0 * strength) / 64.0,
        (-3.0 + 6.0 * strength) / 32.0,
        (1.0 - 2.0 * strength) / 64.0,
    ]
    band = np.zeros((length, length))
    for reach in range(4):
        band = band + np.where(distance == reach, coeffs[reach], 0.0)
    right_side = np.where(interior[:, None], band, np.where(offset == 0, 1.0, 0.0))
    coupling = np.where(interior, strength, 0.0)
    return thomas_solve(coupling, np.ones(length), coupling, right_side)


def derivative_table(length):
    positions = np.arange(length)
    offset = positions[None, :] - positions[:, None]
    distance = np.abs(offset)
    direction = np.sign(offset) * 1.0
    boundary = (positions == 0) | (positions == length - 1)
    second = (positions == 1) | (positions == length - 2)
    interior = ~(boundary | second)
    below_diag = np.where(
        interior, 1.0 / 3.0, np.where(second, 0.25, np.where(positions == length - 1, 2.0, 0.0))
    )
    above_diag = np.where(
        interior, 1.0 / 3.0, np.where(second, 0.25, np.where(positions == 0, 2.0, 0.0))
    )
    inner_rows = direction * (
        np.where(distance == 1, 7.0 / 9.0, 0.0) + np.where(distance == 2, 1.0 / 36.0, 0.0)
    )
    second_rows = direction * np.where(distance == 1, 0.75, 0.0)
    first_row = np.where(
        offset == 0, -2.5, np.where(offset == 1, 2.0, np.where(offset == 2, 0.5, 0.0))
    )
    final_row = np.where(
        offset == 0, 2.5, np.where(offset == -1, -2.0, np.where(offset == -2, -0.5, 0.0))
    )
    right_side = np.where(
        interior[:, None],
        inner_rows,
        np.where(
            second[:, None], second_rows, np.where((positions == 0)[:, None], first_row, final_row)
        ),
    )
    return thomas_solve(below_diag, np.ones(length), above_diag, right_side)


class Plan:
    def __init__(self, table, scal, cells):
        self.table, self.scal, self.cells = table, scal, cells
        self.devices = table * scal
        self.cap = max(2, 5 * GROUP // (2 * table))
        self.near = LANES // table
        self.far = self.cap - self.near
        self.quad = 4 * self.far
        assert cells == table * GROUP and table * self.quad == LANES
        self.code = 1 << (self.cap - 1).bit_length()
        self.scalars = SCAL_ALL // scal
        self.cols = self.scalars * K // LANES
        self.few = self.scalars // 4
        self.rows = self.scalars + self.few
        self.nx = BX * table
        self.chunks = self.devices + self.devices // 4
        self.padded = -(-self.chunks // LANES) * LANES


def iota(shape, dim):
    return lax.broadcasted_iota(jnp.int32, shape, dim)


def pieces_of(values, count):
    pieces = []
    for _ in range(count - 1):
        piece = values.astype(jnp.bfloat16)
        pieces.append(piece)
        values = values - piece.astype(jnp.float32)
    pieces.append(values.astype(jnp.bfloat16))
    return pieces


def dot_rows(a, b):
    return lax.dot_general(a, b, (((1,), (1,)), ((), ())), preferred_element_type=jnp.float32)


def request_kernel(
    plan,
    coords_in,
    owner_in,
    bin_in,
    table_in,
    out_ref,
    early_ref,
    x_ref,
    coords_ref,
    owner_ref,
    bin_ref,
    sem,
):
    p = plan
    row_count = p.cells // LANES
    copies = [
        pltpu.make_async_copy(owner_in, owner_ref, sem.at[0]),
        pltpu.make_async_copy(bin_in, bin_ref, sem.at[1]),
        pltpu.make_async_copy(coords_in, coords_ref, sem.at[2]),
    ]
    early = pltpu.make_async_copy(
        table_in.at[pl.ds(0, early_ref.shape[0])], early_ref, sem.at[3]
    )
    for copy in copies + [early]:
        copy.start()
    for copy in copies:
        copy.wait()
    half = iota((1, LANES), 1) // GROUP
    shard_ids = iota((p.table, LANES), 0)
    owners = owner_ref[...]
    bins = bin_ref[...]
    address = ((bins >> 3) * (8 * p.cols) + (bins & 7)).astype(jnp.float32)
    hits = [owners[i : i + 1, :] == shard_ids for i in range(row_count)]
    before = iota((LANES, LANES), 0)
    after = iota((LANES, LANES), 1)
    earlier = ((before < after) & (before // GROUP == after // GROUP)).astype(jnp.bfloat16)
    ones = jnp.concatenate([h.astype(jnp.float32) for h in hits], axis=0)
    counts = jnp.dot(ones.astype(jnp.bfloat16), earlier, preferred_element_type=jnp.float32)
    x_ref[0:4, :] = coords_ref[...]
    x_ref[5:8, :] = jnp.zeros((3, p.cells), jnp.float32)
    for i in range(row_count):
        x_ref[4:5, i * LANES : (i + 1) * LANES] = address[i : i + 1, :]
    lane_rows = iota((LANES, LANES), 0)
    left, right, codes = [], [], []
    for i in range(row_count):
        span = slice(i * p.table, (i + 1) * p.table)
        rank = jnp.sum(ones[span] * counts[span], axis=0, keepdims=True).astype(jnp.int32)
        codes.append((owners[i : i + 1, :] * p.code + rank).astype(jnp.float32))
        group = 2 * i + half
        near = jnp.where(rank < p.near, group * p.near + rank, -1)
        far = jnp.where(rank >= p.near, group * p.far + rank - p.near, -1)
        right.append(
            jnp.concatenate(
                [
                    (lane_rows == near).astype(jnp.float32),
                    (lane_rows % 32 == far).astype(jnp.float32),
                ],
                axis=0,
            ).astype(jnp.bfloat16)
        )
        fields = x_ref[:, i * LANES : (i + 1) * LANES]
        chosen = []
        for piece in pieces_of(fields, 3):
            piece = jnp.where(hits[i][:, None, :], piece.astype(jnp.float32)[None], 0.0)
            chosen.append(piece.reshape(p.table * 8, LANES).astype(jnp.bfloat16))
        left.append(jnp.concatenate(chosen, axis=0))
    placed = dot_rows(jnp.concatenate(left, axis=1), jnp.concatenate(right, axis=1))
    total = p.table * 8
    placed = placed[0:total] + placed[total : 2 * total] + placed[2 * total :]
    sub = iota((8, LANES), 0)
    block = iota((8, LANES), 1) // 32
    for o in range(p.table):
        near_part = placed[o * 8 : (o + 1) * 8, :LANES]
        far_part = placed[o * 8 : (o + 1) * 8, LANES:]
        far_coords = jnp.sum(jnp.where(sub == block, far_part, 0.0), axis=0, keepdims=True)
        message = jnp.where(
            sub < 5,
            near_part,
            jnp.where(sub == 5, far_coords, jnp.where(sub == 6, far_part[4:5], codes[o // 2])),
        )
        for sc in range(p.scal):
            out_ref[o * p.scal + sc] = message
    early.wait()


def spline_rows(f):
    shape = (K, f[0].shape[1])
    k = iota(shape, 0)
    product = None
    for axis, bit in ((0, 16), (1, 8), (2, 4)):
        factor = jnp.where((k & bit) != 0, f[axis], 1.0 - f[axis])
        product = factor if product is None else product * factor
    last = f[3]
    square = last * last
    cube = square * last
    remain = 1.0 - last
    basis = [
        remain * remain * remain / 6.0,
        (3.0 * cube - 6.0 * square + 4.0) / 6.0,
        (-3.0 * cube + 3.0 * square + 3.0 * last + 1.0) / 6.0,
        cube / 6.0,
    ]
    d = k & 3
    cubic = jnp.where(d == 0, basis[0], jnp.where(d == 1, basis[1], jnp.where(d == 2, basis[2], basis[3])))
    return product * cubic


def swap_blocks(x, count, width):
    row, block = iota(x.shape, 0), iota(x.shape, 1) // width
    bit = 1
    while bit < count:
        up = pltpu.roll(pltpu.roll(x, x.shape[0] - bit, 0), bit * width, 1)
        down = pltpu.roll(pltpu.roll(x, bit, 0), LANES - bit * width, 1)
        low_row, low_block = (row & bit) == 0, (block & bit) == 0
        x = jnp.where(low_row == low_block, x, jnp.where(low_row, up, down))
        bit *= 2
    return x


def fill_slots(plan, recv_ref, out_ref):
    p = plan
    table_at, scal_at = lax.axis_index("table"), lax.axis_index("scal")
    part_x = p.nx // 4
    width = LG * part_x
    codes = recv_ref[pl.ds(scal_at * 8 + 7, p.table, stride=8 * p.scal), :].astype(jnp.bfloat16)
    step = LANES
    for h in range(4):
        x = iota((1, width), 1) % part_x + h * part_x
        inside = (iota((1, width), 1) // part_x) * BX + x % BX + GROUP * (table_at % 2)
        move = (iota((LANES, width), 0) == inside).astype(jnp.float32).astype(jnp.bfloat16)
        moved = jnp.dot(codes, move, preferred_element_type=jnp.float32)
        t = x // BX
        moved = jnp.where(iota((p.table, width), 0) == t, moved, 0.0)
        code = jnp.sum(moved, axis=0, keepdims=True).astype(jnp.int32)
        shard, slot = code // p.code, code % p.code
        t = t - h * (p.table // 4)
        near = (shard // 4) * LANES + (shard % 4) * 32 + t * p.near + slot
        quad = shard // 4
        far = (p.table // 4 + quad // 4) * LANES + (quad % 4) * 32
        far = far + t * p.quad + (shard % 4) * p.far + slot - p.near
        chosen = jnp.where(slot < p.near, near, far)
        rows = iota((step, width), 0)
        for start in range(0, out_ref.shape[1], step):
            hit = rows == chosen - start
            out_ref[h, start : start + step, :] = jnp.where(hit, 1.0, 0.0).astype(jnp.bfloat16)


def swap_four(tiles):
    block = iota((1, LANES), 1) // 32
    for bit in (2, 1):
        low = (block & bit) == 0
        turned = [pltpu.roll(tile, 32 * bit, 1) for tile in tiles]
        back = [pltpu.roll(tile, LANES - 32 * bit, 1) for tile in tiles] if bit == 1 else turned
        out = list(tiles)
        for i in range(4):
            if not i & bit:
                out[i] = jnp.where(low, tiles[i], turned[i + bit])
                out[i + bit] = jnp.where(low, back[i], tiles[i + bit])
        tiles = out
    return tiles


def lookup_kernel(
    plan,
    recv_ref,
    early_ref,
    table_in,
    out_ref,
    place_ref,
    table_ref,
    ints_ref,
    field_ref,
    tile_ref,
    sem,
    *rest,
):
    p = plan
    idx_refs, stores = rest[:16], rest[16:]
    quads = p.table // 4
    early = early_ref.shape[0]
    late = table_ref.shape[0] - early
    loads = [
        pltpu.make_async_copy(
            table_in.at[pl.ds(early, late // 2)], table_ref.at[pl.ds(early, late // 2)], sem.at[1]
        ),
        pltpu.make_async_copy(
            table_in.at[pl.ds(early + late // 2, late // 2)],
            table_ref.at[pl.ds(early + late // 2, late // 2)],
            sem.at[2],
        ),
        pltpu.make_async_copy(early_ref, table_ref.at[pl.ds(0, early)], sem.at[3]),
    ]
    loads[0].start()

    def received(r):
        rows = [recv_ref[pl.ds(s * 8 + r, p.table, stride=8 * p.scal), :] for s in range(p.scal)]
        return jnp.concatenate(rows, axis=0)

    addresses = jnp.concatenate([received(4), received(6)], axis=0)
    addresses = swap_blocks(addresses, p.table, p.near)
    order = [addresses[: p.devices]]
    for s in range(p.scal):
        first = p.devices + s * p.table
        order.append(addresses[first : first + quads])
    blank = p.padded - p.chunks
    order.append(jnp.zeros((blank, LANES), jnp.float32))
    order = jnp.concatenate(order, axis=0)
    for first in range(0, p.padded, LANES):
        turned = order[first : first + LANES].T
        ints_ref[:, first : first + LANES] = turned.astype(jnp.int32)
    copies = [
        pltpu.make_async_copy(ints_ref.at[pl.ds(8 * i, 8)], idx_refs[i], sem.at[0])
        for i in range(16)
    ]
    for copy in copies:
        copy.start()
    for load in loads[1:]:
        load.start()
    fields = jnp.concatenate([received(f) for f in (0, 1, 2, 3, 5)], axis=0)
    fields = swap_blocks(fields, p.table, p.near)
    for f in range(4):
        field_ref[f * p.chunks : f * p.chunks + p.devices, :] = fields[
            f * p.devices : (f + 1) * p.devices
        ]
        for s in range(p.scal):
            first = 4 * p.devices + s * p.table + f * quads
            to = f * p.chunks + p.devices + s * quads
            field_ref[to : to + quads, :] = fields[first : first + quads]
    fill_slots(p, recv_ref, place_ref)
    for copy in copies:
        copy.wait()

    def fetch(store, chunk, part):
        step = LANES // p.cols
        for slot in range(part * step, (part + 1) * step):
            address = idx_refs[slot // 8][slot % 8, chunk]
            if p.cols == 1:
                store[slot : slot + 1, :] = table_ref[pl.ds(address, 1), :]
            else:
                store[slot * p.cols : (slot + 1) * p.cols, :] = table_ref[
                    pl.ds(address, p.cols, stride=8), :
                ]

    def reduce(store, chunk, ahead=None):
        weights = spline_rows([field_ref[pl.ds(f * p.chunks + chunk, 1), :] for f in range(4)])
        parts = []
        for c in range(p.cols):
            rows = pl.ds(c, LANES, stride=p.cols) if p.cols > 1 else pl.ds(0, LANES)
            turned = store[rows, :].T
            for m in range(4):
                product = turned[m * K : (m + 1) * K] * weights
                parts.append((product[0:8] + product[8:16]) + (product[16:24] + product[24:32]))
            if ahead is not None:
                ahead(c)
        tile = jnp.sum(jnp.concatenate(parts, axis=0).reshape(p.scalars, 8, LANES), axis=1)
        tile_ref[pl.ds(pl.multiple_of(chunk * p.scalars, p.scalars), p.scalars), :] = tile

    for load in loads:
        load.wait()
    for n in range(BATCH):
        for c in range(p.cols):
            fetch(stores[n], n, c)

    def batch(now, half, more):
        for n in range(BATCH):
            ahead = None
            if more:
                store = stores[(1 - half) * BATCH + n]
                ahead = functools.partial(fetch, store, now + BATCH + n)
            reduce(stores[half * BATCH + n], now + n, ahead)

    def two_batches(i, carry):
        batch(2 * i * BATCH, 0, True)
        batch((2 * i + 1) * BATCH, 1, True)
        return carry

    lax.fori_loop(0, p.chunks // (2 * BATCH) - 1, two_batches, 0)
    batch(p.chunks - 2 * BATCH, 0, True)
    batch(p.chunks - BATCH, 1, False)

    for g in range(p.table):
        for s in range(p.scal):
            dest, chunk = g * p.scal + s, s * p.table + g
            out_ref[dest * p.rows : dest * p.rows + p.scalars, :] = tile_ref[
                chunk * p.scalars : (chunk + 1) * p.scalars, :
            ]
    quad_of = (iota((1, LANES), 1) // p.far) % 4
    for quad in range(quads):
        for s in range(p.scal):
            first = (p.devices + s * quads + quad) * p.scalars
            tile = tile_ref[first : first + p.scalars, :]
            turned = [pltpu.roll(tile, (d * p.far) % LANES, 1) if d else tile for d in range(4)]
            wrapped = [
                pltpu.roll(tile, (-d * p.far) % LANES, 1) if d else tile for d in range(4)
            ]
            for i in range(4):
                message = jnp.zeros((p.few, LANES), jnp.float32)
                for b in range(4):
                    moved = turned[b - i] if b >= i else wrapped[i - b]
                    message = jnp.where(
                        quad_of == b, moved[b * p.few : (b + 1) * p.few], message
                    )
                start = ((quad * 4 + i) * p.scal + s) * p.rows + p.scalars
                out_ref[start : start + p.few, :] = message


def lookup_scratch(plan, table_shape):
    p = plan
    return [
        pltpu.VMEM(table_shape, jnp.float32),
        pltpu.VMEM((LANES, p.padded), jnp.int32),
        pltpu.VMEM((4 * p.chunks, LANES), jnp.float32),
        pltpu.VMEM((p.chunks * p.scalars, LANES), jnp.float32),
        pltpu.SemaphoreType.DMA((4,)),
    ] + [pltpu.SMEM((8, p.padded), jnp.int32)] * 16 + [pltpu.VMEM((p.cols * LANES, LANES), jnp.float32) for _ in range(2 * BATCH)]


def filter_kernel(plan, recv_ref, place_ref, op_ref, filtered_ref, gradient_ref, *left_refs):
    p = plan
    quad_of = (iota((1, LANES), 1) // p.far) % 4

    def put(tiles, first_row, col):
        for left_ref, tile in zip(left_refs, swap_four(tiles), strict=True):
            left_ref[first_row : first_row + tile.shape[0], col : col + LANES] = tile

    for sc in range(p.scal):
        for o in range(0, p.table, 4):
            starts = [((o + i) * p.scal + sc) * p.rows for i in range(4)]
            tiles = [recv_ref[start : start + p.scalars, :] for start in starts]
            put(tiles, sc * p.scalars, o // 4 * LANES)
        for quad in range(0, p.table // 4, 4):
            tiles = []
            for n in range(4):
                starts = [((quad + n) * 4 + i) * p.scal + sc for i in range(4)]
                starts = [start * p.rows + p.scalars for start in starts]
                tile = []
                for b in range(4):
                    part = jnp.zeros((p.few, LANES), jnp.float32)
                    for i in range(4):
                        turned = recv_ref[starts[i] : starts[i] + p.few, :]
                        turned = pltpu.roll(turned, ((i - b) * p.far) % LANES, 1)
                        part = jnp.where(quad_of == i, turned, part)
                    tile.append(part)
                tiles.append(jnp.concatenate(tile, axis=0))
            put(tiles, sc * p.scalars, (p.table // 4 + quad // 4) * LANES)
    sides = []
    for h in range(4):
        left = jnp.concatenate(pieces_of(left_refs[h][...], 3), axis=0)
        values = jnp.dot(left, place_ref[h], preferred_element_type=jnp.float32)
        sides.append(
            values[0:SCAL_ALL] + values[SCAL_ALL : 2 * SCAL_ALL] + values[2 * SCAL_ALL :]
        )
    part_x = p.nx // 4
    if part_x == 32:
        lines = []
        for first in range(0, LG * part_x, LANES):
            lines.extend(swap_four([side[:, first : first + LANES] for side in sides]))
    else:
        lines = [
            jnp.concatenate([side[:, r * part_x : (r + 1) * part_x] for side in sides], axis=1)
            for r in range(LG)
        ]
    lines = jnp.concatenate(lines, axis=0)
    lines, op = pieces_of(lines, 2), pieces_of(op_ref[...], 2)
    both = jnp.dot(
        jnp.concatenate([lines[0], lines[0], lines[1]], axis=1),
        jnp.concatenate([op[0], op[1], op[0]], axis=0),
        preferred_element_type=jnp.float32,
    )
    for r in range(LG):
        rows = slice(r * SCAL_ALL, (r + 1) * SCAL_ALL)
        for part in range(p.nx // LANES):
            at = pl.ds(part * SCAL_ALL * LG + r, SCAL_ALL, stride=LG)
            first = part * LANES
            filtered_ref[at, :] = both[rows, first : first + LANES]
            gradient_ref[at, :] = both[rows, p.nx + first : p.nx + first + LANES]


VMEM = pl.BlockSpec(memory_space=pltpu.VMEM)
SMEM = pl.BlockSpec(memory_space=pltpu.SMEM)
HBM = pl.BlockSpec(memory_space=pltpu.HBM)


def call(kernel, plan, out_shape, in_specs, scratch, limit, cost, name):
    many = isinstance(out_shape, tuple)
    return pl.pallas_call(
        functools.partial(kernel, plan),
        out_shape=out_shape,
        in_specs=in_specs,
        out_specs=(VMEM,) * len(out_shape) if many else VMEM,
        scratch_shapes=scratch,
        compiler_params=pltpu.CompilerParams(vmem_limit_bytes=limit << 20),
        cost_estimate=pl.CostEstimate(flops=cost, bytes_accessed=cost // 256, transcendentals=0),
        name=name,
    )


def exchange(array):
    return lax.all_to_all(array, AXES, split_axis=0, concat_axis=0, tiled=True)


def on_device(plan, cell_coords, flamelet_table, owner_shard, local_bin):
    p = plan
    f32, i32 = jnp.float32, jnp.int32
    row_count = p.cells // LANES
    owners = owner_shard.reshape(row_count, LANES)
    bins = local_bin.reshape(row_count, LANES)
    bin_count, depth = flamelet_table.shape
    table = flamelet_table.reshape(bin_count // 8, 8, p.cols, LANES).transpose(0, 2, 1, 3)
    table = table.reshape(bin_count * p.cols, LANES)
    requests, early = call(
        request_kernel,
        p,
        (
            jax.ShapeDtypeStruct((p.devices, 8, LANES), f32),
            jax.ShapeDtypeStruct((bin_count * p.cols * 11 // 32, LANES), f32),
        ),
        [HBM] * 4,
        [
            pltpu.VMEM((8, p.cells), f32),
            pltpu.VMEM(cell_coords.shape, f32),
            pltpu.VMEM(owners.shape, i32),
            pltpu.VMEM(bins.shape, i32),
            pltpu.SemaphoreType.DMA((4,)),
        ],
        32,
        1 << 20,
        "requests",
    )(*[pltpu.with_memory_space_constraint(a, pltpu.HBM) for a in (cell_coords, owners, bins, table)])
    received = exchange(requests).reshape(p.devices * 8, LANES)
    replies, place = call(
        lookup_kernel,
        p,
        (
            jax.ShapeDtypeStruct((p.devices * p.rows, LANES), f32),
            jax.ShapeDtypeStruct((4, p.table * 5 * LANES // 16, LG * p.nx // 4), jnp.bfloat16),
        ),
        [VMEM, VMEM, HBM],
        lookup_scratch(p, table.shape),
        30,
        1 << 24,
        "lookup",
    )(received, early, pltpu.with_memory_space_constraint(table, pltpu.HBM))
    answers = exchange(replies.reshape(p.devices, 1, p.rows * LANES))
    answers = answers.reshape(p.devices * p.rows, LANES)

    filter_op = filter_table(p.nx).T
    both_op = np.concatenate([filter_op, filter_op @ derivative_table(p.nx).T], axis=1)
    both_op = jnp.asarray(both_op.astype(np.float32))
    out = jax.ShapeDtypeStruct((p.nx // LANES * SCAL_ALL * LG, LANES), f32)
    outs = call(
        filter_kernel,
        p,
        (out, out),
        [VMEM] * 3,
        [pltpu.VMEM((SCAL_ALL, p.table * 5 * LANES // 16), f32)] * 4,
        8 + p.nx * p.table // 64,
        1 << 24,
        "filter",
    )(answers, place, both_op)
    outs = [out.reshape(p.nx // LANES, SCAL_ALL, LG, LANES).transpose(1, 2, 0, 3) for out in outs]
    return tuple(out.reshape(SCAL_ALL, LG, p.nx) for out in outs)


def solution(mesh):
    table, scal = mesh.shape["table"], mesh.shape["scal"]

    def step(cell_coords, flamelet_table, owner_shard, local_bin):
        plan = Plan(table, scal, cell_coords.shape[1])
        return on_device(plan, cell_coords, flamelet_table, owner_shard, local_bin)

    return jax.shard_map(
        step,
        mesh=mesh,
        in_specs=(
            P(None, AXES),
            P("table", "scal"),
            P(AXES, None),
            P(AXES),
        ),
        out_specs=(P(None, AXES, None), P(None, AXES, None)),
        check_vma=False,
    )
```

```python
import functools

import jax
import jax.numpy as jnp
import numpy as np
from jax import lax
from jax.experimental import pallas as pl
from jax.experimental.pallas import tpu as pltpu
from jax.sharding import PartitionSpec as P

SCAL_ALL = 32
K = 32
BX = 8
LG = 8
GROUP = BX * LG
LANES = 128
AXES = ("table", "scal")
BATCH = 4

strength = 0.499


def thomas_solve(below, middle, above, right_side):
    length = middle.shape[0]
    upper_factor = np.zeros(length)
    solved = np.zeros(right_side.shape)
    for row in range(length):
        if row == 0:
            denom = middle[0]
            solved[0] = right_side[0] / denom
        else:
            denom = middle[row] - below[row] * upper_factor[row - 1]
            solved[row] = (right_side[row] - below[row] * solved[row - 1]) / denom
        upper_factor[row] = above[row] / denom
    for row in range(length - 2, -1, -1):
        solved[row] = solved[row] - upper_factor[row] * solved[row + 1]
    return solved


def filter_table(length):
    positions = np.arange(length)
    offset = positions[None, :] - positions[:, None]
    distance = np.abs(offset)
    interior = (positions >= 3) & (positions <= length - 4)
    coeffs = [
        (11.0 + 10.0 * strength) / 16.0,
        (15.0 + 34.0 * strength) / 64.0,
        (-3.0 + 6.0 * strength) / 32.0,
        (1.0 - 2.0 * strength) / 64.0,
    ]
    band = np.zeros((length, length))
    for reach in range(4):
        band = band + np.where(distance == reach, coeffs[reach], 0.0)
    right_side = np.where(interior[:, None], band, np.where(offset == 0, 1.0, 0.0))
    coupling = np.where(interior, strength, 0.0)
    return thomas_solve(coupling, np.ones(length), coupling, right_side)


def derivative_table(length):
    positions = np.arange(length)
    offset = positions[None, :] - positions[:, None]
    distance = np.abs(offset)
    direction = np.sign(offset) * 1.0
    boundary = (positions == 0) | (positions == length - 1)
    second = (positions == 1) | (positions == length - 2)
    interior = ~(boundary | second)
    below_diag = np.where(
        interior, 1.0 / 3.0, np.where(second, 0.25, np.where(positions == length - 1, 2.0, 0.0))
    )
    above_diag = np.where(
        interior, 1.0 / 3.0, np.where(second, 0.25, np.where(positions == 0, 2.0, 0.0))
    )
    inner_rows = direction * (
        np.where(distance == 1, 7.0 / 9.0, 0.0) + np.where(distance == 2, 1.0 / 36.0, 0.0)
    )
    second_rows = direction * np.where(distance == 1, 0.75, 0.0)
    first_row = np.where(
        offset == 0, -2.5, np.where(offset == 1, 2.0, np.where(offset == 2, 0.5, 0.0))
    )
    final_row = np.where(
        offset == 0, 2.5, np.where(offset == -1, -2.0, np.where(offset == -2, -0.5, 0.0))
    )
    right_side = np.where(
        interior[:, None],
        inner_rows,
        np.where(
            second[:, None], second_rows, np.where((positions == 0)[:, None], first_row, final_row)
        ),
    )
    return thomas_solve(below_diag, np.ones(length), above_diag, right_side)


class Plan:
    def __init__(self, table, scal, cells):
        self.table, self.scal, self.cells = table, scal, cells
        self.devices = table * scal
        self.cap = max(2, 5 * GROUP // (2 * table))
        self.near = LANES // table
        self.far = self.cap - self.near
        self.quad = 4 * self.far
        assert cells == table * GROUP and table * self.quad == LANES
        self.code = 1 << (self.cap - 1).bit_length()
        self.scalars = SCAL_ALL // scal
        self.cols = self.scalars * K // LANES
        self.few = self.scalars // 4
        self.rows = self.scalars + self.few
        self.nx = BX * table
        self.chunks = self.devices + self.devices // 4
        self.padded = -(-self.chunks // LANES) * LANES


def iota(shape, dim):
    return lax.broadcasted_iota(jnp.int32, shape, dim)


def pieces_of(values, count):
    pieces = []
    for _ in range(count - 1):
        piece = values.astype(jnp.bfloat16)
        pieces.append(piece)
        values = values - piece.astype(jnp.float32)
    pieces.append(values.astype(jnp.bfloat16))
    return pieces


def dot_rows(a, b):
    return lax.dot_general(a, b, (((1,), (1,)), ((), ())), preferred_element_type=jnp.float32)


def request_kernel(
    plan,
    coords_in,
    owner_in,
    bin_in,
    table_in,
    out_ref,
    early_ref,
    x_ref,
    coords_ref,
    owner_ref,
    bin_ref,
    sem,
):
    p = plan
    row_count = p.cells // LANES
    copies = [
        pltpu.make_async_copy(owner_in, owner_ref, sem.at[0]),
        pltpu.make_async_copy(bin_in, bin_ref, sem.at[1]),
        pltpu.make_async_copy(coords_in, coords_ref, sem.at[2]),
    ]
    early = pltpu.make_async_copy(
        table_in.at[pl.ds(0, early_ref.shape[0])], early_ref, sem.at[3]
    )
    for copy in copies + [early]:
        copy.start()
    for copy in copies:
        copy.wait()
    half = iota((1, LANES), 1) // GROUP
    shard_ids = iota((p.table, LANES), 0)
    owners = owner_ref[...]
    bins = bin_ref[...]
    address = ((bins >> 3) * (8 * p.cols) + (bins & 7)).astype(jnp.float32)
    hits = [owners[i : i + 1, :] == shard_ids for i in range(row_count)]
    before = iota((LANES, LANES), 0)
    after = iota((LANES, LANES), 1)
    earlier = ((before < after) & (before // GROUP == after // GROUP)).astype(jnp.bfloat16)
    ones = jnp.concatenate([h.astype(jnp.float32) for h in hits], axis=0)
    counts = jnp.dot(ones.astype(jnp.bfloat16), earlier, preferred_element_type=jnp.float32)
    x_ref[0:4, :] = coords_ref[...]
    x_ref[5:8, :] = jnp.zeros((3, p.cells), jnp.float32)
    for i in range(row_count):
        x_ref[4:5, i * LANES : (i + 1) * LANES] = address[i : i + 1, :]
    lane_rows = iota((LANES, LANES), 0)
    left, right, codes = [], [], []
    for i in range(row_count):
        span = slice(i * p.table, (i + 1) * p.table)
        rank = jnp.sum(ones[span] * counts[span], axis=0, keepdims=True).astype(jnp.int32)
        codes.append((owners[i : i + 1, :] * p.code + rank).astype(jnp.float32))
        group = 2 * i + half
        near = jnp.where(rank < p.near, group * p.near + rank, -1)
        far = jnp.where(rank >= p.near, group * p.far + rank - p.near, -1)
        right.append(
            jnp.concatenate(
                [
                    (lane_rows == near).astype(jnp.float32),
                    (lane_rows % 32 == far).astype(jnp.float32),
                ],
                axis=0,
            ).astype(jnp.bfloat16)
        )
        fields = x_ref[:, i * LANES : (i + 1) * LANES]
        chosen = []
        for piece in pieces_of(fields, 3):
            piece = jnp.where(hits[i][:, None, :], piece.astype(jnp.float32)[None], 0.0)
            chosen.append(piece.reshape(p.table * 8, LANES).astype(jnp.bfloat16))
        left.append(jnp.concatenate(chosen, axis=0))
    placed = dot_rows(jnp.concatenate(left, axis=1), jnp.concatenate(right, axis=1))
    total = p.table * 8
    placed = placed[0:total] + placed[total : 2 * total] + placed[2 * total :]
    sub = iota((8, LANES), 0)
    block = iota((8, LANES), 1) // 32
    for o in range(p.table):
        near_part = placed[o * 8 : (o + 1) * 8, :LANES]
        far_part = placed[o * 8 : (o + 1) * 8, LANES:]
        far_coords = jnp.sum(jnp.where(sub == block, far_part, 0.0), axis=0, keepdims=True)
        message = jnp.where(
            sub < 5,
            near_part,
            jnp.where(sub == 5, far_coords, jnp.where(sub == 6, far_part[4:5], codes[o // 2])),
        )
        for sc in range(p.scal):
            out_ref[o * p.scal + sc] = message
    early.wait()


def spline_rows(f):
    shape = (K, f[0].shape[1])
    k = iota(shape, 0)
    product = None
    for axis, bit in ((0, 16), (1, 8), (2, 4)):
        factor = jnp.where((k & bit) != 0, f[axis], 1.0 - f[axis])
        product = factor if product is None else product * factor
    last = f[3]
    square = last * last
    cube = square * last
    remain = 1.0 - last
    basis = [
        remain * remain * remain / 6.0,
        (3.0 * cube - 6.0 * square + 4.0) / 6.0,
        (-3.0 * cube + 3.0 * square + 3.0 * last + 1.0) / 6.0,
        cube / 6.0,
    ]
    d = k & 3
    cubic = jnp.where(d == 0, basis[0], jnp.where(d == 1, basis[1], jnp.where(d == 2, basis[2], basis[3])))
    return product * cubic


def swap_blocks(x, count, width):
    row, block = iota(x.shape, 0), iota(x.shape, 1) // width
    bit = 1
    while bit < count:
        up = pltpu.roll(pltpu.roll(x, x.shape[0] - bit, 0), bit * width, 1)
        down = pltpu.roll(pltpu.roll(x, bit, 0), LANES - bit * width, 1)
        low_row, low_block = (row & bit) == 0, (block & bit) == 0
        x = jnp.where(low_row == low_block, x, jnp.where(low_row, up, down))
        bit *= 2
    return x


def fill_slots(plan, recv_ref, out_ref):
    p = plan
    table_at, scal_at = lax.axis_index("table"), lax.axis_index("scal")
    part_x = p.nx // 4
    width = LG * part_x
    codes = recv_ref[pl.ds(scal_at * 8 + 7, p.table, stride=8 * p.scal), :].astype(jnp.bfloat16)
    step = LANES
    for h in range(4):
        x = iota((1, width), 1) % part_x + h * part_x
        inside = (iota((1, width), 1) // part_x) * BX + x % BX + GROUP * (table_at % 2)
        move = (iota((LANES, width), 0) == inside).astype(jnp.float32).astype(jnp.bfloat16)
        moved = jnp.dot(codes, move, preferred_element_type=jnp.float32)
        t = x // BX
        moved = jnp.where(iota((p.table, width), 0) == t, moved, 0.0)
        code = jnp.sum(moved, axis=0, keepdims=True).astype(jnp.int32)
        shard, slot = code // p.code, code % p.code
        t = t - h * (p.table // 4)
        near = (shard // 4) * LANES + (shard % 4) * 32 + t * p.near + slot
        quad = shard // 4
        far = (p.table // 4 + quad // 4) * LANES + (quad % 4) * 32
        far = far + t * p.quad + (shard % 4) * p.far + slot - p.near
        chosen = jnp.where(slot < p.near, near, far)
        rows = iota((step, width), 0)
        for start in range(0, out_ref.shape[1], step):
            hit = rows == chosen - start
            out_ref[h, start : start + step, :] = jnp.where(hit, 1.0, 0.0).astype(jnp.bfloat16)


def swap_four(tiles):
    block = iota((1, LANES), 1) // 32
    for bit in (2, 1):
        low = (block & bit) == 0
        turned = [pltpu.roll(tile, 32 * bit, 1) for tile in tiles]
        back = [pltpu.roll(tile, LANES - 32 * bit, 1) for tile in tiles] if bit == 1 else turned
        out = list(tiles)
        for i in range(4):
            if not i & bit:
                out[i] = jnp.where(low, tiles[i], turned[i + bit])
                out[i + bit] = jnp.where(low, back[i], tiles[i + bit])
        tiles = out
    return tiles


def lookup_kernel(
    plan,
    recv_ref,
    early_ref,
    table_in,
    out_ref,
    place_ref,
    table_ref,
    ints_ref,
    field_ref,
    tile_ref,
    sem,
    *rest,
):
    p = plan
    idx_refs, stores = rest[:16], rest[16:]
    quads = p.table // 4
    early = early_ref.shape[0]
    late = table_ref.shape[0] - early
    loads = [
        pltpu.make_async_copy(
            table_in.at[pl.ds(early, late // 2)], table_ref.at[pl.ds(early, late // 2)], sem.at[1]
        ),
        pltpu.make_async_copy(
            table_in.at[pl.ds(early + late // 2, late // 2)],
            table_ref.at[pl.ds(early + late // 2, late // 2)],
            sem.at[2],
        ),
        pltpu.make_async_copy(early_ref, table_ref.at[pl.ds(0, early)], sem.at[3]),
    ]
    loads[0].start()

    def received(r):
        rows = [recv_ref[pl.ds(s * 8 + r, p.table, stride=8 * p.scal), :] for s in range(p.scal)]
        return jnp.concatenate(rows, axis=0)

    addresses = jnp.concatenate([received(4), received(6)], axis=0)
    addresses = swap_blocks(addresses, p.table, p.near)
    order = [addresses[: p.devices]]
    for s in range(p.scal):
        first = p.devices + s * p.table
        order.append(addresses[first : first + quads])
    blank = p.padded - p.chunks
    order.append(jnp.zeros((blank, LANES), jnp.float32))
    order = jnp.concatenate(order, axis=0)
    for first in range(0, p.padded, LANES):
        turned = order[first : first + LANES].T
        ints_ref[:, first : first + LANES] = turned.astype(jnp.int32)
    copies = [
        pltpu.make_async_copy(ints_ref.at[pl.ds(8 * i, 8)], idx_refs[i], sem.at[0])
        for i in range(16)
    ]
    for copy in copies:
        copy.start()
    for load in loads[1:]:
        load.start()
    fields = jnp.concatenate([received(f) for f in (0, 1, 2, 3, 5)], axis=0)
    fields = swap_blocks(fields, p.table, p.near)
    for f in range(4):
        field_ref[f * p.chunks : f * p.chunks + p.devices, :] = fields[
            f * p.devices : (f + 1) * p.devices
        ]
        for s in range(p.scal):
            first = 4 * p.devices + s * p.table + f * quads
            to = f * p.chunks + p.devices + s * quads
            field_ref[to : to + quads, :] = fields[first : first + quads]
    fill_slots(p, recv_ref, place_ref)
    for copy in copies:
        copy.wait()

    def fetch(store, chunk, part):
        step = LANES // p.cols
        for slot in range(part * step, (part + 1) * step, 2):
            rows = []
            for i in (slot, slot + 1):
                address = idx_refs[i // 8][i % 8, chunk]
                if p.cols == 1:
                    rows.append(table_ref[pl.ds(address, 1), :])
                else:
                    rows.append(table_ref[pl.ds(address, p.cols, stride=8), :])
            store[slot * p.cols : (slot + 2) * p.cols, :] = jnp.concatenate(rows, axis=0)

    def reduce(store, chunk, ahead=None):
        weights = spline_rows([field_ref[pl.ds(f * p.chunks + chunk, 1), :] for f in range(4)])
        parts = []
        for c in range(p.cols):
            rows = pl.ds(c, LANES, stride=p.cols) if p.cols > 1 else pl.ds(0, LANES)
            turned = store[rows, :].T
            for m in range(4):
                product = turned[m * K : (m + 1) * K] * weights
                parts.append((product[0:8] + product[8:16]) + (product[16:24] + product[24:32]))
            if ahead is not None:
                ahead(c)
        tile = jnp.sum(jnp.concatenate(parts, axis=0).reshape(p.scalars, 8, LANES), axis=1)
        tile_ref[pl.ds(pl.multiple_of(chunk * p.scalars, p.scalars), p.scalars), :] = tile

    for load in loads:
        load.wait()
    for n in range(BATCH):
        for c in range(p.cols):
            fetch(stores[n], n, c)

    def batch(now, half, more):
        for n in range(BATCH):
            ahead = None
            if more:
                store = stores[(1 - half) * BATCH + n]
                ahead = functools.partial(fetch, store, now + BATCH + n)
            reduce(stores[half * BATCH + n], now + n, ahead)

    def two_batches(i, carry):
        batch(2 * i * BATCH, 0, True)
        batch((2 * i + 1) * BATCH, 1, True)
        return carry

    lax.fori_loop(0, p.chunks // (2 * BATCH) - 1, two_batches, 0)
    batch(p.chunks - 2 * BATCH, 0, True)
    batch(p.chunks - BATCH, 1, False)

    for g in range(p.table):
        for s in range(p.scal):
            dest, chunk = g * p.scal + s, s * p.table + g
            out_ref[dest * p.rows : dest * p.rows + p.scalars, :] = tile_ref[
                chunk * p.scalars : (chunk + 1) * p.scalars, :
            ]
    quad_of = (iota((1, LANES), 1) // p.far) % 4
    for quad in range(quads):
        for s in range(p.scal):
            first = (p.devices + s * quads + quad) * p.scalars
            tile = tile_ref[first : first + p.scalars, :]
            turned = [pltpu.roll(tile, (d * p.far) % LANES, 1) if d else tile for d in range(4)]
            wrapped = [
                pltpu.roll(tile, (-d * p.far) % LANES, 1) if d else tile for d in range(4)
            ]
            for i in range(4):
                message = jnp.zeros((p.few, LANES), jnp.float32)
                for b in range(4):
                    moved = turned[b - i] if b >= i else wrapped[i - b]
                    message = jnp.where(
                        quad_of == b, moved[b * p.few : (b + 1) * p.few], message
                    )
                start = ((quad * 4 + i) * p.scal + s) * p.rows + p.scalars
                out_ref[start : start + p.few, :] = message


def lookup_scratch(plan, table_shape):
    p = plan
    return [
        pltpu.VMEM(table_shape, jnp.float32),
        pltpu.VMEM((LANES, p.padded), jnp.int32),
        pltpu.VMEM((4 * p.chunks, LANES), jnp.float32),
        pltpu.VMEM((p.chunks * p.scalars, LANES), jnp.float32),
        pltpu.SemaphoreType.DMA((4,)),
    ] + [pltpu.SMEM((8, p.padded), jnp.int32)] * 16 + [pltpu.VMEM((p.cols * LANES, LANES), jnp.float32) for _ in range(2 * BATCH)]


def filter_kernel(plan, recv_ref, place_ref, op_ref, filtered_ref, gradient_ref, *left_refs):
    p = plan
    quad_of = (iota((1, LANES), 1) // p.far) % 4

    def put(tiles, first_row, col):
        for left_ref, tile in zip(left_refs, swap_four(tiles), strict=True):
            left_ref[first_row : first_row + tile.shape[0], col : col + LANES] = tile

    for sc in range(p.scal):
        for o in range(0, p.table, 4):
            starts = [((o + i) * p.scal + sc) * p.rows for i in range(4)]
            tiles = [recv_ref[start : start + p.scalars, :] for start in starts]
            put(tiles, sc * p.scalars, o // 4 * LANES)
        for quad in range(0, p.table // 4, 4):
            tiles = []
            for n in range(4):
                starts = [((quad + n) * 4 + i) * p.scal + sc for i in range(4)]
                starts = [start * p.rows + p.scalars for start in starts]
                tile = []
                for b in range(4):
                    part = jnp.zeros((p.few, LANES), jnp.float32)
                    for i in range(4):
                        turned = recv_ref[starts[i] : starts[i] + p.few, :]
                        turned = pltpu.roll(turned, ((i - b) * p.far) % LANES, 1)
                        part = jnp.where(quad_of == i, turned, part)
                    tile.append(part)
                tiles.append(jnp.concatenate(tile, axis=0))
            put(tiles, sc * p.scalars, (p.table // 4 + quad // 4) * LANES)
    sides = []
    for h in range(4):
        left = jnp.concatenate(pieces_of(left_refs[h][...], 3), axis=0)
        values = jnp.dot(left, place_ref[h], preferred_element_type=jnp.float32)
        sides.append(
            values[0:SCAL_ALL] + values[SCAL_ALL : 2 * SCAL_ALL] + values[2 * SCAL_ALL :]
        )
    part_x = p.nx // 4
    if part_x == 32:
        lines = []
        for first in range(0, LG * part_x, LANES):
            lines.extend(swap_four([side[:, first : first + LANES] for side in sides]))
    else:
        lines = [
            jnp.concatenate([side[:, r * part_x : (r + 1) * part_x] for side in sides], axis=1)
            for r in range(LG)
        ]
    lines = jnp.concatenate(lines, axis=0)
    lines, op = pieces_of(lines, 2), pieces_of(op_ref[...], 2)
    both = jnp.dot(
        jnp.concatenate([lines[0], lines[0], lines[1]], axis=1),
        jnp.concatenate([op[0], op[1], op[0]], axis=0),
        preferred_element_type=jnp.float32,
    )
    for r in range(LG):
        rows = slice(r * SCAL_ALL, (r + 1) * SCAL_ALL)
        for part in range(p.nx // LANES):
            at = pl.ds(part * SCAL_ALL * LG + r, SCAL_ALL, stride=LG)
            first = part * LANES
            filtered_ref[at, :] = both[rows, first : first + LANES]
            gradient_ref[at, :] = both[rows, p.nx + first : p.nx + first + LANES]


VMEM = pl.BlockSpec(memory_space=pltpu.VMEM)
SMEM = pl.BlockSpec(memory_space=pltpu.SMEM)
HBM = pl.BlockSpec(memory_space=pltpu.HBM)


def call(kernel, plan, out_shape, in_specs, scratch, limit, cost, name):
    many = isinstance(out_shape, tuple)
    return pl.pallas_call(
        functools.partial(kernel, plan),
        out_shape=out_shape,
        in_specs=in_specs,
        out_specs=(VMEM,) * len(out_shape) if many else VMEM,
        scratch_shapes=scratch,
        compiler_params=pltpu.CompilerParams(vmem_limit_bytes=limit << 20),
        cost_estimate=pl.CostEstimate(flops=cost, bytes_accessed=cost // 256, transcendentals=0),
        name=name,
    )


def exchange(array):
    return lax.all_to_all(array, AXES, split_axis=0, concat_axis=0, tiled=True)


def on_device(plan, cell_coords, flamelet_table, owner_shard, local_bin):
    p = plan
    f32, i32 = jnp.float32, jnp.int32
    row_count = p.cells // LANES
    owners = owner_shard.reshape(row_count, LANES)
    bins = local_bin.reshape(row_count, LANES)
    bin_count, depth = flamelet_table.shape
    table = flamelet_table.reshape(bin_count // 8, 8, p.cols, LANES).transpose(0, 2, 1, 3)
    table = table.reshape(bin_count * p.cols, LANES)
    requests, early = call(
        request_kernel,
        p,
        (
            jax.ShapeDtypeStruct((p.devices, 8, LANES), f32),
            jax.ShapeDtypeStruct((bin_count * p.cols * 11 // 32, LANES), f32),
        ),
        [HBM] * 4,
        [
            pltpu.VMEM((8, p.cells), f32),
            pltpu.VMEM(cell_coords.shape, f32),
            pltpu.VMEM(owners.shape, i32),
            pltpu.VMEM(bins.shape, i32),
            pltpu.SemaphoreType.DMA((4,)),
        ],
        32,
        1 << 20,
        "requests",
    )(*[pltpu.with_memory_space_constraint(a, pltpu.HBM) for a in (cell_coords, owners, bins, table)])
    received = exchange(requests).reshape(p.devices * 8, LANES)
    replies, place = call(
        lookup_kernel,
        p,
        (
            jax.ShapeDtypeStruct((p.devices * p.rows, LANES), f32),
            jax.ShapeDtypeStruct((4, p.table * 5 * LANES // 16, LG * p.nx // 4), jnp.bfloat16),
        ),
        [VMEM, VMEM, HBM],
        lookup_scratch(p, table.shape),
        30,
        1 << 24,
        "lookup",
    )(received, early, pltpu.with_memory_space_constraint(table, pltpu.HBM))
    answers = exchange(replies.reshape(p.devices, 1, p.rows * LANES))
    answers = answers.reshape(p.devices * p.rows, LANES)

    filter_op = filter_table(p.nx).T
    both_op = np.concatenate([filter_op, filter_op @ derivative_table(p.nx).T], axis=1)
    both_op = jnp.asarray(both_op.astype(np.float32))
    out = jax.ShapeDtypeStruct((p.nx // LANES * SCAL_ALL * LG, LANES), f32)
    outs = call(
        filter_kernel,
        p,
        (out, out),
        [VMEM] * 3,
        [pltpu.VMEM((SCAL_ALL, p.table * 5 * LANES // 16), f32)] * 4,
        8 + p.nx * p.table // 64,
        1 << 24,
        "filter",
    )(answers, place, both_op)
    outs = [out.reshape(p.nx // LANES, SCAL_ALL, LG, LANES).transpose(1, 2, 0, 3) for out in outs]
    return tuple(out.reshape(SCAL_ALL, LG, p.nx) for out in outs)


def solution(mesh):
    table, scal = mesh.shape["table"], mesh.shape["scal"]

    def step(cell_coords, flamelet_table, owner_shard, local_bin):
        plan = Plan(table, scal, cell_coords.shape[1])
        return on_device(plan, cell_coords, flamelet_table, owner_shard, local_bin)

    return jax.shard_map(
        step,
        mesh=mesh,
        in_specs=(
            P(None, AXES),
            P("table", "scal"),
            P(AXES, None),
            P(AXES),
        ),
        out_specs=(P(None, AXES, None), P(None, AXES, None)),
        check_vma=False,
    )
```

```python
import functools

import jax
import jax.numpy as jnp
import numpy as np
from jax import lax
from jax.experimental import pallas as pl
from jax.experimental.pallas import tpu as pltpu
from jax.sharding import PartitionSpec as P

SCAL_ALL = 32
K = 32
BX = 8
LG = 8
GROUP = BX * LG
LANES = 128
AXES = ("table", "scal")
BATCH = 4
SENT = 7

strength = 0.499


def thomas_solve(below, middle, above, right_side):
    length = middle.shape[0]
    upper_factor = np.zeros(length)
    solved = np.zeros(right_side.shape)
    for row in range(length):
        if row == 0:
            denom = middle[0]
            solved[0] = right_side[0] / denom
        else:
            denom = middle[row] - below[row] * upper_factor[row - 1]
            solved[row] = (right_side[row] - below[row] * solved[row - 1]) / denom
        upper_factor[row] = above[row] / denom
    for row in range(length - 2, -1, -1):
        solved[row] = solved[row] - upper_factor[row] * solved[row + 1]
    return solved


def filter_table(length):
    positions = np.arange(length)
    offset = positions[None, :] - positions[:, None]
    distance = np.abs(offset)
    interior = (positions >= 3) & (positions <= length - 4)
    coeffs = [
        (11.0 + 10.0 * strength) / 16.0,
        (15.0 + 34.0 * strength) / 64.0,
        (-3.0 + 6.0 * strength) / 32.0,
        (1.0 - 2.0 * strength) / 64.0,
    ]
    band = np.zeros((length, length))
    for reach in range(4):
        band = band + np.where(distance == reach, coeffs[reach], 0.0)
    right_side = np.where(interior[:, None], band, np.where(offset == 0, 1.0, 0.0))
    coupling = np.where(interior, strength, 0.0)
    return thomas_solve(coupling, np.ones(length), coupling, right_side)


def derivative_table(length):
    positions = np.arange(length)
    offset = positions[None, :] - positions[:, None]
    distance = np.abs(offset)
    direction = np.sign(offset) * 1.0
    boundary = (positions == 0) | (positions == length - 1)
    second = (positions == 1) | (positions == length - 2)
    interior = ~(boundary | second)
    below_diag = np.where(
        interior, 1.0 / 3.0, np.where(second, 0.25, np.where(positions == length - 1, 2.0, 0.0))
    )
    above_diag = np.where(
        interior, 1.0 / 3.0, np.where(second, 0.25, np.where(positions == 0, 2.0, 0.0))
    )
    inner_rows = direction * (
        np.where(distance == 1, 7.0 / 9.0, 0.0) + np.where(distance == 2, 1.0 / 36.0, 0.0)
    )
    second_rows = direction * np.where(distance == 1, 0.75, 0.0)
    first_row = np.where(
        offset == 0, -2.5, np.where(offset == 1, 2.0, np.where(offset == 2, 0.5, 0.0))
    )
    final_row = np.where(
        offset == 0, 2.5, np.where(offset == -1, -2.0, np.where(offset == -2, -0.5, 0.0))
    )
    right_side = np.where(
        interior[:, None],
        inner_rows,
        np.where(
            second[:, None], second_rows, np.where((positions == 0)[:, None], first_row, final_row)
        ),
    )
    return thomas_solve(below_diag, np.ones(length), above_diag, right_side)


class Plan:
    def __init__(self, table, scal, cells):
        self.table, self.scal, self.cells = table, scal, cells
        self.devices = table * scal
        self.cap = max(2, 5 * GROUP // (2 * table))
        self.near = LANES // table
        self.far = self.cap - self.near
        self.quad = 4 * self.far
        assert cells == table * GROUP and table * self.quad == LANES
        self.code = 1 << (self.cap - 1).bit_length()
        self.scalars = SCAL_ALL // scal
        self.cols = self.scalars * K // LANES
        self.few = self.scalars // 4
        self.rows = self.scalars + self.few
        self.nx = BX * table
        self.chunks = self.devices + self.devices // 4
        self.padded = -(-self.chunks // LANES) * LANES


def iota(shape, dim):
    return lax.broadcasted_iota(jnp.int32, shape, dim)


def pieces_of(values, count):
    pieces = []
    for _ in range(count - 1):
        piece = values.astype(jnp.bfloat16)
        pieces.append(piece)
        values = values - piece.astype(jnp.float32)
    pieces.append(values.astype(jnp.bfloat16))
    return pieces


def dot_rows(a, b):
    return lax.dot_general(a, b, (((1,), (1,)), ((), ())), preferred_element_type=jnp.float32)


def request_kernel(
    plan,
    coords_in,
    owner_in,
    bin_in,
    table_in,
    out_ref,
    early_ref,
    x_ref,
    coords_ref,
    owner_ref,
    bin_ref,
    sem,
):
    p = plan
    row_count = p.cells // LANES
    copies = [
        pltpu.make_async_copy(owner_in, owner_ref, sem.at[0]),
        pltpu.make_async_copy(bin_in, bin_ref, sem.at[1]),
        pltpu.make_async_copy(coords_in, coords_ref, sem.at[2]),
    ]
    early = pltpu.make_async_copy(
        table_in.at[pl.ds(0, early_ref.shape[0])], early_ref, sem.at[3]
    )
    for copy in copies + [early]:
        copy.start()
    for copy in copies:
        copy.wait()
    half = iota((1, LANES), 1) // GROUP
    shard_ids = iota((p.table, LANES), 0)
    owners = owner_ref[...]
    bins = bin_ref[...]
    address = ((bins >> 3) * (8 * p.cols) + (bins & 7)).astype(jnp.float32)
    hits = [owners[i : i + 1, :] == shard_ids for i in range(row_count)]
    before = iota((LANES, LANES), 0)
    after = iota((LANES, LANES), 1)
    earlier = ((before < after) & (before // GROUP == after // GROUP)).astype(jnp.bfloat16)
    ones = jnp.concatenate([h.astype(jnp.float32) for h in hits], axis=0)
    counts = jnp.dot(ones.astype(jnp.bfloat16), earlier, preferred_element_type=jnp.float32)
    x_ref[0:4, :] = coords_ref[...]
    x_ref[5:8, :] = jnp.zeros((3, p.cells), jnp.float32)
    for i in range(row_count):
        x_ref[4:5, i * LANES : (i + 1) * LANES] = address[i : i + 1, :]
    lane_rows = iota((LANES, LANES), 0)
    left, right, codes = [], [], []
    for i in range(row_count):
        span = slice(i * p.table, (i + 1) * p.table)
        rank = jnp.sum(ones[span] * counts[span], axis=0, keepdims=True).astype(jnp.int32)
        codes.append((owners[i : i + 1, :] * p.code + rank).astype(jnp.float32))
        group = 2 * i + half
        near = jnp.where(rank < p.near, group * p.near + rank, -1)
        far = jnp.where(rank >= p.near, group * p.far + rank - p.near, -1)
        right.append(
            jnp.concatenate(
                [
                    (lane_rows == near).astype(jnp.float32),
                    (lane_rows % 32 == far).astype(jnp.float32),
                ],
                axis=0,
            ).astype(jnp.bfloat16)
        )
        fields = x_ref[:, i * LANES : (i + 1) * LANES]
        chosen = []
        for piece in pieces_of(fields, 3):
            piece = jnp.where(hits[i][:, None, :], piece.astype(jnp.float32)[None], 0.0)
            chosen.append(piece.reshape(p.table * 8, LANES).astype(jnp.bfloat16))
        left.append(jnp.concatenate(chosen, axis=0))
    placed = dot_rows(jnp.concatenate(left, axis=1), jnp.concatenate(right, axis=1))
    total = p.table * 8
    placed = placed[0:total] + placed[total : 2 * total] + placed[2 * total :]
    sub = iota((8, LANES), 0)
    block = iota((8, LANES), 1) // 32
    upper = iota((1, LANES), 1) >= GROUP
    for o in range(p.table):
        near_part = placed[o * 8 : (o + 1) * 8, :LANES]
        far_part = placed[o * 8 : (o + 1) * 8, LANES:]
        far_coords = jnp.sum(jnp.where(sub == block, far_part, 0.0), axis=0, keepdims=True)
        code = codes[o // 2] if o % 2 else pltpu.roll(codes[o // 2], GROUP, 1)
        message = jnp.where(
            sub < 5,
            near_part,
            jnp.where(sub == 5, far_coords, jnp.where(upper, code, far_part[4:5])),
        )
        for sc in range(p.scal):
            start = (o * p.scal + sc) * SENT
            out_ref[start : start + SENT, :] = message[:SENT]
    early.wait()


def spline_rows(f):
    shape = (K, f[0].shape[1])
    k = iota(shape, 0)
    product = None
    for axis, bit in ((0, 16), (1, 8), (2, 4)):
        factor = jnp.where((k & bit) != 0, f[axis], 1.0 - f[axis])
        product = factor if product is None else product * factor
    last = f[3]
    square = last * last
    cube = square * last
    remain = 1.0 - last
    basis = [
        remain * remain * remain / 6.0,
        (3.0 * cube - 6.0 * square + 4.0) / 6.0,
        (-3.0 * cube + 3.0 * square + 3.0 * last + 1.0) / 6.0,
        cube / 6.0,
    ]
    d = k & 3
    cubic = jnp.where(d == 0, basis[0], jnp.where(d == 1, basis[1], jnp.where(d == 2, basis[2], basis[3])))
    return product * cubic


def swap_blocks(x, count, width):
    row, block = iota(x.shape, 0), iota(x.shape, 1) // width
    bit = 1
    while bit < count:
        up = pltpu.roll(pltpu.roll(x, x.shape[0] - bit, 0), bit * width, 1)
        down = pltpu.roll(pltpu.roll(x, bit, 0), LANES - bit * width, 1)
        low_row, low_block = (row & bit) == 0, (block & bit) == 0
        x = jnp.where(low_row == low_block, x, jnp.where(low_row, up, down))
        bit *= 2
    return x


def fill_slots(plan, recv_ref, out_ref):
    p = plan
    scal_at = lax.axis_index("scal")
    part_x = p.nx // 4
    width = LG * part_x
    codes = jnp.zeros((p.table, LANES), jnp.float32)
    for s in range(p.scal):
        rows = recv_ref[pl.ds(s * SENT + 6, p.table, stride=SENT * p.scal), :]
        codes = jnp.where(scal_at == s, rows, codes)
    codes = codes.astype(jnp.bfloat16)
    step = LANES
    for h in range(4):
        x = iota((1, width), 1) % part_x + h * part_x
        inside = (iota((1, width), 1) // part_x) * BX + x % BX + GROUP
        move = (iota((LANES, width), 0) == inside).astype(jnp.float32).astype(jnp.bfloat16)
        moved = jnp.dot(codes, move, preferred_element_type=jnp.float32)
        t = x // BX
        moved = jnp.where(iota((p.table, width), 0) == t, moved, 0.0)
        code = jnp.sum(moved, axis=0, keepdims=True).astype(jnp.int32)
        shard, slot = code // p.code, code % p.code
        t = t - h * (p.table // 4)
        near = (shard // 4) * LANES + (shard % 4) * 32 + t * p.near + slot
        quad = shard // 4
        far = (p.table // 4 + quad // 4) * LANES + (quad % 4) * 32
        far = far + t * p.quad + (shard % 4) * p.far + slot - p.near
        chosen = jnp.where(slot < p.near, near, far)
        rows = iota((step, width), 0)
        for start in range(0, out_ref.shape[1], step):
            hit = rows == chosen - start
            out_ref[h, start : start + step, :] = jnp.where(hit, 1.0, 0.0).astype(jnp.bfloat16)


def swap_four(tiles):
    block = iota((1, LANES), 1) // 32
    for bit in (2, 1):
        low = (block & bit) == 0
        turned = [pltpu.roll(tile, 32 * bit, 1) for tile in tiles]
        back = [pltpu.roll(tile, LANES - 32 * bit, 1) for tile in tiles] if bit == 1 else turned
        out = list(tiles)
        for i in range(4):
            if not i & bit:
                out[i] = jnp.where(low, tiles[i], turned[i + bit])
                out[i + bit] = jnp.where(low, back[i], tiles[i + bit])
        tiles = out
    return tiles


def lookup_kernel(
    plan,
    recv_ref,
    early_ref,
    table_in,
    out_ref,
    place_ref,
    table_ref,
    ints_ref,
    field_ref,
    tile_ref,
    sem,
    *rest,
):
    p = plan
    idx_refs, stores = rest[:16], rest[16:]
    quads = p.table // 4
    early = early_ref.shape[0]
    late = table_in.shape[0] - early
    loads = [
        pltpu.make_async_copy(
            table_in.at[pl.ds(early, late // 2)], table_ref.at[pl.ds(early, late // 2)], sem.at[1]
        ),
        pltpu.make_async_copy(
            table_in.at[pl.ds(early + late // 2, late // 2)],
            table_ref.at[pl.ds(early + late // 2, late // 2)],
            sem.at[2],
        ),
        pltpu.make_async_copy(early_ref, table_ref.at[pl.ds(0, early)], sem.at[3]),
    ]
    loads[0].start()

    def received(r):
        rows = [recv_ref[pl.ds(s * SENT + r, p.table, stride=SENT * p.scal), :] for s in range(p.scal)]
        return jnp.concatenate(rows, axis=0)

    addresses = jnp.concatenate([received(4), received(6)], axis=0)
    addresses = swap_blocks(addresses, p.table, p.near)
    order = [addresses[: p.devices]]
    for s in range(p.scal):
        first = p.devices + s * p.table
        order.append(addresses[first : first + quads])
    blank = p.padded - p.chunks
    order.append(jnp.zeros((blank, LANES), jnp.float32))
    order = jnp.concatenate(order, axis=0)
    for first in range(0, p.padded, LANES):
        turned = order[first : first + LANES].T
        ints_ref[:, first : first + LANES] = turned.astype(jnp.int32)
    copies = [
        pltpu.make_async_copy(ints_ref.at[pl.ds(8 * i, 8)], idx_refs[i], sem.at[0])
        for i in range(16)
    ]
    for copy in copies:
        copy.start()
    for load in loads[1:]:
        load.start()
    fields = jnp.concatenate([received(f) for f in (0, 1, 2, 3, 5)], axis=0)
    fields = swap_blocks(fields, p.table, p.near)
    for f in range(4):
        field_ref[f * p.chunks : f * p.chunks + p.devices, :] = fields[
            f * p.devices : (f + 1) * p.devices
        ]
        for s in range(p.scal):
            first = 4 * p.devices + s * p.table + f * quads
            to = f * p.chunks + p.devices + s * quads
            field_ref[to : to + quads, :] = fields[first : first + quads]
    fill_slots(p, recv_ref, place_ref)
    for copy in copies:
        copy.wait()

    def fetch(store, chunk, part):
        step = LANES // p.cols
        for slot in range(part * step, (part + 1) * step, 2):
            rows = []
            for i in (slot, slot + 1):
                address = idx_refs[i // 8][i % 8, chunk]
                if p.cols == 1:
                    rows.append(table_ref[pl.ds(address, 1), :])
                else:
                    rows.append(table_ref[pl.ds(address, p.cols, stride=8), :])
            store[slot * p.cols : (slot + 2) * p.cols, :] = jnp.concatenate(rows, axis=0)

    def reduce(store, chunk, ahead=None):
        weights = spline_rows([field_ref[pl.ds(f * p.chunks + chunk, 1), :] for f in range(4)])
        parts = []
        for c in range(p.cols):
            rows = pl.ds(c, LANES, stride=p.cols) if p.cols > 1 else pl.ds(0, LANES)
            turned = store[rows, :].T
            for m in range(4):
                product = turned[m * K : (m + 1) * K] * weights
                parts.append((product[0:8] + product[8:16]) + (product[16:24] + product[24:32]))
            if ahead is not None:
                ahead(c)
        tile = jnp.sum(jnp.concatenate(parts, axis=0).reshape(p.scalars, 8, LANES), axis=1)
        tile_ref[pl.ds(pl.multiple_of(chunk * p.scalars, p.scalars), p.scalars), :] = tile

    for load in loads:
        load.wait()
    for n in range(BATCH):
        for c in range(p.cols):
            fetch(stores[n], n, c)

    def batch(now, half, more):
        for n in range(BATCH):
            ahead = None
            if more:
                store = stores[(1 - half) * BATCH + n]
                ahead = functools.partial(fetch, store, now + BATCH + n)
            reduce(stores[half * BATCH + n], now + n, ahead)

    def two_batches(i, carry):
        batch(2 * i * BATCH, 0, True)
        batch((2 * i + 1) * BATCH, 1, True)
        return carry

    lax.fori_loop(0, p.chunks // (2 * BATCH) - 1, two_batches, 0)
    batch(p.chunks - 2 * BATCH, 0, True)
    batch(p.chunks - BATCH, 1, False)

    for g in range(p.table):
        for s in range(p.scal):
            dest, chunk = g * p.scal + s, s * p.table + g
            out_ref[dest * p.rows : dest * p.rows + p.scalars, :] = tile_ref[
                chunk * p.scalars : (chunk + 1) * p.scalars, :
            ]
    quad_of = (iota((1, LANES), 1) // p.far) % 4
    for quad in range(quads):
        for s in range(p.scal):
            first = (p.devices + s * quads + quad) * p.scalars
            tile = tile_ref[first : first + p.scalars, :]
            turned = [pltpu.roll(tile, (d * p.far) % LANES, 1) if d else tile for d in range(4)]
            wrapped = [
                pltpu.roll(tile, (-d * p.far) % LANES, 1) if d else tile for d in range(4)
            ]
            for i in range(4):
                message = jnp.zeros((p.few, LANES), jnp.float32)
                for b in range(4):
                    moved = turned[b - i] if b >= i else wrapped[i - b]
                    message = jnp.where(
                        quad_of == b, moved[b * p.few : (b + 1) * p.few], message
                    )
                start = ((quad * 4 + i) * p.scal + s) * p.rows + p.scalars
                out_ref[start : start + p.few, :] = message


def lookup_scratch(plan, table_shape):
    p = plan
    return [
        pltpu.VMEM((table_shape[0] + 8 * p.cols, LANES), jnp.float32),
        pltpu.VMEM((LANES, p.padded), jnp.int32),
        pltpu.VMEM((4 * p.chunks, LANES), jnp.float32),
        pltpu.VMEM((p.chunks * p.scalars, LANES), jnp.float32),
        pltpu.SemaphoreType.DMA((4,)),
    ] + [pltpu.SMEM((8, p.padded), jnp.int32)] * 16 + [pltpu.VMEM((p.cols * LANES, LANES), jnp.float32) for _ in range(2 * BATCH)]


def filter_kernel(plan, recv_ref, place_ref, op_ref, filtered_ref, gradient_ref, *left_refs):
    p = plan
    quad_of = (iota((1, LANES), 1) // p.far) % 4

    def put(tiles, first_row, col):
        for left_ref, tile in zip(left_refs, swap_four(tiles), strict=True):
            left_ref[first_row : first_row + tile.shape[0], col : col + LANES] = tile

    for sc in range(p.scal):
        for o in range(0, p.table, 4):
            starts = [((o + i) * p.scal + sc) * p.rows for i in range(4)]
            tiles = [recv_ref[start : start + p.scalars, :] for start in starts]
            put(tiles, sc * p.scalars, o // 4 * LANES)
        for quad in range(0, p.table // 4, 4):
            tiles = []
            for n in range(4):
                starts = [((quad + n) * 4 + i) * p.scal + sc for i in range(4)]
                starts = [start * p.rows + p.scalars for start in starts]
                tile = []
                for b in range(4):
                    part = jnp.zeros((p.few, LANES), jnp.float32)
                    for i in range(4):
                        turned = recv_ref[starts[i] : starts[i] + p.few, :]
                        turned = pltpu.roll(turned, ((i - b) * p.far) % LANES, 1)
                        part = jnp.where(quad_of == i, turned, part)
                    tile.append(part)
                tiles.append(jnp.concatenate(tile, axis=0))
            put(tiles, sc * p.scalars, (p.table // 4 + quad // 4) * LANES)
    sides = []
    for h in range(4):
        left = jnp.concatenate(pieces_of(left_refs[h][...], 3), axis=0)
        values = jnp.dot(left, place_ref[h], preferred_element_type=jnp.float32)
        sides.append(
            values[0:SCAL_ALL] + values[SCAL_ALL : 2 * SCAL_ALL] + values[2 * SCAL_ALL :]
        )
    part_x = p.nx // 4
    if part_x == 32:
        lines = []
        for first in range(0, LG * part_x, LANES):
            lines.extend(swap_four([side[:, first : first + LANES] for side in sides]))
    else:
        lines = [
            jnp.concatenate([side[:, r * part_x : (r + 1) * part_x] for side in sides], axis=1)
            for r in range(LG)
        ]
    lines = jnp.concatenate(lines, axis=0)
    lines, op = pieces_of(lines, 2), pieces_of(op_ref[...], 2)
    both = jnp.dot(
        jnp.concatenate([lines[0], lines[0], lines[1]], axis=1),
        jnp.concatenate([op[0], op[1], op[0]], axis=0),
        preferred_element_type=jnp.float32,
    )
    for r in range(LG):
        rows = slice(r * SCAL_ALL, (r + 1) * SCAL_ALL)
        for part in range(p.nx // LANES):
            at = pl.ds(part * SCAL_ALL * LG + r, SCAL_ALL, stride=LG)
            first = part * LANES
            filtered_ref[at, :] = both[rows, first : first + LANES]
            gradient_ref[at, :] = both[rows, p.nx + first : p.nx + first + LANES]


VMEM = pl.BlockSpec(memory_space=pltpu.VMEM)
SMEM = pl.BlockSpec(memory_space=pltpu.SMEM)
HBM = pl.BlockSpec(memory_space=pltpu.HBM)


def call(kernel, plan, out_shape, in_specs, scratch, limit, cost, name):
    many = isinstance(out_shape, tuple)
    return pl.pallas_call(
        functools.partial(kernel, plan),
        out_shape=out_shape,
        in_specs=in_specs,
        out_specs=(VMEM,) * len(out_shape) if many else VMEM,
        scratch_shapes=scratch,
        compiler_params=pltpu.CompilerParams(vmem_limit_bytes=limit << 20),
        cost_estimate=pl.CostEstimate(flops=cost, bytes_accessed=cost // 256, transcendentals=0),
        name=name,
    )


def exchange(array):
    return lax.all_to_all(array, AXES, split_axis=0, concat_axis=0, tiled=True)


def on_device(plan, cell_coords, flamelet_table, owner_shard, local_bin):
    p = plan
    f32, i32 = jnp.float32, jnp.int32
    row_count = p.cells // LANES
    owners = owner_shard.reshape(row_count, LANES)
    bins = local_bin.reshape(row_count, LANES)
    bin_count, depth = flamelet_table.shape
    table = flamelet_table.reshape(bin_count // 8, 8, p.cols, LANES).transpose(0, 2, 1, 3)
    table = table.reshape(bin_count * p.cols, LANES)
    requests, early = call(
        request_kernel,
        p,
        (
            jax.ShapeDtypeStruct((p.devices * SENT, LANES), f32),
            jax.ShapeDtypeStruct((bin_count * p.cols * 11 // 32, LANES), f32),
        ),
        [HBM] * 4,
        [
            pltpu.VMEM((8, p.cells), f32),
            pltpu.VMEM(cell_coords.shape, f32),
            pltpu.VMEM(owners.shape, i32),
            pltpu.VMEM(bins.shape, i32),
            pltpu.SemaphoreType.DMA((4,)),
        ],
        32,
        1 << 20,
        "requests",
    )(*[pltpu.with_memory_space_constraint(a, pltpu.HBM) for a in (cell_coords, owners, bins, table)])
    received = exchange(requests.reshape(p.devices, 1, SENT * LANES))
    received = received.reshape(p.devices * SENT, LANES)
    replies, place = call(
        lookup_kernel,
        p,
        (
            jax.ShapeDtypeStruct((p.devices * p.rows, LANES), f32),
            jax.ShapeDtypeStruct((4, p.table * 5 * LANES // 16, LG * p.nx // 4), jnp.bfloat16),
        ),
        [VMEM, VMEM, HBM],
        lookup_scratch(p, table.shape),
        30,
        1 << 24,
        "lookup",
    )(received, early, pltpu.with_memory_space_constraint(table, pltpu.HBM))
    answers = exchange(replies.reshape(p.devices, 1, p.rows * LANES))
    answers = answers.reshape(p.devices * p.rows, LANES)

    filter_op = filter_table(p.nx).T
    both_op = np.concatenate([filter_op, filter_op @ derivative_table(p.nx).T], axis=1)
    both_op = jnp.asarray(both_op.astype(np.float32))
    out = jax.ShapeDtypeStruct((p.nx // LANES * SCAL_ALL * LG, LANES), f32)
    outs = call(
        filter_kernel,
        p,
        (out, out),
        [VMEM] * 3,
        [pltpu.VMEM((SCAL_ALL, p.table * 5 * LANES // 16), f32)] * 4,
        8 + p.nx * p.table // 64,
        1 << 24,
        "filter",
    )(answers, place, both_op)
    outs = [out.reshape(p.nx // LANES, SCAL_ALL, LG, LANES).transpose(1, 2, 0, 3) for out in outs]
    return tuple(out.reshape(SCAL_ALL, LG, p.nx) for out in outs)


def solution(mesh):
    table, scal = mesh.shape["table"], mesh.shape["scal"]

    def step(cell_coords, flamelet_table, owner_shard, local_bin):
        plan = Plan(table, scal, cell_coords.shape[1])
        return on_device(plan, cell_coords, flamelet_table, owner_shard, local_bin)

    return jax.shard_map(
        step,
        mesh=mesh,
        in_specs=(
            P(None, AXES),
            P("table", "scal"),
            P(AXES, None),
            P(AXES),
        ),
        out_specs=(P(None, AXES, None), P(None, AXES, None)),
        check_vma=False,
    )
```

```python
import functools

import jax
import jax.numpy as jnp
import numpy as np
from jax import lax
from jax.experimental import pallas as pl
from jax.experimental.pallas import tpu as pltpu
from jax.sharding import PartitionSpec as P

SCAL_ALL = 32
K = 32
BX = 8
LG = 8
GROUP = BX * LG
LANES = 128
AXES = ("table", "scal")
BATCH = 4
SENT = 7

strength = 0.499


def thomas_solve(below, middle, above, right_side):
    length = middle.shape[0]
    upper_factor = np.zeros(length)
    solved = np.zeros(right_side.shape)
    for row in range(length):
        if row == 0:
            denom = middle[0]
            solved[0] = right_side[0] / denom
        else:
            denom = middle[row] - below[row] * upper_factor[row - 1]
            solved[row] = (right_side[row] - below[row] * solved[row - 1]) / denom
        upper_factor[row] = above[row] / denom
    for row in range(length - 2, -1, -1):
        solved[row] = solved[row] - upper_factor[row] * solved[row + 1]
    return solved


def filter_table(length):
    positions = np.arange(length)
    offset = positions[None, :] - positions[:, None]
    distance = np.abs(offset)
    interior = (positions >= 3) & (positions <= length - 4)
    coeffs = [
        (11.0 + 10.0 * strength) / 16.0,
        (15.0 + 34.0 * strength) / 64.0,
        (-3.0 + 6.0 * strength) / 32.0,
        (1.0 - 2.0 * strength) / 64.0,
    ]
    band = np.zeros((length, length))
    for reach in range(4):
        band = band + np.where(distance == reach, coeffs[reach], 0.0)
    right_side = np.where(interior[:, None], band, np.where(offset == 0, 1.0, 0.0))
    coupling = np.where(interior, strength, 0.0)
    return thomas_solve(coupling, np.ones(length), coupling, right_side)


def derivative_table(length):
    positions = np.arange(length)
    offset = positions[None, :] - positions[:, None]
    distance = np.abs(offset)
    direction = np.sign(offset) * 1.0
    boundary = (positions == 0) | (positions == length - 1)
    second = (positions == 1) | (positions == length - 2)
    interior = ~(boundary | second)
    below_diag = np.where(
        interior, 1.0 / 3.0, np.where(second, 0.25, np.where(positions == length - 1, 2.0, 0.0))
    )
    above_diag = np.where(
        interior, 1.0 / 3.0, np.where(second, 0.25, np.where(positions == 0, 2.0, 0.0))
    )
    inner_rows = direction * (
        np.where(distance == 1, 7.0 / 9.0, 0.0) + np.where(distance == 2, 1.0 / 36.0, 0.0)
    )
    second_rows = direction * np.where(distance == 1, 0.75, 0.0)
    first_row = np.where(
        offset == 0, -2.5, np.where(offset == 1, 2.0, np.where(offset == 2, 0.5, 0.0))
    )
    final_row = np.where(
        offset == 0, 2.5, np.where(offset == -1, -2.0, np.where(offset == -2, -0.5, 0.0))
    )
    right_side = np.where(
        interior[:, None],
        inner_rows,
        np.where(
            second[:, None], second_rows, np.where((positions == 0)[:, None], first_row, final_row)
        ),
    )
    return thomas_solve(below_diag, np.ones(length), above_diag, right_side)


class Plan:
    def __init__(self, table, scal, cells):
        self.table, self.scal, self.cells = table, scal, cells
        self.devices = table * scal
        self.cap = max(2, 5 * GROUP // (2 * table))
        self.near = LANES // table
        self.far = self.cap - self.near
        self.quad = 4 * self.far
        assert cells == table * GROUP and table * self.quad == LANES
        self.code = 1 << (self.cap - 1).bit_length()
        self.scalars = SCAL_ALL // scal
        self.cols = self.scalars * K // LANES
        self.few = self.scalars // 4
        self.rows = self.scalars + self.few
        self.nx = BX * table
        self.chunks = self.devices + self.devices // 4
        self.padded = -(-self.chunks // LANES) * LANES


def iota(shape, dim):
    return lax.broadcasted_iota(jnp.int32, shape, dim)


def pieces_of(values, count):
    pieces = []
    for _ in range(count - 1):
        piece = values.astype(jnp.bfloat16)
        pieces.append(piece)
        values = values - piece.astype(jnp.float32)
    pieces.append(values.astype(jnp.bfloat16))
    return pieces


def dot_rows(a, b):
    return lax.dot_general(a, b, (((1,), (1,)), ((), ())), preferred_element_type=jnp.float32)


def request_kernel(
    plan,
    coords_in,
    owner_in,
    bin_in,
    table_in,
    out_ref,
    early_ref,
    x_ref,
    coords_ref,
    owner_ref,
    bin_ref,
    sem,
):
    p = plan
    row_count = p.cells // LANES
    copies = [
        pltpu.make_async_copy(owner_in, owner_ref, sem.at[0]),
        pltpu.make_async_copy(bin_in, bin_ref, sem.at[1]),
        pltpu.make_async_copy(coords_in, coords_ref, sem.at[2]),
    ]
    early = pltpu.make_async_copy(
        table_in.at[pl.ds(0, early_ref.shape[0])], early_ref, sem.at[3]
    )
    for copy in copies + [early]:
        copy.start()
    for copy in copies:
        copy.wait()
    half = iota((1, LANES), 1) // GROUP
    shard_ids = iota((p.table, LANES), 0)
    owners = owner_ref[...]
    bins = bin_ref[...]
    address = ((bins >> 3) * (8 * p.cols) + (bins & 7)).astype(jnp.float32)
    hits = [owners[i : i + 1, :] == shard_ids for i in range(row_count)]
    before = iota((LANES, LANES), 0)
    after = iota((LANES, LANES), 1)
    earlier = ((before < after) & (before // GROUP == after // GROUP)).astype(jnp.bfloat16)
    ones = jnp.concatenate([h.astype(jnp.float32) for h in hits], axis=0)
    counts = jnp.dot(ones.astype(jnp.bfloat16), earlier, preferred_element_type=jnp.float32)
    x_ref[0:4, :] = coords_ref[...]
    x_ref[5:8, :] = jnp.zeros((3, p.cells), jnp.float32)
    for i in range(row_count):
        x_ref[4:5, i * LANES : (i + 1) * LANES] = address[i : i + 1, :]
    lane_rows = iota((LANES, LANES), 0)
    left, right, codes = [], [], []
    for i in range(row_count):
        span = slice(i * p.table, (i + 1) * p.table)
        rank = jnp.sum(ones[span] * counts[span], axis=0, keepdims=True).astype(jnp.int32)
        codes.append((owners[i : i + 1, :] * p.code + rank).astype(jnp.float32))
        group = 2 * i + half
        near = jnp.where(rank < p.near, group * p.near + rank, -1)
        far = jnp.where(rank >= p.near, group * p.far + rank - p.near, -1)
        right.append(
            jnp.concatenate(
                [
                    (lane_rows == near).astype(jnp.float32),
                    (lane_rows % 32 == far).astype(jnp.float32),
                ],
                axis=0,
            ).astype(jnp.bfloat16)
        )
        fields = x_ref[:, i * LANES : (i + 1) * LANES]
        chosen = []
        for piece in pieces_of(fields, 3):
            piece = jnp.where(hits[i][:, None, :], piece.astype(jnp.float32)[None], 0.0)
            chosen.append(piece.reshape(p.table * 8, LANES).astype(jnp.bfloat16))
        left.append(jnp.concatenate(chosen, axis=0))
    placed = dot_rows(jnp.concatenate(left, axis=1), jnp.concatenate(right, axis=1))
    total = p.table * 8
    placed = placed[0:total] + placed[total : 2 * total] + placed[2 * total :]
    sub = iota((8, LANES), 0)
    block = iota((8, LANES), 1) // 32
    upper = iota((1, LANES), 1) >= GROUP
    for o in range(p.table):
        near_part = placed[o * 8 : (o + 1) * 8, :LANES]
        far_part = placed[o * 8 : (o + 1) * 8, LANES:]
        far_coords = jnp.sum(jnp.where(sub == block, far_part, 0.0), axis=0, keepdims=True)
        code = codes[o // 2] if o % 2 else pltpu.roll(codes[o // 2], GROUP, 1)
        message = jnp.where(
            sub < 5,
            near_part,
            jnp.where(sub == 5, far_coords, jnp.where(upper, code, far_part[4:5])),
        )
        for sc in range(p.scal):
            start = (sc * p.table + o) * SENT
            out_ref[start : start + SENT, :] = message[:SENT]
    early.wait()


def spline_rows(f):
    shape = (K, f[0].shape[1])
    k = iota(shape, 0)
    product = None
    for axis, bit in ((0, 16), (1, 8), (2, 4)):
        factor = jnp.where((k & bit) != 0, f[axis], 1.0 - f[axis])
        product = factor if product is None else product * factor
    last = f[3]
    square = last * last
    cube = square * last
    remain = 1.0 - last
    basis = [
        remain * remain * remain / 6.0,
        (3.0 * cube - 6.0 * square + 4.0) / 6.0,
        (-3.0 * cube + 3.0 * square + 3.0 * last + 1.0) / 6.0,
        cube / 6.0,
    ]
    d = k & 3
    cubic = jnp.where(d == 0, basis[0], jnp.where(d == 1, basis[1], jnp.where(d == 2, basis[2], basis[3])))
    return product * cubic


def swap_blocks(x, count, width):
    row, block = iota(x.shape, 0), iota(x.shape, 1) // width
    bit = 1
    while bit < count:
        up = pltpu.roll(pltpu.roll(x, x.shape[0] - bit, 0), bit * width, 1)
        down = pltpu.roll(pltpu.roll(x, bit, 0), LANES - bit * width, 1)
        low_row, low_block = (row & bit) == 0, (block & bit) == 0
        x = jnp.where(low_row == low_block, x, jnp.where(low_row, up, down))
        bit *= 2
    return x


def fill_slots(plan, recv_ref, out_ref):
    p = plan
    scal_at = lax.axis_index("scal")
    part_x = p.nx // 4
    width = LG * part_x
    codes = jnp.zeros((p.table, LANES), jnp.float32)
    for s in range(p.scal):
        rows = recv_ref[pl.ds(s * p.table * SENT + 6, p.table, stride=SENT), :]
        codes = jnp.where(scal_at == s, rows, codes)
    codes = codes.astype(jnp.bfloat16)
    step = LANES
    for h in range(4):
        x = iota((1, width), 1) % part_x + h * part_x
        inside = (iota((1, width), 1) // part_x) * BX + x % BX + GROUP
        move = (iota((LANES, width), 0) == inside).astype(jnp.float32).astype(jnp.bfloat16)
        moved = jnp.dot(codes, move, preferred_element_type=jnp.float32)
        t = x // BX
        moved = jnp.where(iota((p.table, width), 0) == t, moved, 0.0)
        code = jnp.sum(moved, axis=0, keepdims=True).astype(jnp.int32)
        shard, slot = code // p.code, code % p.code
        t = t - h * (p.table // 4)
        near = (shard // 4) * LANES + (shard % 4) * 32 + t * p.near + slot
        quad = shard // 4
        far = (p.table // 4 + quad // 4) * LANES + (quad % 4) * 32
        far = far + t * p.quad + (shard % 4) * p.far + slot - p.near
        chosen = jnp.where(slot < p.near, near, far)
        rows = iota((step, width), 0)
        for start in range(0, out_ref.shape[1], step):
            hit = rows == chosen - start
            out_ref[h, start : start + step, :] = jnp.where(hit, 1.0, 0.0).astype(jnp.bfloat16)


def swap_four(tiles):
    block = iota((1, LANES), 1) // 32
    for bit in (2, 1):
        low = (block & bit) == 0
        turned = [pltpu.roll(tile, 32 * bit, 1) for tile in tiles]
        back = [pltpu.roll(tile, LANES - 32 * bit, 1) for tile in tiles] if bit == 1 else turned
        out = list(tiles)
        for i in range(4):
            if not i & bit:
                out[i] = jnp.where(low, tiles[i], turned[i + bit])
                out[i + bit] = jnp.where(low, back[i], tiles[i + bit])
        tiles = out
    return tiles


def lookup_kernel(
    plan,
    recv_ref,
    early_ref,
    table_in,
    out_ref,
    place_ref,
    table_ref,
    ints_ref,
    field_ref,
    tile_ref,
    sem,
    *rest,
):
    p = plan
    idx_refs, stores = rest[:16], rest[16:]
    quads = p.table // 4
    early = early_ref.shape[0]
    late = table_in.shape[0] - early
    loads = [
        pltpu.make_async_copy(
            table_in.at[pl.ds(early, late // 2)], table_ref.at[pl.ds(early, late // 2)], sem.at[1]
        ),
        pltpu.make_async_copy(
            table_in.at[pl.ds(early + late // 2, late // 2)],
            table_ref.at[pl.ds(early + late // 2, late // 2)],
            sem.at[2],
        ),
        pltpu.make_async_copy(early_ref, table_ref.at[pl.ds(0, early)], sem.at[3]),
    ]
    loads[0].start()

    def received(r):
        rows = [recv_ref[pl.ds(s * p.table * SENT + r, p.table, stride=SENT), :] for s in range(p.scal)]
        return jnp.concatenate(rows, axis=0)

    addresses = jnp.concatenate([received(4), received(6)], axis=0)
    addresses = swap_blocks(addresses, p.table, p.near)
    order = [addresses[: p.devices]]
    for s in range(p.scal):
        first = p.devices + s * p.table
        order.append(addresses[first : first + quads])
    blank = p.padded - p.chunks
    order.append(jnp.zeros((blank, LANES), jnp.float32))
    order = jnp.concatenate(order, axis=0)
    for first in range(0, p.padded, LANES):
        turned = order[first : first + LANES].T
        ints_ref[:, first : first + LANES] = turned.astype(jnp.int32)
    copies = [
        pltpu.make_async_copy(ints_ref.at[pl.ds(8 * i, 8)], idx_refs[i], sem.at[0])
        for i in range(16)
    ]
    for copy in copies:
        copy.start()
    for load in loads[1:]:
        load.start()
    fields = jnp.concatenate([received(f) for f in (0, 1, 2, 3, 5)], axis=0)
    fields = swap_blocks(fields, p.table, p.near)
    for f in range(4):
        field_ref[f * p.chunks : f * p.chunks + p.devices, :] = fields[
            f * p.devices : (f + 1) * p.devices
        ]
        for s in range(p.scal):
            first = 4 * p.devices + s * p.table + f * quads
            to = f * p.chunks + p.devices + s * quads
            field_ref[to : to + quads, :] = fields[first : first + quads]
    fill_slots(p, recv_ref, place_ref)
    for copy in copies:
        copy.wait()

    def fetch(store, chunk, part):
        step = LANES // p.cols
        for slot in range(part * step, (part + 1) * step, 2):
            rows = []
            for i in (slot, slot + 1):
                address = idx_refs[i // 8][i % 8, chunk]
                if p.cols == 1:
                    rows.append(table_ref[pl.ds(address, 1), :])
                else:
                    rows.append(table_ref[pl.ds(address, p.cols, stride=8), :])
            store[slot * p.cols : (slot + 2) * p.cols, :] = jnp.concatenate(rows, axis=0)

    def reduce(store, chunk, ahead=None):
        weights = spline_rows([field_ref[pl.ds(f * p.chunks + chunk, 1), :] for f in range(4)])
        parts = []
        for c in range(p.cols):
            rows = pl.ds(c, LANES, stride=p.cols) if p.cols > 1 else pl.ds(0, LANES)
            turned = store[rows, :].T
            for m in range(4):
                product = turned[m * K : (m + 1) * K] * weights
                parts.append((product[0:8] + product[8:16]) + (product[16:24] + product[24:32]))
            if ahead is not None:
                ahead(c)
        tile = jnp.sum(jnp.concatenate(parts, axis=0).reshape(p.scalars, 8, LANES), axis=1)
        tile_ref[pl.ds(pl.multiple_of(chunk * p.scalars, p.scalars), p.scalars), :] = tile

    for load in loads:
        load.wait()
    for n in range(BATCH):
        for c in range(p.cols):
            fetch(stores[n], n, c)

    def batch(now, half, more):
        for n in range(BATCH):
            ahead = None
            if more:
                store = stores[(1 - half) * BATCH + n]
                ahead = functools.partial(fetch, store, now + BATCH + n)
            reduce(stores[half * BATCH + n], now + n, ahead)

    def two_batches(i, carry):
        batch(2 * i * BATCH, 0, True)
        batch((2 * i + 1) * BATCH, 1, True)
        return carry

    lax.fori_loop(0, p.chunks // (2 * BATCH) - 1, two_batches, 0)
    batch(p.chunks - 2 * BATCH, 0, True)
    batch(p.chunks - BATCH, 1, False)

    for g in range(p.table):
        for s in range(p.scal):
            dest, chunk = g * p.scal + s, s * p.table + g
            out_ref[dest * p.rows : dest * p.rows + p.scalars, :] = tile_ref[
                chunk * p.scalars : (chunk + 1) * p.scalars, :
            ]
    quad_of = (iota((1, LANES), 1) // p.far) % 4
    for quad in range(quads):
        for s in range(p.scal):
            first = (p.devices + s * quads + quad) * p.scalars
            tile = tile_ref[first : first + p.scalars, :]
            turned = [pltpu.roll(tile, (d * p.far) % LANES, 1) if d else tile for d in range(4)]
            wrapped = [
                pltpu.roll(tile, (-d * p.far) % LANES, 1) if d else tile for d in range(4)
            ]
            for i in range(4):
                message = jnp.zeros((p.few, LANES), jnp.float32)
                for b in range(4):
                    moved = turned[b - i] if b >= i else wrapped[i - b]
                    message = jnp.where(
                        quad_of == b, moved[b * p.few : (b + 1) * p.few], message
                    )
                start = ((quad * 4 + i) * p.scal + s) * p.rows + p.scalars
                out_ref[start : start + p.few, :] = message


def lookup_scratch(plan, table_shape):
    p = plan
    return [
        pltpu.VMEM((table_shape[0] + 8 * p.cols, LANES), jnp.float32),
        pltpu.VMEM((LANES, p.padded), jnp.int32),
        pltpu.VMEM((4 * p.chunks, LANES), jnp.float32),
        pltpu.VMEM((p.chunks * p.scalars, LANES), jnp.float32),
        pltpu.SemaphoreType.DMA((4,)),
    ] + [pltpu.SMEM((8, p.padded), jnp.int32)] * 16 + [pltpu.VMEM((p.cols * LANES, LANES), jnp.float32) for _ in range(2 * BATCH)]


def filter_kernel(plan, recv_ref, place_ref, op_ref, filtered_ref, gradient_ref, *left_refs):
    p = plan
    quad_of = (iota((1, LANES), 1) // p.far) % 4

    def put(tiles, first_row, col):
        for left_ref, tile in zip(left_refs, swap_four(tiles), strict=True):
            left_ref[first_row : first_row + tile.shape[0], col : col + LANES] = tile

    for sc in range(p.scal):
        for o in range(0, p.table, 4):
            starts = [((o + i) * p.scal + sc) * p.rows for i in range(4)]
            tiles = [recv_ref[start : start + p.scalars, :] for start in starts]
            put(tiles, sc * p.scalars, o // 4 * LANES)
        for quad in range(0, p.table // 4, 4):
            tiles = []
            for n in range(4):
                starts = [((quad + n) * 4 + i) * p.scal + sc for i in range(4)]
                starts = [start * p.rows + p.scalars for start in starts]
                tile = []
                for b in range(4):
                    part = jnp.zeros((p.few, LANES), jnp.float32)
                    for i in range(4):
                        turned = recv_ref[starts[i] : starts[i] + p.few, :]
                        turned = pltpu.roll(turned, ((i - b) * p.far) % LANES, 1)
                        part = jnp.where(quad_of == i, turned, part)
                    tile.append(part)
                tiles.append(jnp.concatenate(tile, axis=0))
            put(tiles, sc * p.scalars, (p.table // 4 + quad // 4) * LANES)
    sides = []
    for h in range(4):
        left = jnp.concatenate(pieces_of(left_refs[h][...], 3), axis=0)
        values = jnp.dot(left, place_ref[h], preferred_element_type=jnp.float32)
        sides.append(
            values[0:SCAL_ALL] + values[SCAL_ALL : 2 * SCAL_ALL] + values[2 * SCAL_ALL :]
        )
    part_x = p.nx // 4
    if part_x == 32:
        lines = []
        for first in range(0, LG * part_x, LANES):
            lines.extend(swap_four([side[:, first : first + LANES] for side in sides]))
    else:
        lines = [
            jnp.concatenate([side[:, r * part_x : (r + 1) * part_x] for side in sides], axis=1)
            for r in range(LG)
        ]
    lines = jnp.concatenate(lines, axis=0)
    lines, op = pieces_of(lines, 2), pieces_of(op_ref[...], 2)
    both = jnp.dot(
        jnp.concatenate([lines[0], lines[0], lines[1]], axis=1),
        jnp.concatenate([op[0], op[1], op[0]], axis=0),
        preferred_element_type=jnp.float32,
    )
    for r in range(LG):
        rows = slice(r * SCAL_ALL, (r + 1) * SCAL_ALL)
        for part in range(p.nx // LANES):
            at = pl.ds(part * SCAL_ALL * LG + r, SCAL_ALL, stride=LG)
            first = part * LANES
            filtered_ref[at, :] = both[rows, first : first + LANES]
            gradient_ref[at, :] = both[rows, p.nx + first : p.nx + first + LANES]


VMEM = pl.BlockSpec(memory_space=pltpu.VMEM)
SMEM = pl.BlockSpec(memory_space=pltpu.SMEM)
HBM = pl.BlockSpec(memory_space=pltpu.HBM)


def call(kernel, plan, out_shape, in_specs, scratch, limit, cost, name):
    many = isinstance(out_shape, tuple)
    return pl.pallas_call(
        functools.partial(kernel, plan),
        out_shape=out_shape,
        in_specs=in_specs,
        out_specs=(VMEM,) * len(out_shape) if many else VMEM,
        scratch_shapes=scratch,
        compiler_params=pltpu.CompilerParams(vmem_limit_bytes=limit << 20),
        cost_estimate=pl.CostEstimate(flops=cost, bytes_accessed=cost // 256, transcendentals=0),
        name=name,
    )


def exchange(array, axes):
    return lax.all_to_all(array, axes, split_axis=0, concat_axis=0, tiled=True)


def on_device(plan, cell_coords, flamelet_table, owner_shard, local_bin):
    p = plan
    f32, i32 = jnp.float32, jnp.int32
    row_count = p.cells // LANES
    owners = owner_shard.reshape(row_count, LANES)
    bins = local_bin.reshape(row_count, LANES)
    bin_count, depth = flamelet_table.shape
    table = flamelet_table.reshape(bin_count // 8, 8, p.cols, LANES).transpose(0, 2, 1, 3)
    table = table.reshape(bin_count * p.cols, LANES)
    requests, early = call(
        request_kernel,
        p,
        (
            jax.ShapeDtypeStruct((p.devices * SENT, LANES), f32),
            jax.ShapeDtypeStruct((bin_count * p.cols * 11 // 32, LANES), f32),
        ),
        [HBM] * 4,
        [
            pltpu.VMEM((8, p.cells), f32),
            pltpu.VMEM(cell_coords.shape, f32),
            pltpu.VMEM(owners.shape, i32),
            pltpu.VMEM(bins.shape, i32),
            pltpu.SemaphoreType.DMA((4,)),
        ],
        32,
        1 << 20,
        "requests",
    )(*[pltpu.with_memory_space_constraint(a, pltpu.HBM) for a in (cell_coords, owners, bins, table)])
    received = exchange(requests.reshape(p.devices, 1, SENT * LANES), AXES[::-1])
    received = received.reshape(p.devices * SENT, LANES)
    replies, place = call(
        lookup_kernel,
        p,
        (
            jax.ShapeDtypeStruct((p.devices * p.rows, LANES), f32),
            jax.ShapeDtypeStruct((4, p.table * 5 * LANES // 16, LG * p.nx // 4), jnp.bfloat16),
        ),
        [VMEM, VMEM, HBM],
        lookup_scratch(p, table.shape),
        30,
        1 << 24,
        "lookup",
    )(received, early, pltpu.with_memory_space_constraint(table, pltpu.HBM))
    answers = exchange(replies.reshape(p.devices, 1, p.rows * LANES), AXES)
    answers = answers.reshape(p.devices * p.rows, LANES)

    filter_op = filter_table(p.nx).T
    both_op = np.concatenate([filter_op, filter_op @ derivative_table(p.nx).T], axis=1)
    both_op = jnp.asarray(both_op.astype(np.float32))
    out = jax.ShapeDtypeStruct((p.nx // LANES * SCAL_ALL * LG, LANES), f32)
    outs = call(
        filter_kernel,
        p,
        (out, out),
        [VMEM] * 3,
        [pltpu.VMEM((SCAL_ALL, p.table * 5 * LANES // 16), f32)] * 4,
        8 + p.nx * p.table // 64,
        1 << 24,
        "filter",
    )(answers, place, both_op)
    outs = [out.reshape(p.nx // LANES, SCAL_ALL, LG, LANES).transpose(1, 2, 0, 3) for out in outs]
    return tuple(out.reshape(SCAL_ALL, LG, p.nx) for out in outs)


def solution(mesh):
    table, scal = mesh.shape["table"], mesh.shape["scal"]

    def step(cell_coords, flamelet_table, owner_shard, local_bin):
        plan = Plan(table, scal, cell_coords.shape[1])
        return on_device(plan, cell_coords, flamelet_table, owner_shard, local_bin)

    return jax.shard_map(
        step,
        mesh=mesh,
        in_specs=(
            P(None, AXES),
            P("table", "scal"),
            P(AXES, None),
            P(AXES),
        ),
        out_specs=(P(None, AXES, None), P(None, AXES, None)),
        check_vma=False,
    )
```

```python
import functools

import jax
import jax.numpy as jnp
import numpy as np
from jax import lax
from jax.experimental import pallas as pl
from jax.experimental.pallas import tpu as pltpu
from jax.sharding import PartitionSpec as P

SCAL_ALL = 32
K = 32
BX = 8
LG = 8
GROUP = BX * LG
LANES = 128
AXES = ("table", "scal")
BATCH = 4
SENT = 7

strength = 0.499


def thomas_solve(below, middle, above, right_side):
    length = middle.shape[0]
    upper_factor = np.zeros(length)
    solved = np.zeros(right_side.shape)
    for row in range(length):
        if row == 0:
            denom = middle[0]
            solved[0] = right_side[0] / denom
        else:
            denom = middle[row] - below[row] * upper_factor[row - 1]
            solved[row] = (right_side[row] - below[row] * solved[row - 1]) / denom
        upper_factor[row] = above[row] / denom
    for row in range(length - 2, -1, -1):
        solved[row] = solved[row] - upper_factor[row] * solved[row + 1]
    return solved


def filter_table(length):
    positions = np.arange(length)
    offset = positions[None, :] - positions[:, None]
    distance = np.abs(offset)
    interior = (positions >= 3) & (positions <= length - 4)
    coeffs = [
        (11.0 + 10.0 * strength) / 16.0,
        (15.0 + 34.0 * strength) / 64.0,
        (-3.0 + 6.0 * strength) / 32.0,
        (1.0 - 2.0 * strength) / 64.0,
    ]
    band = np.zeros((length, length))
    for reach in range(4):
        band = band + np.where(distance == reach, coeffs[reach], 0.0)
    right_side = np.where(interior[:, None], band, np.where(offset == 0, 1.0, 0.0))
    coupling = np.where(interior, strength, 0.0)
    return thomas_solve(coupling, np.ones(length), coupling, right_side)


def derivative_table(length):
    positions = np.arange(length)
    offset = positions[None, :] - positions[:, None]
    distance = np.abs(offset)
    direction = np.sign(offset) * 1.0
    boundary = (positions == 0) | (positions == length - 1)
    second = (positions == 1) | (positions == length - 2)
    interior = ~(boundary | second)
    below_diag = np.where(
        interior, 1.0 / 3.0, np.where(second, 0.25, np.where(positions == length - 1, 2.0, 0.0))
    )
    above_diag = np.where(
        interior, 1.0 / 3.0, np.where(second, 0.25, np.where(positions == 0, 2.0, 0.0))
    )
    inner_rows = direction * (
        np.where(distance == 1, 7.0 / 9.0, 0.0) + np.where(distance == 2, 1.0 / 36.0, 0.0)
    )
    second_rows = direction * np.where(distance == 1, 0.75, 0.0)
    first_row = np.where(
        offset == 0, -2.5, np.where(offset == 1, 2.0, np.where(offset == 2, 0.5, 0.0))
    )
    final_row = np.where(
        offset == 0, 2.5, np.where(offset == -1, -2.0, np.where(offset == -2, -0.5, 0.0))
    )
    right_side = np.where(
        interior[:, None],
        inner_rows,
        np.where(
            second[:, None], second_rows, np.where((positions == 0)[:, None], first_row, final_row)
        ),
    )
    return thomas_solve(below_diag, np.ones(length), above_diag, right_side)


class Plan:
    def __init__(self, table, scal, cells):
        self.table, self.scal, self.cells = table, scal, cells
        self.devices = table * scal
        self.cap = max(2, 5 * GROUP // (2 * table))
        self.near = LANES // table
        self.far = self.cap - self.near
        self.quad = 4 * self.far
        assert cells == table * GROUP and table * self.quad == LANES
        self.code = 1 << (self.cap - 1).bit_length()
        self.scalars = SCAL_ALL // scal
        self.cols = self.scalars * K // LANES
        self.few = self.scalars // 4
        self.rows = self.scalars + self.few
        self.nx = BX * table
        self.chunks = self.devices + self.devices // 4
        self.padded = -(-self.chunks // LANES) * LANES


def iota(shape, dim):
    return lax.broadcasted_iota(jnp.int32, shape, dim)


def pieces_of(values, count):
    pieces = []
    for _ in range(count - 1):
        piece = values.astype(jnp.bfloat16)
        pieces.append(piece)
        values = values - piece.astype(jnp.float32)
    pieces.append(values.astype(jnp.bfloat16))
    return pieces


def dot_rows(a, b):
    return lax.dot_general(a, b, (((1,), (1,)), ((), ())), preferred_element_type=jnp.float32)


def request_kernel(
    plan,
    coords_in,
    owner_in,
    bin_in,
    table_in,
    out_ref,
    early_ref,
    x_ref,
    coords_ref,
    owner_ref,
    bin_ref,
    sem,
):
    p = plan
    row_count = p.cells // LANES
    copies = [
        pltpu.make_async_copy(owner_in, owner_ref, sem.at[0]),
        pltpu.make_async_copy(bin_in, bin_ref, sem.at[1]),
        pltpu.make_async_copy(coords_in, coords_ref, sem.at[2]),
    ]
    early = pltpu.make_async_copy(
        table_in.at[pl.ds(0, early_ref.shape[0])], early_ref, sem.at[3]
    )
    for copy in copies + [early]:
        copy.start()
    for copy in copies:
        copy.wait()
    half = iota((1, LANES), 1) // GROUP
    shard_ids = iota((p.table, LANES), 0)
    owners = owner_ref[...]
    bins = bin_ref[...]
    address = ((bins >> 3) * (8 * p.cols) + (bins & 7)).astype(jnp.float32)
    hits = [owners[i : i + 1, :] == shard_ids for i in range(row_count)]
    before = iota((LANES, LANES), 0)
    after = iota((LANES, LANES), 1)
    earlier = ((before < after) & (before // GROUP == after // GROUP)).astype(jnp.bfloat16)
    ones = jnp.concatenate([h.astype(jnp.float32) for h in hits], axis=0)
    counts = jnp.dot(ones.astype(jnp.bfloat16), earlier, preferred_element_type=jnp.float32)
    x_ref[0:4, :] = coords_ref[...]
    x_ref[5:8, :] = jnp.zeros((3, p.cells), jnp.float32)
    for i in range(row_count):
        x_ref[4:5, i * LANES : (i + 1) * LANES] = address[i : i + 1, :]
    lane_rows = iota((LANES, LANES), 0)
    left, right, codes = [], [], []
    for i in range(row_count):
        span = slice(i * p.table, (i + 1) * p.table)
        rank = jnp.sum(ones[span] * counts[span], axis=0, keepdims=True).astype(jnp.int32)
        codes.append((owners[i : i + 1, :] * p.code + rank).astype(jnp.float32))
        group = 2 * i + half
        near = jnp.where(rank < p.near, group * p.near + rank, -1)
        far = jnp.where(rank >= p.near, group * p.far + rank - p.near, -1)
        right.append(
            jnp.concatenate(
                [
                    (lane_rows == near).astype(jnp.float32),
                    (lane_rows % 32 == far).astype(jnp.float32),
                ],
                axis=0,
            ).astype(jnp.bfloat16)
        )
        fields = x_ref[:, i * LANES : (i + 1) * LANES]
        chosen = []
        for piece in pieces_of(fields, 3):
            piece = jnp.where(hits[i][:, None, :], piece.astype(jnp.float32)[None], 0.0)
            chosen.append(piece.reshape(p.table * 8, LANES).astype(jnp.bfloat16))
        left.append(jnp.concatenate(chosen, axis=0))
    placed = dot_rows(jnp.concatenate(left, axis=1), jnp.concatenate(right, axis=1))
    total = p.table * 8
    placed = placed[0:total] + placed[total : 2 * total] + placed[2 * total :]
    sub = iota((8, LANES), 0)
    block = iota((8, LANES), 1) // 32
    upper = iota((1, LANES), 1) >= GROUP
    for o in range(p.table):
        near_part = placed[o * 8 : (o + 1) * 8, :LANES]
        far_part = placed[o * 8 : (o + 1) * 8, LANES:]
        far_coords = jnp.sum(jnp.where(sub == block, far_part, 0.0), axis=0, keepdims=True)
        code = codes[o // 2] if o % 2 else pltpu.roll(codes[o // 2], GROUP, 1)
        message = jnp.where(
            sub < 5,
            near_part,
            jnp.where(sub == 5, far_coords, jnp.where(upper, code, far_part[4:5])),
        )
        for sc in range(p.scal):
            start = (sc * p.table + o) * SENT
            out_ref[start : start + SENT, :] = message[:SENT]
    early.wait()


def spline_rows(f):
    shape = (K, f[0].shape[1])
    k = iota(shape, 0)
    product = None
    for axis, bit in ((0, 16), (1, 8), (2, 4)):
        factor = jnp.where((k & bit) != 0, f[axis], 1.0 - f[axis])
        product = factor if product is None else product * factor
    last = f[3]
    square = last * last
    cube = square * last
    remain = 1.0 - last
    basis = [
        remain * remain * remain / 6.0,
        (3.0 * cube - 6.0 * square + 4.0) / 6.0,
        (-3.0 * cube + 3.0 * square + 3.0 * last + 1.0) / 6.0,
        cube / 6.0,
    ]
    d = k & 3
    cubic = jnp.where(d == 0, basis[0], jnp.where(d == 1, basis[1], jnp.where(d == 2, basis[2], basis[3])))
    return product * cubic


def swap_blocks(x, count, width):
    row, block = iota(x.shape, 0), iota(x.shape, 1) // width
    bit = 1
    while bit < count:
        up = pltpu.roll(pltpu.roll(x, x.shape[0] - bit, 0), bit * width, 1)
        down = pltpu.roll(pltpu.roll(x, bit, 0), LANES - bit * width, 1)
        low_row, low_block = (row & bit) == 0, (block & bit) == 0
        x = jnp.where(low_row == low_block, x, jnp.where(low_row, up, down))
        bit *= 2
    return x


def fill_slots(plan, recv_ref, out_ref):
    p = plan
    scal_at = lax.axis_index("scal")
    part_x = p.nx // 4
    width = LG * part_x
    codes = jnp.zeros((p.table, LANES), jnp.float32)
    for s in range(p.scal):
        rows = recv_ref[pl.ds(s * p.table * SENT + 6, p.table, stride=SENT), :]
        codes = jnp.where(scal_at == s, rows, codes)
    codes = codes.astype(jnp.bfloat16)
    step = LANES
    for h in range(4):
        x = iota((1, width), 1) % part_x + h * part_x
        inside = (iota((1, width), 1) // part_x) * BX + x % BX + GROUP
        move = (iota((LANES, width), 0) == inside).astype(jnp.float32).astype(jnp.bfloat16)
        moved = jnp.dot(codes, move, preferred_element_type=jnp.float32)
        t = x // BX
        moved = jnp.where(iota((p.table, width), 0) == t, moved, 0.0)
        code = jnp.sum(moved, axis=0, keepdims=True).astype(jnp.int32)
        shard, slot = code // p.code, code % p.code
        t = t - h * (p.table // 4)
        near = (shard // 4) * LANES + (shard % 4) * 32 + t * p.near + slot
        quad = shard // 4
        far = (p.table // 4 + quad // 4) * LANES + (quad % 4) * 32
        far = far + t * p.quad + (shard % 4) * p.far + slot - p.near
        chosen = jnp.where(slot < p.near, near, far)
        rows = iota((step, width), 0)
        for start in range(0, out_ref.shape[1], step):
            hit = rows == chosen - start
            out_ref[h, start : start + step, :] = jnp.where(hit, 1.0, 0.0).astype(jnp.bfloat16)


def swap_four(tiles):
    block = iota((1, LANES), 1) // 32
    for bit in (2, 1):
        low = (block & bit) == 0
        turned = [pltpu.roll(tile, 32 * bit, 1) for tile in tiles]
        back = [pltpu.roll(tile, LANES - 32 * bit, 1) for tile in tiles] if bit == 1 else turned
        out = list(tiles)
        for i in range(4):
            if not i & bit:
                out[i] = jnp.where(low, tiles[i], turned[i + bit])
                out[i + bit] = jnp.where(low, back[i], tiles[i + bit])
        tiles = out
    return tiles


def lookup_kernel(
    plan,
    recv_ref,
    early_ref,
    table_in,
    out_ref,
    place_ref,
    table_ref,
    ints_ref,
    field_ref,
    tile_ref,
    sem,
    *rest,
):
    p = plan
    idx_refs, stores = rest[:16], rest[16:]
    quads = p.table // 4
    early = early_ref.shape[0]
    late = table_in.shape[0] - early
    loads = [
        pltpu.make_async_copy(
            table_in.at[pl.ds(early, late // 2)], table_ref.at[pl.ds(early, late // 2)], sem.at[1]
        ),
        pltpu.make_async_copy(
            table_in.at[pl.ds(early + late // 2, late // 2)],
            table_ref.at[pl.ds(early + late // 2, late // 2)],
            sem.at[2],
        ),
        pltpu.make_async_copy(early_ref, table_ref.at[pl.ds(0, early)], sem.at[3]),
    ]
    loads[0].start()

    def received(r):
        rows = [recv_ref[pl.ds(s * p.table * SENT + r, p.table, stride=SENT), :] for s in range(p.scal)]
        return jnp.concatenate(rows, axis=0)

    addresses = jnp.concatenate([received(4), received(6)], axis=0)
    addresses = swap_blocks(addresses, p.table, p.near)
    order = [addresses[: p.devices]]
    for s in range(p.scal):
        first = p.devices + s * p.table
        order.append(addresses[first : first + quads])
    blank = p.padded - p.chunks
    order.append(jnp.zeros((blank, LANES), jnp.float32))
    order = jnp.concatenate(order, axis=0)
    for first in range(0, p.padded, LANES):
        turned = order[first : first + LANES].T
        ints_ref[:, first : first + LANES] = turned.astype(jnp.int32)
    copies = [
        pltpu.make_async_copy(ints_ref.at[pl.ds(8 * i, 8)], idx_refs[i], sem.at[0])
        for i in range(16)
    ]
    for copy in copies:
        copy.start()
    for load in loads[1:]:
        load.start()
    fields = jnp.concatenate([received(f) for f in (0, 1, 2, 3, 5)], axis=0)
    fields = swap_blocks(fields, p.table, p.near)
    for f in range(4):
        field_ref[f * p.chunks : f * p.chunks + p.devices, :] = fields[
            f * p.devices : (f + 1) * p.devices
        ]
        for s in range(p.scal):
            first = 4 * p.devices + s * p.table + f * quads
            to = f * p.chunks + p.devices + s * quads
            field_ref[to : to + quads, :] = fields[first : first + quads]
    fill_slots(p, recv_ref, place_ref)
    for copy in copies:
        copy.wait()

    def fetch(store, chunk, part):
        step = LANES // p.cols
        for slot in range(part * step, (part + 1) * step, 2):
            rows = []
            for i in (slot, slot + 1):
                address = idx_refs[i // 8][i % 8, chunk]
                if p.cols == 1:
                    rows.append(table_ref[pl.ds(address, 1), :])
                else:
                    rows.append(table_ref[pl.ds(address, p.cols, stride=8), :])
            store[slot * p.cols : (slot + 2) * p.cols, :] = jnp.concatenate(rows, axis=0)

    def reduce(store, chunk, ahead=None):
        weights = spline_rows([field_ref[pl.ds(f * p.chunks + chunk, 1), :] for f in range(4)])
        parts = []
        for c in range(p.cols):
            rows = pl.ds(c, LANES, stride=p.cols) if p.cols > 1 else pl.ds(0, LANES)
            turned = store[rows, :].T
            for m in range(4):
                product = turned[m * K : (m + 1) * K] * weights
                parts.append((product[0:8] + product[8:16]) + (product[16:24] + product[24:32]))
            if ahead is not None:
                ahead(c)
        tile = jnp.sum(jnp.concatenate(parts, axis=0).reshape(p.scalars, 8, LANES), axis=1)
        tile_ref[pl.ds(pl.multiple_of(chunk * p.scalars, p.scalars), p.scalars), :] = tile

    for load in loads:
        load.wait()
    for n in range(BATCH):
        for c in range(p.cols):
            fetch(stores[n], n, c)

    def batch(now, half, more):
        for n in range(BATCH):
            ahead = None
            if more:
                store = stores[(1 - half) * BATCH + n]
                ahead = functools.partial(fetch, store, now + BATCH + n)
            reduce(stores[half * BATCH + n], now + n, ahead)

    def two_batches(i, carry):
        batch(2 * i * BATCH, 0, True)
        batch((2 * i + 1) * BATCH, 1, True)
        return carry

    lax.fori_loop(0, p.chunks // (2 * BATCH) - 1, two_batches, 0)
    batch(p.chunks - 2 * BATCH, 0, True)
    batch(p.chunks - BATCH, 1, False)

    for g in range(p.table):
        for s in range(p.scal):
            dest, chunk = g * p.scal + s, s * p.table + g
            out_ref[dest * p.rows : dest * p.rows + p.scalars, :] = tile_ref[
                chunk * p.scalars : (chunk + 1) * p.scalars, :
            ]
    quad_of = (iota((1, LANES), 1) // p.far) % 4
    for quad in range(quads):
        for s in range(p.scal):
            first = (p.devices + s * quads + quad) * p.scalars
            tile = tile_ref[first : first + p.scalars, :]
            turned = [pltpu.roll(tile, (d * p.far) % LANES, 1) if d else tile for d in range(4)]
            wrapped = [
                pltpu.roll(tile, (-d * p.far) % LANES, 1) if d else tile for d in range(4)
            ]
            for i in range(4):
                message = jnp.zeros((p.few, LANES), jnp.float32)
                for b in range(4):
                    moved = turned[b - i] if b >= i else wrapped[i - b]
                    message = jnp.where(
                        quad_of == b, moved[b * p.few : (b + 1) * p.few], message
                    )
                start = ((quad * 4 + i) * p.scal + s) * p.rows + p.scalars
                out_ref[start : start + p.few, :] = message


def lookup_scratch(plan, table_shape):
    p = plan
    return [
        pltpu.VMEM((table_shape[0] + 8 * p.cols, LANES), jnp.float32),
        pltpu.VMEM((LANES, p.padded), jnp.int32),
        pltpu.VMEM((4 * p.chunks, LANES), jnp.float32),
        pltpu.VMEM((p.chunks * p.scalars, LANES), jnp.float32),
        pltpu.SemaphoreType.DMA((4,)),
    ] + [pltpu.SMEM((8, p.padded), jnp.int32)] * 16 + [pltpu.VMEM((p.cols * LANES, LANES), jnp.float32) for _ in range(2 * BATCH)]


def filter_kernel(plan, recv_ref, place_ref, op_ref, filtered_ref, gradient_ref, *left_refs):
    p = plan
    quad_of = (iota((1, LANES), 1) // p.far) % 4

    def put(tiles, first_row, col):
        for left_ref, tile in zip(left_refs, swap_four(tiles), strict=True):
            left_ref[first_row : first_row + tile.shape[0], col : col + LANES] = tile

    for sc in range(p.scal):
        for o in range(0, p.table, 4):
            starts = [((o + i) * p.scal + sc) * p.rows for i in range(4)]
            tiles = [recv_ref[start : start + p.scalars, :] for start in starts]
            put(tiles, sc * p.scalars, o // 4 * LANES)
        for quad in range(0, p.table // 4, 4):
            tiles = []
            for n in range(4):
                starts = [((quad + n) * 4 + i) * p.scal + sc for i in range(4)]
                starts = [start * p.rows + p.scalars for start in starts]
                tile = []
                for b in range(4):
                    part = jnp.zeros((p.few, LANES), jnp.float32)
                    for i in range(4):
                        turned = recv_ref[starts[i] : starts[i] + p.few, :]
                        turned = pltpu.roll(turned, ((i - b) * p.far) % LANES, 1)
                        part = jnp.where(quad_of == i, turned, part)
                    tile.append(part)
                tiles.append(jnp.concatenate(tile, axis=0))
            put(tiles, sc * p.scalars, (p.table // 4 + quad // 4) * LANES)
    sides = []
    for h in range(4):
        left = jnp.concatenate(pieces_of(left_refs[h][...], 2), axis=0)
        values = jnp.dot(left, place_ref[h], preferred_element_type=jnp.float32)
        sides.append(values[:SCAL_ALL] + values[SCAL_ALL:])
    part_x = p.nx // 4
    if part_x == 32:
        lines = []
        for first in range(0, LG * part_x, LANES):
            lines.extend(swap_four([side[:, first : first + LANES] for side in sides]))
    else:
        lines = [
            jnp.concatenate([side[:, r * part_x : (r + 1) * part_x] for side in sides], axis=1)
            for r in range(LG)
        ]
    lines = jnp.concatenate(lines, axis=0)
    lines, op = pieces_of(lines, 2), pieces_of(op_ref[...], 2)
    both = jnp.dot(
        jnp.concatenate([lines[0], lines[0], lines[1]], axis=1),
        jnp.concatenate([op[0], op[1], op[0]], axis=0),
        preferred_element_type=jnp.float32,
    )
    for r in range(LG):
        rows = slice(r * SCAL_ALL, (r + 1) * SCAL_ALL)
        for part in range(p.nx // LANES):
            at = pl.ds(part * SCAL_ALL * LG + r, SCAL_ALL, stride=LG)
            first = part * LANES
            filtered_ref[at, :] = both[rows, first : first + LANES]
            gradient_ref[at, :] = both[rows, p.nx + first : p.nx + first + LANES]


VMEM = pl.BlockSpec(memory_space=pltpu.VMEM)
SMEM = pl.BlockSpec(memory_space=pltpu.SMEM)
HBM = pl.BlockSpec(memory_space=pltpu.HBM)


def call(kernel, plan, out_shape, in_specs, scratch, limit, cost, name):
    many = isinstance(out_shape, tuple)
    return pl.pallas_call(
        functools.partial(kernel, plan),
        out_shape=out_shape,
        in_specs=in_specs,
        out_specs=(VMEM,) * len(out_shape) if many else VMEM,
        scratch_shapes=scratch,
        compiler_params=pltpu.CompilerParams(vmem_limit_bytes=limit << 20),
        cost_estimate=pl.CostEstimate(flops=cost, bytes_accessed=cost // 256, transcendentals=0),
        name=name,
    )


def exchange(array, axes):
    return lax.all_to_all(array, axes, split_axis=0, concat_axis=0, tiled=True)


def on_device(plan, cell_coords, flamelet_table, owner_shard, local_bin):
    p = plan
    f32, i32 = jnp.float32, jnp.int32
    row_count = p.cells // LANES
    owners = owner_shard.reshape(row_count, LANES)
    bins = local_bin.reshape(row_count, LANES)
    bin_count, depth = flamelet_table.shape
    table = flamelet_table.reshape(bin_count // 8, 8, p.cols, LANES).transpose(0, 2, 1, 3)
    table = table.reshape(bin_count * p.cols, LANES)
    requests, early = call(
        request_kernel,
        p,
        (
            jax.ShapeDtypeStruct((p.devices * SENT, LANES), f32),
            jax.ShapeDtypeStruct((bin_count * p.cols * 11 // 32, LANES), f32),
        ),
        [HBM] * 4,
        [
            pltpu.VMEM((8, p.cells), f32),
            pltpu.VMEM(cell_coords.shape, f32),
            pltpu.VMEM(owners.shape, i32),
            pltpu.VMEM(bins.shape, i32),
            pltpu.SemaphoreType.DMA((4,)),
        ],
        32,
        1 << 20,
        "requests",
    )(*[pltpu.with_memory_space_constraint(a, pltpu.HBM) for a in (cell_coords, owners, bins, table)])
    received = exchange(requests.reshape(p.devices, 1, SENT * LANES), AXES[::-1])
    received = received.reshape(p.devices * SENT, LANES)
    replies, place = call(
        lookup_kernel,
        p,
        (
            jax.ShapeDtypeStruct((p.devices * p.rows, LANES), f32),
            jax.ShapeDtypeStruct((4, p.table * 5 * LANES // 16, LG * p.nx // 4), jnp.bfloat16),
        ),
        [VMEM, VMEM, HBM],
        lookup_scratch(p, table.shape),
        30,
        1 << 24,
        "lookup",
    )(received, early, pltpu.with_memory_space_constraint(table, pltpu.HBM))
    answers = exchange(replies.reshape(p.devices, 1, p.rows * LANES), AXES)
    answers = answers.reshape(p.devices * p.rows, LANES)

    filter_op = filter_table(p.nx).T
    both_op = np.concatenate([filter_op, filter_op @ derivative_table(p.nx).T], axis=1)
    both_op = jnp.asarray(both_op.astype(np.float32))
    out = jax.ShapeDtypeStruct((p.nx // LANES * SCAL_ALL * LG, LANES), f32)
    outs = call(
        filter_kernel,
        p,
        (out, out),
        [VMEM] * 3,
        [pltpu.VMEM((SCAL_ALL, p.table * 5 * LANES // 16), f32)] * 4,
        8 + p.nx * p.table // 64,
        1 << 24,
        "filter",
    )(answers, place, both_op)
    outs = [out.reshape(p.nx // LANES, SCAL_ALL, LG, LANES).transpose(1, 2, 0, 3) for out in outs]
    return tuple(out.reshape(SCAL_ALL, LG, p.nx) for out in outs)


def solution(mesh):
    table, scal = mesh.shape["table"], mesh.shape["scal"]

    def step(cell_coords, flamelet_table, owner_shard, local_bin):
        plan = Plan(table, scal, cell_coords.shape[1])
        return on_device(plan, cell_coords, flamelet_table, owner_shard, local_bin)

    return jax.shard_map(
        step,
        mesh=mesh,
        in_specs=(
            P(None, AXES),
            P("table", "scal"),
            P(AXES, None),
            P(AXES),
        ),
        out_specs=(P(None, AXES, None), P(None, AXES, None)),
        check_vma=False,
    )
```

```python
import functools

import jax
import jax.numpy as jnp
import numpy as np
from jax import lax
from jax.experimental import pallas as pl
from jax.experimental.pallas import tpu as pltpu
from jax.sharding import PartitionSpec as P

SCAL_ALL = 32
K = 32
BX = 8
LG = 8
GROUP = BX * LG
LANES = 128
AXES = ("table", "scal")
BATCH = 4
SENT = 7

strength = 0.499


def thomas_solve(below, middle, above, right_side):
    length = middle.shape[0]
    upper_factor = np.zeros(length)
    solved = np.zeros(right_side.shape)
    for row in range(length):
        if row == 0:
            denom = middle[0]
            solved[0] = right_side[0] / denom
        else:
            denom = middle[row] - below[row] * upper_factor[row - 1]
            solved[row] = (right_side[row] - below[row] * solved[row - 1]) / denom
        upper_factor[row] = above[row] / denom
    for row in range(length - 2, -1, -1):
        solved[row] = solved[row] - upper_factor[row] * solved[row + 1]
    return solved


def filter_table(length):
    positions = np.arange(length)
    offset = positions[None, :] - positions[:, None]
    distance = np.abs(offset)
    interior = (positions >= 3) & (positions <= length - 4)
    coeffs = [
        (11.0 + 10.0 * strength) / 16.0,
        (15.0 + 34.0 * strength) / 64.0,
        (-3.0 + 6.0 * strength) / 32.0,
        (1.0 - 2.0 * strength) / 64.0,
    ]
    band = np.zeros((length, length))
    for reach in range(4):
        band = band + np.where(distance == reach, coeffs[reach], 0.0)
    right_side = np.where(interior[:, None], band, np.where(offset == 0, 1.0, 0.0))
    coupling = np.where(interior, strength, 0.0)
    return thomas_solve(coupling, np.ones(length), coupling, right_side)


def derivative_table(length):
    positions = np.arange(length)
    offset = positions[None, :] - positions[:, None]
    distance = np.abs(offset)
    direction = np.sign(offset) * 1.0
    boundary = (positions == 0) | (positions == length - 1)
    second = (positions == 1) | (positions == length - 2)
    interior = ~(boundary | second)
    below_diag = np.where(
        interior, 1.0 / 3.0, np.where(second, 0.25, np.where(positions == length - 1, 2.0, 0.0))
    )
    above_diag = np.where(
        interior, 1.0 / 3.0, np.where(second, 0.25, np.where(positions == 0, 2.0, 0.0))
    )
    inner_rows = direction * (
        np.where(distance == 1, 7.0 / 9.0, 0.0) + np.where(distance == 2, 1.0 / 36.0, 0.0)
    )
    second_rows = direction * np.where(distance == 1, 0.75, 0.0)
    first_row = np.where(
        offset == 0, -2.5, np.where(offset == 1, 2.0, np.where(offset == 2, 0.5, 0.0))
    )
    final_row = np.where(
        offset == 0, 2.5, np.where(offset == -1, -2.0, np.where(offset == -2, -0.5, 0.0))
    )
    right_side = np.where(
        interior[:, None],
        inner_rows,
        np.where(
            second[:, None], second_rows, np.where((positions == 0)[:, None], first_row, final_row)
        ),
    )
    return thomas_solve(below_diag, np.ones(length), above_diag, right_side)


class Plan:
    def __init__(self, table, scal, cells):
        self.table, self.scal, self.cells = table, scal, cells
        self.devices = table * scal
        self.cap = max(2, 5 * GROUP // (2 * table))
        self.near = LANES // table
        self.far = self.cap - self.near
        self.quad = 4 * self.far
        assert cells == table * GROUP and table * self.quad == LANES
        self.code = 1 << (self.cap - 1).bit_length()
        self.scalars = SCAL_ALL // scal
        self.cols = self.scalars * K // LANES
        self.few = self.scalars // 4
        self.rows = self.scalars + self.few
        self.nx = BX * table
        self.chunks = self.devices + self.devices // 4
        self.padded = -(-self.chunks // LANES) * LANES


def iota(shape, dim):
    return lax.broadcasted_iota(jnp.int32, shape, dim)


def pieces_of(values, count):
    pieces = []
    for _ in range(count - 1):
        piece = values.astype(jnp.bfloat16)
        pieces.append(piece)
        values = values - piece.astype(jnp.float32)
    pieces.append(values.astype(jnp.bfloat16))
    return pieces


def dot_rows(a, b):
    return lax.dot_general(a, b, (((1,), (1,)), ((), ())), preferred_element_type=jnp.float32)


def request_kernel(
    plan,
    coords_in,
    owner_in,
    bin_in,
    table_in,
    out_ref,
    early_ref,
    x_ref,
    coords_ref,
    owner_ref,
    bin_ref,
    sem,
):
    p = plan
    row_count = p.cells // LANES
    copies = [
        pltpu.make_async_copy(owner_in, owner_ref, sem.at[0]),
        pltpu.make_async_copy(bin_in, bin_ref, sem.at[1]),
        pltpu.make_async_copy(coords_in, coords_ref, sem.at[2]),
    ]
    early = pltpu.make_async_copy(
        table_in.at[pl.ds(0, early_ref.shape[0])], early_ref, sem.at[3]
    )
    for copy in copies + [early]:
        copy.start()
    for copy in copies:
        copy.wait()
    half = iota((1, LANES), 1) // GROUP
    shard_ids = iota((p.table, LANES), 0)
    owners = owner_ref[...]
    bins = bin_ref[...]
    address = ((bins >> 3) * (8 * p.cols) + (bins & 7)).astype(jnp.float32)
    hits = [owners[i : i + 1, :] == shard_ids for i in range(row_count)]
    before = iota((LANES, LANES), 0)
    after = iota((LANES, LANES), 1)
    earlier = ((before < after) & (before // GROUP == after // GROUP)).astype(jnp.bfloat16)
    ones = jnp.concatenate([h.astype(jnp.float32) for h in hits], axis=0)
    counts = jnp.dot(ones.astype(jnp.bfloat16), earlier, preferred_element_type=jnp.float32)
    x_ref[0:4, :] = coords_ref[...]
    x_ref[5:8, :] = jnp.zeros((3, p.cells), jnp.float32)
    for i in range(row_count):
        x_ref[4:5, i * LANES : (i + 1) * LANES] = address[i : i + 1, :]
    lane_rows = iota((LANES, LANES), 0)
    left, right, codes = [], [], []
    for i in range(row_count):
        span = slice(i * p.table, (i + 1) * p.table)
        rank = jnp.sum(ones[span] * counts[span], axis=0, keepdims=True).astype(jnp.int32)
        codes.append((owners[i : i + 1, :] * p.code + rank).astype(jnp.float32))
        group = 2 * i + half
        near = jnp.where(rank < p.near, group * p.near + rank, -1)
        far = jnp.where(rank >= p.near, group * p.far + rank - p.near, -1)
        right.append(
            jnp.concatenate(
                [
                    (lane_rows == near).astype(jnp.float32),
                    (lane_rows % 32 == far).astype(jnp.float32),
                ],
                axis=0,
            ).astype(jnp.bfloat16)
        )
        fields = x_ref[:, i * LANES : (i + 1) * LANES]
        chosen = []
        for piece in pieces_of(fields, 3):
            piece = jnp.where(hits[i][:, None, :], piece.astype(jnp.float32)[None], 0.0)
            chosen.append(piece.reshape(p.table * 8, LANES).astype(jnp.bfloat16))
        left.append(jnp.concatenate(chosen, axis=0))
    placed = dot_rows(jnp.concatenate(left, axis=1), jnp.concatenate(right, axis=1))
    total = p.table * 8
    placed = placed[0:total] + placed[total : 2 * total] + placed[2 * total :]
    sub = iota((8, LANES), 0)
    block = iota((8, LANES), 1) // 32
    upper = iota((1, LANES), 1) >= GROUP
    for o in range(p.table):
        near_part = placed[o * 8 : (o + 1) * 8, :LANES]
        far_part = placed[o * 8 : (o + 1) * 8, LANES:]
        far_coords = jnp.sum(jnp.where(sub == block, far_part, 0.0), axis=0, keepdims=True)
        code = codes[o // 2] if o % 2 else pltpu.roll(codes[o // 2], GROUP, 1)
        message = jnp.where(
            sub < 5,
            near_part,
            jnp.where(sub == 5, far_coords, jnp.where(upper, code, far_part[4:5])),
        )
        for sc in range(p.scal):
            start = (sc * p.table + o) * SENT
            out_ref[start : start + SENT, :] = message[:SENT]
    early.wait()


def spline_rows(f):
    shape = (K, f[0].shape[1])
    k = iota(shape, 0)
    product = None
    for axis, bit in ((0, 16), (1, 8), (2, 4)):
        factor = jnp.where((k & bit) != 0, f[axis], 1.0 - f[axis])
        product = factor if product is None else product * factor
    last = f[3]
    square = last * last
    cube = square * last
    remain = 1.0 - last
    basis = [
        remain * remain * remain / 6.0,
        (3.0 * cube - 6.0 * square + 4.0) / 6.0,
        (-3.0 * cube + 3.0 * square + 3.0 * last + 1.0) / 6.0,
        cube / 6.0,
    ]
    d = k & 3
    cubic = jnp.where(d == 0, basis[0], jnp.where(d == 1, basis[1], jnp.where(d == 2, basis[2], basis[3])))
    return product * cubic


def swap_blocks(x, count, width):
    row, block = iota(x.shape, 0), iota(x.shape, 1) // width
    bit = 1
    while bit < count:
        up = pltpu.roll(pltpu.roll(x, x.shape[0] - bit, 0), bit * width, 1)
        down = pltpu.roll(pltpu.roll(x, bit, 0), LANES - bit * width, 1)
        low_row, low_block = (row & bit) == 0, (block & bit) == 0
        x = jnp.where(low_row == low_block, x, jnp.where(low_row, up, down))
        bit *= 2
    return x


def fill_slots(plan, recv_ref, out_ref):
    p = plan
    scal_at = lax.axis_index("scal")
    part_x = p.nx // 4
    width = LG * part_x
    codes = jnp.zeros((p.table, LANES), jnp.float32)
    for s in range(p.scal):
        rows = recv_ref[pl.ds(s * p.table * SENT + 6, p.table, stride=SENT), :]
        codes = jnp.where(scal_at == s, rows, codes)
    codes = codes.astype(jnp.bfloat16)
    step = LANES
    for h in range(4):
        x = iota((1, width), 1) % part_x + h * part_x
        inside = (iota((1, width), 1) // part_x) * BX + x % BX + GROUP
        move = (iota((LANES, width), 0) == inside).astype(jnp.float32).astype(jnp.bfloat16)
        moved = jnp.dot(codes, move, preferred_element_type=jnp.float32)
        t = x // BX
        moved = jnp.where(iota((p.table, width), 0) == t, moved, 0.0)
        code = jnp.sum(moved, axis=0, keepdims=True).astype(jnp.int32)
        shard, slot = code // p.code, code % p.code
        t = t - h * (p.table // 4)
        near = (shard // 4) * LANES + (shard % 4) * 32 + t * p.near + slot
        quad = shard // 4
        far = (p.table // 4 + quad // 4) * LANES + (quad % 4) * 32
        far = far + t * p.quad + (shard % 4) * p.far + slot - p.near
        chosen = jnp.where(slot < p.near, near, far)
        rows = iota((step, width), 0)
        for start in range(0, out_ref.shape[1], step):
            hit = rows == chosen - start
            out_ref[h, start : start + step, :] = jnp.where(hit, 1.0, 0.0).astype(jnp.bfloat16)


def swap_four(tiles):
    block = iota((1, LANES), 1) // 32
    for bit in (2, 1):
        low = (block & bit) == 0
        turned = [pltpu.roll(tile, 32 * bit, 1) for tile in tiles]
        back = [pltpu.roll(tile, LANES - 32 * bit, 1) for tile in tiles] if bit == 1 else turned
        out = list(tiles)
        for i in range(4):
            if not i & bit:
                out[i] = jnp.where(low, tiles[i], turned[i + bit])
                out[i + bit] = jnp.where(low, back[i], tiles[i + bit])
        tiles = out
    return tiles


def lookup_kernel(
    plan,
    recv_ref,
    early_ref,
    table_in,
    out_ref,
    place_ref,
    table_ref,
    ints_ref,
    field_ref,
    tile_ref,
    sem,
    *rest,
):
    p = plan
    idx_refs, stores = rest[:16], rest[16:]
    quads = p.table // 4
    early = early_ref.shape[0]
    late = table_in.shape[0] - early
    loads = [
        pltpu.make_async_copy(
            table_in.at[pl.ds(early, late // 2)], table_ref.at[pl.ds(early, late // 2)], sem.at[1]
        ),
        pltpu.make_async_copy(
            table_in.at[pl.ds(early + late // 2, late // 2)],
            table_ref.at[pl.ds(early + late // 2, late // 2)],
            sem.at[2],
        ),
        pltpu.make_async_copy(early_ref, table_ref.at[pl.ds(0, early)], sem.at[3]),
    ]
    loads[0].start()

    def received(r):
        rows = [recv_ref[pl.ds(s * p.table * SENT + r, p.table, stride=SENT), :] for s in range(p.scal)]
        return jnp.concatenate(rows, axis=0)

    addresses = jnp.concatenate([received(4), received(6)], axis=0)
    addresses = swap_blocks(addresses, p.table, p.near)
    order = [addresses[: p.devices]]
    for s in range(p.scal):
        first = p.devices + s * p.table
        order.append(addresses[first : first + quads])
    blank = p.padded - p.chunks
    order.append(jnp.zeros((blank, LANES), jnp.float32))
    order = jnp.concatenate(order, axis=0)
    for first in range(0, p.padded, LANES):
        turned = order[first : first + LANES].T
        ints_ref[:, first : first + LANES] = turned.astype(jnp.int32)
    copies = [
        pltpu.make_async_copy(ints_ref.at[pl.ds(8 * i, 8)], idx_refs[i], sem.at[0])
        for i in range(16)
    ]
    for copy in copies:
        copy.start()
    for load in loads[1:]:
        load.start()
    fields = jnp.concatenate([received(f) for f in (0, 1, 2, 3, 5)], axis=0)
    fields = swap_blocks(fields, p.table, p.near)
    for f in range(4):
        field_ref[f * p.chunks : f * p.chunks + p.devices, :] = fields[
            f * p.devices : (f + 1) * p.devices
        ]
        for s in range(p.scal):
            first = 4 * p.devices + s * p.table + f * quads
            to = f * p.chunks + p.devices + s * quads
            field_ref[to : to + quads, :] = fields[first : first + quads]
    fill_slots(p, recv_ref, place_ref)
    for copy in copies:
        copy.wait()

    def fetch(store, chunk, part):
        step = LANES // p.cols
        for slot in range(part * step, (part + 1) * step, 2):
            rows = []
            for i in (slot, slot + 1):
                address = idx_refs[i // 8][i % 8, chunk]
                if p.cols == 1:
                    rows.append(table_ref[pl.ds(address, 1), :])
                else:
                    rows.append(table_ref[pl.ds(address, p.cols, stride=8), :])
            store[slot * p.cols : (slot + 2) * p.cols, :] = jnp.concatenate(rows, axis=0)

    def reduce(store, chunk, ahead=None):
        weights = spline_rows([field_ref[pl.ds(f * p.chunks + chunk, 1), :] for f in range(4)])
        parts = []
        for c in range(p.cols):
            rows = pl.ds(c, LANES, stride=p.cols) if p.cols > 1 else pl.ds(0, LANES)
            turned = store[rows, :].T
            for m in range(4):
                product = turned[m * K : (m + 1) * K] * weights
                parts.append((product[0:8] + product[8:16]) + (product[16:24] + product[24:32]))
            if ahead is not None:
                ahead(c)
        tile = jnp.sum(jnp.concatenate(parts, axis=0).reshape(p.scalars, 8, LANES), axis=1)
        tile_ref[pl.ds(pl.multiple_of(chunk * p.scalars, p.scalars), p.scalars), :] = tile

    for load in loads:
        load.wait()
    for n in range(BATCH):
        for c in range(p.cols):
            fetch(stores[n], n, c)

    def batch(now, half, more):
        for n in range(BATCH):
            ahead = None
            if more:
                store = stores[(1 - half) * BATCH + n]
                ahead = functools.partial(fetch, store, now + BATCH + n)
            reduce(stores[half * BATCH + n], now + n, ahead)

    def two_batches(i, carry):
        batch(2 * i * BATCH, 0, True)
        batch((2 * i + 1) * BATCH, 1, True)
        return carry

    lax.fori_loop(0, p.chunks // (2 * BATCH) - 1, two_batches, 0)
    batch(p.chunks - 2 * BATCH, 0, True)
    batch(p.chunks - BATCH, 1, False)

    for g in range(p.table):
        for s in range(p.scal):
            dest = chunk = s * p.table + g
            out_ref[dest * p.rows : dest * p.rows + p.scalars, :] = tile_ref[
                chunk * p.scalars : (chunk + 1) * p.scalars, :
            ]
    quad_of = (iota((1, LANES), 1) // p.far) % 4
    for quad in range(quads):
        for s in range(p.scal):
            first = (p.devices + s * quads + quad) * p.scalars
            tile = tile_ref[first : first + p.scalars, :]
            turned = [pltpu.roll(tile, (d * p.far) % LANES, 1) if d else tile for d in range(4)]
            wrapped = [
                pltpu.roll(tile, (-d * p.far) % LANES, 1) if d else tile for d in range(4)
            ]
            for i in range(4):
                message = jnp.zeros((p.few, LANES), jnp.float32)
                for b in range(4):
                    moved = turned[b - i] if b >= i else wrapped[i - b]
                    message = jnp.where(
                        quad_of == b, moved[b * p.few : (b + 1) * p.few], message
                    )
                start = (s * p.table + quad * 4 + i) * p.rows + p.scalars
                out_ref[start : start + p.few, :] = message


def lookup_scratch(plan, table_shape):
    p = plan
    return [
        pltpu.VMEM((table_shape[0] + 8 * p.cols, LANES), jnp.float32),
        pltpu.VMEM((LANES, p.padded), jnp.int32),
        pltpu.VMEM((4 * p.chunks, LANES), jnp.float32),
        pltpu.VMEM((p.chunks * p.scalars, LANES), jnp.float32),
        pltpu.SemaphoreType.DMA((4,)),
    ] + [pltpu.SMEM((8, p.padded), jnp.int32)] * 16 + [pltpu.VMEM((p.cols * LANES, LANES), jnp.float32) for _ in range(2 * BATCH)]


def filter_kernel(plan, recv_ref, place_ref, op_ref, filtered_ref, gradient_ref, *left_refs):
    p = plan
    quad_of = (iota((1, LANES), 1) // p.far) % 4

    def put(tiles, first_row, col):
        for left_ref, tile in zip(left_refs, swap_four(tiles), strict=True):
            left_ref[first_row : first_row + tile.shape[0], col : col + LANES] = tile

    for sc in range(p.scal):
        for o in range(0, p.table, 4):
            starts = [(sc * p.table + o + i) * p.rows for i in range(4)]
            tiles = [recv_ref[start : start + p.scalars, :] for start in starts]
            put(tiles, sc * p.scalars, o // 4 * LANES)
        for quad in range(0, p.table // 4, 4):
            tiles = []
            for n in range(4):
                starts = [sc * p.table + (quad + n) * 4 + i for i in range(4)]
                starts = [start * p.rows + p.scalars for start in starts]
                tile = []
                for b in range(4):
                    part = jnp.zeros((p.few, LANES), jnp.float32)
                    for i in range(4):
                        turned = recv_ref[starts[i] : starts[i] + p.few, :]
                        turned = pltpu.roll(turned, ((i - b) * p.far) % LANES, 1)
                        part = jnp.where(quad_of == i, turned, part)
                    tile.append(part)
                tiles.append(jnp.concatenate(tile, axis=0))
            put(tiles, sc * p.scalars, (p.table // 4 + quad // 4) * LANES)
    sides = []
    for h in range(4):
        left = jnp.concatenate(pieces_of(left_refs[h][...], 2), axis=0)
        values = jnp.dot(left, place_ref[h], preferred_element_type=jnp.float32)
        sides.append(values[:SCAL_ALL] + values[SCAL_ALL:])
    part_x = p.nx // 4
    if part_x == 32:
        lines = []
        for first in range(0, LG * part_x, LANES):
            lines.extend(swap_four([side[:, first : first + LANES] for side in sides]))
    else:
        lines = [
            jnp.concatenate([side[:, r * part_x : (r + 1) * part_x] for side in sides], axis=1)
            for r in range(LG)
        ]
    lines = jnp.concatenate(lines, axis=0)
    lines, op = pieces_of(lines, 2), pieces_of(op_ref[...], 2)
    both = jnp.dot(
        jnp.concatenate([lines[0], lines[0], lines[1]], axis=1),
        jnp.concatenate([op[0], op[1], op[0]], axis=0),
        preferred_element_type=jnp.float32,
    )
    for r in range(LG):
        rows = slice(r * SCAL_ALL, (r + 1) * SCAL_ALL)
        for part in range(p.nx // LANES):
            at = pl.ds(part * SCAL_ALL * LG + r, SCAL_ALL, stride=LG)
            first = part * LANES
            filtered_ref[at, :] = both[rows, first : first + LANES]
            gradient_ref[at, :] = both[rows, p.nx + first : p.nx + first + LANES]


VMEM = pl.BlockSpec(memory_space=pltpu.VMEM)
SMEM = pl.BlockSpec(memory_space=pltpu.SMEM)
HBM = pl.BlockSpec(memory_space=pltpu.HBM)


def call(kernel, plan, out_shape, in_specs, scratch, limit, cost, name):
    many = isinstance(out_shape, tuple)
    return pl.pallas_call(
        functools.partial(kernel, plan),
        out_shape=out_shape,
        in_specs=in_specs,
        out_specs=(VMEM,) * len(out_shape) if many else VMEM,
        scratch_shapes=scratch,
        compiler_params=pltpu.CompilerParams(vmem_limit_bytes=limit << 20),
        cost_estimate=pl.CostEstimate(flops=cost, bytes_accessed=cost // 256, transcendentals=0),
        name=name,
    )


def exchange(array, axes):
    return lax.all_to_all(array, axes, split_axis=0, concat_axis=0, tiled=True)


def on_device(plan, cell_coords, flamelet_table, owner_shard, local_bin):
    p = plan
    f32, i32 = jnp.float32, jnp.int32
    row_count = p.cells // LANES
    owners = owner_shard.reshape(row_count, LANES)
    bins = local_bin.reshape(row_count, LANES)
    bin_count, depth = flamelet_table.shape
    table = flamelet_table.reshape(bin_count // 8, 8, p.cols, LANES).transpose(0, 2, 1, 3)
    table = table.reshape(bin_count * p.cols, LANES)
    requests, early = call(
        request_kernel,
        p,
        (
            jax.ShapeDtypeStruct((p.devices * SENT, LANES), f32),
            jax.ShapeDtypeStruct((bin_count * p.cols * 11 // 32, LANES), f32),
        ),
        [HBM] * 4,
        [
            pltpu.VMEM((8, p.cells), f32),
            pltpu.VMEM(cell_coords.shape, f32),
            pltpu.VMEM(owners.shape, i32),
            pltpu.VMEM(bins.shape, i32),
            pltpu.SemaphoreType.DMA((4,)),
        ],
        32,
        1 << 20,
        "requests",
    )(*[pltpu.with_memory_space_constraint(a, pltpu.HBM) for a in (cell_coords, owners, bins, table)])
    received = exchange(requests.reshape(p.devices, 1, SENT * LANES), AXES[::-1])
    received = received.reshape(p.devices * SENT, LANES)
    replies, place = call(
        lookup_kernel,
        p,
        (
            jax.ShapeDtypeStruct((p.devices * p.rows, LANES), f32),
            jax.ShapeDtypeStruct((4, p.table * 5 * LANES // 16, LG * p.nx // 4), jnp.bfloat16),
        ),
        [VMEM, VMEM, HBM],
        lookup_scratch(p, table.shape),
        30,
        1 << 24,
        "lookup",
    )(received, early, pltpu.with_memory_space_constraint(table, pltpu.HBM))
    answers = exchange(replies.reshape(p.devices, 1, p.rows * LANES), AXES[::-1])
    answers = answers.reshape(p.devices * p.rows, LANES)

    filter_op = filter_table(p.nx).T
    both_op = np.concatenate([filter_op, filter_op @ derivative_table(p.nx).T], axis=1)
    both_op = jnp.asarray(both_op.astype(np.float32))
    out = jax.ShapeDtypeStruct((p.nx // LANES * SCAL_ALL * LG, LANES), f32)
    outs = call(
        filter_kernel,
        p,
        (out, out),
        [VMEM] * 3,
        [pltpu.VMEM((SCAL_ALL, p.table * 5 * LANES // 16), f32)] * 4,
        8 + p.nx * p.table // 64,
        1 << 24,
        "filter",
    )(answers, place, both_op)
    outs = [out.reshape(p.nx // LANES, SCAL_ALL, LG, LANES).transpose(1, 2, 0, 3) for out in outs]
    return tuple(out.reshape(SCAL_ALL, LG, p.nx) for out in outs)


def solution(mesh):
    table, scal = mesh.shape["table"], mesh.shape["scal"]

    def step(cell_coords, flamelet_table, owner_shard, local_bin):
        plan = Plan(table, scal, cell_coords.shape[1])
        return on_device(plan, cell_coords, flamelet_table, owner_shard, local_bin)

    return jax.shard_map(
        step,
        mesh=mesh,
        in_specs=(
            P(None, AXES),
            P("table", "scal"),
            P(AXES, None),
            P(AXES),
        ),
        out_specs=(P(None, AXES, None), P(None, AXES, None)),
        check_vma=False,
    )
```
